512 devices in a mesh: img: 64 (over y_lo, x, z), vol: 8 (over y_hi, core).
Axes of the slice: x: 4, y: 8 (y_hi: 4, y_lo: 2; y = y_hi * 2 + y_lo), z: 8, core: 2. Of those that a mesh axis runs over, the one named last changes fastest.
Arguments:
- images: bfloat16 [512, 512, 512], P(('img', 'vol')), may hold values from -6 to 6
- defocus: float32 [512], P(('img', 'vol')), may hold values from 40 to 400
- noise: float32 [512], P(('img', 'vol')), may hold values from 102.4 to 1024
- orient: int32 [512, 4], P(('img', 'vol')), may hold values from 0 to 767
- planes: int32 [2, 768, 512], P(None, None, 'img'), may hold values from 0 to 31, as said below
- weights: bfloat16 [2, 768, 512], P(None, None, 'img'), may hold values from 0.099609375 to 0.8984375
- volume: bfloat16 [32, 512, 1024], P('vol', 'img'), may hold values from -6 to 6
- data_old: float32 [32, 512, 1024], P('vol', 'img'), may hold values from -6 to 6
- weight_old: float32 [32, 512, 512], P('vol', 'img'), may hold values from 1 to 20
Outputs:
- probs: float32 [512, 4], P(('img', 'vol'))
- data_acc: float32 [32, 512, 1024], P('vol', 'img')
- weight_acc: float32 [32, 512, 512], P('vol', 'img')
The draws below stay inside these ranges and needn't reach their ends.
Inputs may be any that keep to these rules, and one draw needn't show every extreme that they name: `planes`: for every direction and row the two plane indices differ.
All inputs are finite; a program needn't handle non-finite values.
Results may differ from the reference program's by a relative error of at most 0.01325.
Values may be sent and summed in bfloat16 or wider, within the bound.
No kernel may reach another device: no remote copies, remote signals or barrier semaphores. Data moves between devices by JAX's collectives and lax.ppermute only.
A program may use at most 64 MiB of HBM per device.

```python
import math
import jax
import jax.numpy as jnp
from jax import lax

NPIX = 512
NORIENT = 768
ORI = 4
IMG_DEV = 1
IMAGES = 512
NZ = 32
N_VOL = 8


def draw_planes(key, part):
    key = jax.random.fold_in(key, 7)
    first_key, step_key = jax.random.split(key)
    first = jax.random.randint(first_key, (NORIENT, NPIX), 0, NZ)
    offset = jax.random.randint(step_key, (NORIENT, NPIX), 1, NZ)
    second = (first + offset) % NZ
    return jnp.stack([first, second]).astype(jnp.int32)


def place_ends(entries, rng, smallest, top_value):
    longest = entries.shape.index(max(entries.shape))
    spots = []
    for shift in (0, 1):
        where = [jax.random.randint(jax.random.fold_in(rng, axis), (), 0, length) for axis, length in enumerate(entries.shape)]
        where[longest] = (where[longest] + shift) % entries.shape[longest]
        spots.append(tuple(where))
    return entries.at[spots[0]].set(smallest).at[spots[1]].set(top_value)


def level_of(key, extent, shards, low, largest):
    gain = 1.0
    for position, blocks in shards:
        heights = jax.random.uniform(jax.random.fold_in(jax.random.fold_in(key, 6), position), (blocks,), jnp.float32, low / len(shards), largest / len(shards))
        gain = gain * jnp.repeat(jnp.exp(heights), extent[position] // blocks).reshape((-1,) + (1,) * (len(extent) - 1 - position))
    return gain


def scatter_about(stream_key, extent, scale, reach, pieces=(), held_as=jnp.bfloat16):
    level = level_of(stream_key, extent, pieces, -0.22, 0.18) if pieces else 1.0
    result = jax.random.normal(stream_key, extent, jnp.float32) * scale * level
    return jnp.minimum(jnp.maximum(result, -reach), reach).astype(held_as)


def setup_inputs(seed: int = 0) -> dict:
    seeds = jax.random.split(jax.random.key(seed), 10)
    return {
        "images": scatter_about(seeds[0], (IMAGES, NPIX, NPIX), 1.0, 6.0, ((0, 512),)),
        "defocus": jnp.clip(jnp.exp(math.log(400.0) - 2.3025851 * jax.random.uniform(seeds[1], (IMAGES,), jnp.float32) ** level_of(seeds[1], (IMAGES,), ((0, 512),), -0.2, 0.2)), 40.0, 400.0),
        "noise": jnp.clip(jnp.exp(math.log(1024.0) - 2.3025851 * jax.random.uniform(seeds[2], (IMAGES,), jnp.float32) ** level_of(seeds[2], (IMAGES,), ((0, 512),), -0.2, 0.2)), 102.4, 1024.0),
        "orient": place_ends(jax.random.randint(seeds[3], (IMAGES, ORI), 0, NORIENT), jax.random.fold_in(seeds[3], 1), 0, NORIENT - 1).astype(jnp.int32),
        "planes": draw_planes(jax.random.fold_in(seeds[9], 71), 0),
        "weights": jnp.clip(0.099609375 + 0.7988281 * jax.random.uniform(seeds[5], (2, NORIENT, NPIX), jnp.float32) ** level_of(seeds[5], (2, NORIENT, NPIX), ((2, 64),), -0.2, 0.2), 0.099609375, 0.8984375).astype(jnp.bfloat16),
        "volume": scatter_about(seeds[6], (NZ, NPIX, 2 * NPIX), 1.0, 6.0, ((0, 8), (1, 64))),
        "data_old": scatter_about(seeds[7], (NZ, NPIX, 2 * NPIX), 1.0, 6.0, ((0, 8), (1, 64)), jnp.float32),
        "weight_old": jnp.clip(1.0 + 19.0 * jax.random.uniform(seeds[8], (NZ, NPIX, NPIX), jnp.float32) ** level_of(seeds[8], (NZ, NPIX, NPIX), ((0, 8), (1, 64)), -0.2, 0.2), 1.0, 20.0),
    }


AMP = 0.1
PHASE_PART = math.sqrt(0.99)

def dft_tables(npix):
    index = jnp.arange(npix, dtype=jnp.int32)
    product = index[:, None] * index[None, :] % npix
    angle = product.astype(jnp.float32) * (2.0 * math.pi / npix)
    scale = 1.0 / math.sqrt(npix)
    return ((jnp.cos(angle) * scale).astype(jnp.bfloat16), (jnp.sin(angle) * scale).astype(jnp.bfloat16))

def frequency(index, npix):
    return ((index + npix // 2) % npix - npix // 2).astype(jnp.float32) / npix

def contrast(defocus, row_index, npix):
    freq_y = frequency(row_index, npix)
    freq_x = frequency(jnp.arange(npix, dtype=jnp.int32), npix)
    shell = freq_y[:, None] * freq_y[:, None] + freq_x[None, :] * freq_x[None, :]
    phase = defocus[:, None, None] * shell[None]
    return -(PHASE_PART * jnp.sin(phase) + AMP * jnp.cos(phase))

def transform(image, cosine, sine):
    npix = image.shape[0]
    first = jnp.dot(image, jnp.concatenate([cosine, -sine], 1), preferred_element_type=jnp.float32).astype(jnp.bfloat16)
    swapped = jnp.concatenate([first[:, npix:], -first[:, :npix]], 1)
    second = jnp.dot(cosine, first, preferred_element_type=jnp.float32) + jnp.dot(sine, swapped, preferred_element_type=jnp.float32)
    return second.astype(jnp.bfloat16)

def reference(images, defocus, noise, orient, planes, weights, volume, data_old, weight_old):
    cosine, sine = dft_tables(NPIX)
    levels = jnp.arange(NZ, dtype=jnp.int32)
    row_index = jnp.arange(NPIX, dtype=jnp.int32)
    volume_f = volume.astype(jnp.float32)
    highest = lax.Precision.HIGHEST

    def one_image(image, defoc, level, labels):
        fourier = transform(image, cosine, sine)
        ctf = contrast(defoc[None], row_index, NPIX)[0]
        ctf_full = jnp.concatenate([ctf, ctf], 1)
        filtered = (ctf_full * fourier.astype(jnp.float32)).astype(jnp.bfloat16)
        picked = planes[:, labels, :]
        picked_w = weights[:, labels, :].astype(jnp.float32)
        zero = jnp.zeros((), jnp.float32)
        onehot = (jnp.where(picked[0][..., None] == levels, picked_w[0][..., None], zero) + jnp.where(picked[1][..., None] == levels, picked_w[1][..., None], zero)).astype(jnp.bfloat16)
        mix_f = onehot.astype(jnp.float32)
        section = picked_w[0][..., None] * volume_f[picked[0], row_index[None, :]] + picked_w[1][..., None] * volume_f[picked[1], row_index[None, :]]
        cross = lax.optimization_barrier(jnp.sum(filtered.astype(jnp.float32)[None] * section, axis=(1, 2)))
        power = lax.optimization_barrier(jnp.sum((ctf_full * ctf_full)[None] * section * section, axis=(1, 2)))
        score = (cross - 0.5 * power) / level
        prob = jax.nn.softmax(score)
        share = jnp.einsum('o,orz->rz', prob, mix_f, precision=highest).astype(jnp.bfloat16)
        return (prob, share, filtered, (ctf * ctf).astype(jnp.bfloat16))
    group = IMG_DEV * N_VOL
    blocks = IMAGES // group
    block_inputs = (images.reshape(blocks, group, NPIX, NPIX), defocus.reshape(blocks, group), noise.reshape(blocks, group), orient.reshape(blocks, group, ORI))

    def step(carry, block):
        prob, share, filtered, squares = jax.vmap(one_image)(*block)
        share_f = share.astype(jnp.float32)
        data = carry[0] + jnp.einsum('nrz,nrc->zrc', share_f, filtered.astype(jnp.float32), precision=highest)
        weight = carry[1] + jnp.einsum('nrz,nrc->zrc', share_f, squares.astype(jnp.float32), precision=highest)
        return ((data, weight), prob)
    init = (jnp.zeros((NZ, NPIX, 2 * NPIX), jnp.float32), jnp.zeros((NZ, NPIX, NPIX), jnp.float32))
    (data, weight), probs = lax.scan(step, init, block_inputs)
    return (probs.reshape(IMAGES, ORI), data_old + data, weight_old + weight)
```

```python
import functools
import math

import jax
import jax.numpy as jnp
import ml_dtypes
import numpy as np
from jax import lax
from jax.experimental import pallas as pl
from jax.experimental.pallas import tpu as pltpu
from jax.sharding import PartitionSpec as P

AMP = 0.1
TILT = math.asin(AMP)
PI_HIGH = float(np.float32(math.floor(math.pi * 4096) / 4096))
PI_LOW = math.pi - PI_HIGH
VMEM = 32 * 1024 * 1024


def dft_table(npix):
    index = np.arange(npix)
    angle = (index[:, None] * index[None, :] % npix) * (2.0 * math.pi / npix)
    scale = 1.0 / math.sqrt(npix)
    both = np.concatenate([np.cos(angle) * scale, np.sin(angle) * scale], 1)
    return both.astype(np.float32).astype(ml_dtypes.bfloat16)


def frequency(index, npix):
    return ((index + npix // 2) % npix - npix // 2).astype(jnp.float32) / npix


def params():
    return pltpu.CompilerParams(vmem_limit_bytes=VMEM)


def transform_kernel(block, image_ref, table_ref, out_ref, both_ref):
    npix = image_ref.shape[0]
    steps = npix // block

    @pl.loop(0, steps)
    def _(step):
        at = pl.multiple_of(step * block, block)
        first = jnp.dot(
            image_ref[pl.ds(at, block), :], table_ref[...], preferred_element_type=jnp.float32
        )
        real = first[:, :npix].astype(jnp.bfloat16)
        negative = first[:, npix:].astype(jnp.bfloat16)
        below = pl.multiple_of(npix + step * block, block)
        both_ref[pl.ds(at, block), :npix] = real
        both_ref[pl.ds(at, block), npix:] = -negative
        both_ref[pl.ds(below, block), :npix] = -negative
        both_ref[pl.ds(below, block), npix:] = -real

    @pl.loop(0, steps)
    def _(step):
        at = pl.multiple_of(step * block, block)
        out_ref[pl.ds(at, block), :] = jnp.dot(
            table_ref[pl.ds(at, block), :], both_ref[...], preferred_element_type=jnp.float32
        ).astype(jnp.bfloat16)


def transform(image, table):
    npix = image.shape[0]
    return pl.pallas_call(
        functools.partial(transform_kernel, 128),
        out_shape=jax.ShapeDtypeStruct((npix, 2 * npix), jnp.bfloat16),
        scratch_shapes=[pltpu.VMEM((2 * npix, 2 * npix), jnp.bfloat16)],
        compiler_params=params(),
        cost_estimate=pl.CostEstimate(
            flops=6 * npix**3, bytes_accessed=5 * npix * npix * 2, transcendentals=0
        ),
        name="transform",
    )(image, table)


def prepare_kernel(spots_ref, weights_ref, defocus_ref, row_ref, col_ref, mix_ref, turned_ref, ctf_ref, square_ref):
    ori, deep, many = turned_ref.shape
    level = lax.broadcasted_iota(jnp.int32, (deep, many), 0)
    for o in range(ori):
        total = jnp.zeros((deep, many), jnp.float32)
        for k in range(2):
            spot = spots_ref[2 * o + k : 2 * o + k + 1, :]
            weight = weights_ref[2 * o + k : 2 * o + k + 1, :]
            total = total + jnp.where(level == spot, weight, 0.0)
        turned_ref[o] = total.astype(jnp.bfloat16)
        mix_ref[o] = jnp.transpose(total).astype(jnp.bfloat16)
    chi = defocus_ref[...] * (row_ref[...] + col_ref[...])
    turns = jnp.floor((chi + TILT) * (1.0 / math.pi) + 0.5)
    angle = ((chi - turns * PI_HIGH) - turns * PI_LOW) + TILT
    half = turns * 0.5
    sign = 4.0 * (half - jnp.floor(half)) - 1.0
    square = angle * angle
    series = -1.0 / 39916800.0
    for term in (1.0 / 362880.0, -1.0 / 5040.0, 1.0 / 120.0, -1.0 / 6.0, 1.0):
        series = series * square + term
    ctf = sign * (series * angle)
    ctf_ref[...] = ctf
    square_ref[...] = (ctf * ctf).astype(jnp.bfloat16)


def prepare(spots, weights, defocus, row_square, col_square, deep):
    ori = spots.shape[0] // 2
    many = spots.shape[1]
    npix = col_square.shape[1]
    return pl.pallas_call(
        prepare_kernel,
        out_shape=(
            jax.ShapeDtypeStruct((ori, many, deep), jnp.bfloat16),
            jax.ShapeDtypeStruct((ori, deep, many), jnp.bfloat16),
            jax.ShapeDtypeStruct((many, npix), jnp.float32),
            jax.ShapeDtypeStruct((many, npix), jnp.bfloat16),
        ),
        compiler_params=params(),
        cost_estimate=pl.CostEstimate(flops=1 << 25, bytes_accessed=4 << 20, transcendentals=0),
        name="prepare",
    )(spots, weights, defocus, row_square, col_square)


def compare_kernel(steps, rows, step_rows, fourier_ref, ctf_ref, mix_ref, volume_ref, filtered_ref, part_ref, section_ref, total_ref):
    ori, block, deep = mix_ref.shape
    npix = ctf_ref.shape[1]
    step = pl.program_id(0)
    section_ref[...] = jnp.dot(
        mix_ref[...].reshape(ori * block, deep), volume_ref[...], preferred_element_type=jnp.float32
    )

    @pl.loop(0, block // step_rows)
    def _(piece):
        at = pl.multiple_of(piece * step_rows, step_rows)
        ctf = ctf_ref[pl.ds(at, step_rows), :]
        fourier = fourier_ref[pl.ds(at, step_rows), :].astype(jnp.float32)
        real = (ctf * fourier[:, :npix]).astype(jnp.bfloat16)
        imag = (ctf * fourier[:, npix:]).astype(jnp.bfloat16)
        filtered_ref[pl.ds(at, step_rows), :npix] = real
        filtered_ref[pl.ds(at, step_rows), npix:] = imag
        real = real.astype(jnp.float32)
        imag = imag.astype(jnp.float32)
        minus = -0.5 * ctf * ctf
        for o in range(ori):
            below = pl.multiple_of(o * block + at, step_rows)
            s_real = section_ref[pl.ds(below, step_rows), :npix]
            s_imag = section_ref[pl.ds(below, step_rows), npix:]
            score = (
                real * s_real + imag * s_imag + minus * (s_real * s_real + s_imag * s_imag)
            )
            lanes = score[:, :128]
            for chunk in range(1, npix // 128):
                lanes = lanes + score[:, chunk * 128 : (chunk + 1) * 128]
            images = step_rows // rows
            sums = jnp.sum(lanes.reshape(images, rows, 128), axis=1)
            first = pl.multiple_of(step * (block // rows) + piece * images, images)
            total_ref[pl.ds(o * (steps * block // rows) + first, images), :] = sums

    @pl.when(step == steps - 1)
    def _():
        half = total_ref.shape[0] // 2
        upper = jnp.sum(jnp.transpose(total_ref[:half, :]), axis=0, keepdims=True)
        lower = jnp.sum(jnp.transpose(total_ref[half:, :]), axis=0, keepdims=True)
        even = lax.broadcasted_iota(jnp.int32, part_ref.shape, 0) % 2 == 0
        part_ref[...] = jnp.where(even, upper, lower)


def compare(fourier, ctf, mix, volume, rows, copies):
    many, wide = fourier.shape
    ori, _, deep = mix.shape
    steps = 4
    block = many // steps
    images = many // rows
    return pl.pallas_call(
        functools.partial(compare_kernel, steps, rows, 8 * rows),
        grid=(steps,),
        in_specs=[
            pl.BlockSpec((block, wide), lambda i: (i, 0)),
            pl.BlockSpec((block, wide // 2), lambda i: (i, 0)),
            pl.BlockSpec((ori, block, deep), lambda i: (0, i, 0)),
            pl.BlockSpec((deep, wide), lambda i: (0, 0)),
        ],
        out_specs=(
            pl.BlockSpec((block, wide), lambda i: (i, 0)),
            pl.BlockSpec((copies * 2, 2 * images), lambda i: (0, 0)),
        ),
        out_shape=(
            jax.ShapeDtypeStruct((many, wide), jnp.bfloat16),
            jax.ShapeDtypeStruct((copies * 2, 2 * images), jnp.float32),
        ),
        scratch_shapes=[
            pltpu.VMEM((ori * block, wide), jnp.float32),
            pltpu.VMEM((ori * images, 128), jnp.float32),
        ],
        compiler_params=params(),
        cost_estimate=pl.CostEstimate(flops=1 << 30, bytes_accessed=5 << 20, transcendentals=0),
        name="compare",
    )(fourier, ctf, mix, volume)


def project_kernel(rows, part_ref, noise_ref, mix_ref, filtered_ref, square_ref, probs_ref, out_ref):
    ori, deep, many = mix_ref.shape
    wide = filtered_ref.shape[1]
    lanes = part_ref.shape[1]
    images = lanes // 2
    sums = jnp.sum(part_ref[...].reshape(part_ref.shape[0] // 8, 8, lanes), axis=0)
    sums = sums + pltpu.roll(sums, 4, 0)
    sums = sums + pltpu.roll(sums, 2, 0)
    score = sums / noise_ref[...]
    top = jnp.maximum(score, pltpu.roll(score, 1, 0))
    top = jnp.maximum(top, pltpu.roll(top, images, 1))
    power = jnp.exp(score - top)
    whole = power + pltpu.roll(power, 1, 0)
    whole = whole + pltpu.roll(whole, images, 1)
    probs = power / whole
    probs_ref[...] = probs
    image = lax.broadcasted_iota(jnp.int32, (lanes, many), 0)
    owner = lax.broadcasted_iota(jnp.int32, (lanes, many), 1) // rows
    share = jnp.zeros((deep, many), jnp.float32)
    for half in range(2):
        spread = jnp.where(image == owner + half * images, 1.0, 0.0)
        along = jnp.dot(
            probs, spread, preferred_element_type=jnp.float32, precision=lax.Precision.HIGHEST
        )
        for row in range(2):
            share = share + along[row : row + 1, :] * mix_ref[2 * row + half].astype(jnp.float32)
    share = share.astype(jnp.bfloat16)
    out_ref[:, :wide] = jnp.dot(
        share, filtered_ref[...], preferred_element_type=jnp.float32
    ).astype(jnp.bfloat16)
    out_ref[:, wide:] = jnp.dot(
        share, square_ref[...], preferred_element_type=jnp.float32
    ).astype(jnp.bfloat16)


def project(part, noise, mix, filtered, square, rows):
    _, deep, many = mix.shape
    wide = filtered.shape[1]
    return pl.pallas_call(
        functools.partial(project_kernel, rows),
        out_shape=(
            jax.ShapeDtypeStruct((8, part.shape[1]), jnp.float32),
            jax.ShapeDtypeStruct((deep, wide + wide // 2), jnp.bfloat16),
        ),
        compiler_params=params(),
        cost_estimate=pl.CostEstimate(flops=1 << 29, bytes_accessed=4 << 20, transcendentals=0),
        name="project",
    )(part, noise, mix, filtered, square)


def finish_kernel(part_ref, data_ref, weight_ref, data_out, weight_out):
    wide = data_ref.shape[1]
    data = part_ref[0, :, :wide].astype(jnp.float32)
    weight = part_ref[0, :, wide:].astype(jnp.float32)
    for source in range(1, part_ref.shape[0]):
        data = data + part_ref[source, :, :wide].astype(jnp.float32)
        weight = weight + part_ref[source, :, wide:].astype(jnp.float32)
    data_out[...] = data_ref[...] + data
    weight_out[...] = weight_ref[...] + weight


def finish(parts, data_old, weight_old):
    return pl.pallas_call(
        finish_kernel,
        out_shape=(
            jax.ShapeDtypeStruct(data_old.shape, jnp.float32),
            jax.ShapeDtypeStruct(weight_old.shape, jnp.float32),
        ),
        compiler_params=params(),
        cost_estimate=pl.CostEstimate(flops=1 << 20, bytes_accessed=2 << 20, transcendentals=0),
        name="finish",
    )(parts, data_old, weight_old)


def on_device(images, defocus, noise, orient, planes, weights, volume, data_old, weight_old):
    npix = images.shape[1]
    ori = orient.shape[1]
    n_img = lax.axis_size("img")
    n_vol = lax.axis_size("vol")
    rows = npix // n_img
    slab = volume.shape[0]
    deep = n_vol * slab * rows
    many = n_img * rows

    about = jnp.concatenate(
        [orient[0].astype(jnp.float32), defocus, noise, jnp.zeros((2,), jnp.float32)]
    )
    about = jnp.broadcast_to(about[None, None, :], (n_img, 1, ori + 4))
    about = lax.all_to_all(about, "img", split_axis=0, concat_axis=0, tiled=True)[:, 0, :]
    vol_rows = lax.all_to_all(
        jnp.broadcast_to(volume.reshape(1, slab * rows, 2 * npix), (n_vol, slab * rows, 2 * npix)),
        "vol",
        split_axis=0,
        concat_axis=0,
        tiled=True,
    ).reshape(deep, 2 * npix)

    fourier = transform(images[0], jnp.asarray(dft_table(npix)))
    fourier = lax.all_to_all(
        fourier.reshape(n_img, rows, 2 * npix), "img", split_axis=0, concat_axis=0, tiled=True
    ).reshape(many, 2 * npix)

    labels = about[:, :ori].astype(jnp.int32)
    defocus_all = about[:, ori]
    noise_all = about[:, ori + 1]
    local = jnp.arange(rows, dtype=jnp.int32)
    spots = planes[:, labels, :] * rows + local
    spots = jnp.transpose(spots, (2, 0, 1, 3)).reshape(2 * ori, many)
    picked = jnp.transpose(weights[:, labels, :], (2, 0, 1, 3)).reshape(2 * ori, many)
    freq_y = frequency(lax.axis_index("img") * rows + local, npix)
    row_square = jnp.tile(freq_y * freq_y, n_img)[:, None]
    freq_x = frequency(jnp.arange(npix, dtype=jnp.int32), npix)
    mix, turned, ctf, square = prepare(
        spots,
        picked.astype(jnp.float32),
        jnp.repeat(defocus_all, rows)[:, None],
        row_square,
        (freq_x * freq_x)[None, :],
        deep,
    )
    filtered, part = compare(fourier, ctf, mix, vol_rows, rows, n_img)
    part = lax.all_to_all(
        part.reshape(n_img, 2, 2 * n_img), "img", split_axis=0, concat_axis=0, tiled=True
    ).reshape(2 * n_img, 2 * n_img)
    probs, sums = project(part, jnp.tile(noise_all, 2)[None, :], turned, filtered, square, rows)
    sums = lax.all_to_all(
        sums.reshape(n_vol, slab * rows, 3 * npix), "vol", split_axis=0, concat_axis=0, tiled=True
    )
    mine = lax.dynamic_slice_in_dim(
        probs[:2].reshape(2 * 2, n_img), lax.axis_index("img"), 1, 1
    ).reshape(1, ori)
    data, weight = finish(
        sums,
        data_old.reshape(slab * rows, 2 * npix),
        weight_old.reshape(slab * rows, npix),
    )
    return (mine, data.reshape(data_old.shape), weight.reshape(weight_old.shape))


def solution(mesh):
    placed = (
        P(("img", "vol"), None, None),
        P(("img", "vol")),
        P(("img", "vol")),
        P(("img", "vol"), None),
        P(None, None, "img"),
        P(None, None, "img"),
        P("vol", "img", None),
        P("vol", "img", None),
        P("vol", "img", None),
    )
    return jax.shard_map(
        on_device,
        mesh=mesh,
        in_specs=placed,
        out_specs=(P(("img", "vol"), None), P("vol", "img", None), P("vol", "img", None)),
        check_vma=False,
    )
```

```python
import functools
import math

import jax
import jax.numpy as jnp
import ml_dtypes
import numpy as np
from jax import lax
from jax.experimental import pallas as pl
from jax.experimental.pallas import tpu as pltpu
from jax.sharding import PartitionSpec as P

AMP = 0.1
TILT = math.asin(AMP)
PI_HIGH = float(np.float32(math.floor(math.pi * 4096) / 4096))
PI_LOW = math.pi - PI_HIGH
VMEM = 56 * 1024 * 1024
LARGE = 32 * 1024 * 1024
SMALL = 16 * 1024 * 1024
META = 128


def dft_table(npix):
    index = np.arange(npix)
    angle = (index[:, None] * index[None, :] % npix) * (2.0 * math.pi / npix)
    scale = 1.0 / math.sqrt(npix)
    both = np.concatenate([np.cos(angle) * scale, np.sin(angle) * scale], 1)
    return both.astype(np.float32).astype(ml_dtypes.bfloat16)


def frequency(index, npix):
    return ((index + npix // 2) % npix - npix // 2).astype(jnp.float32) / npix


def params(size=VMEM):
    return pltpu.CompilerParams(vmem_limit_bytes=size)


def cost(flops, size):
    return pl.CostEstimate(flops=flops, bytes_accessed=size, transcendentals=0)


def whole():
    return pl.BlockSpec(memory_space=pltpu.VMEM)


def scalar():
    return pl.BlockSpec(memory_space=pltpu.SMEM)


def same(a, b):
    return lax.dot_general(a, b, (((1,), (1,)), ((), ())), preferred_element_type=jnp.float32)


def three_parts(value):
    parts = []
    for _ in range(3):
        part = value.astype(jnp.bfloat16).astype(jnp.float32)
        parts.append(part)
        value = value - part
    return parts


def transform_kernel(chunk, orient_ref, defocus_ref, noise_ref, image_ref, table_ref, out_ref, both_ref):
    npix = image_ref.shape[0]
    ori = orient_ref.shape[1]
    lane = lax.broadcasted_iota(jnp.int32, (8, META), 1)
    codes = jnp.zeros((8, META), jnp.int32)
    for o in range(ori):
        label = orient_ref[0, o]
        codes = jnp.where(lane == o, label & 255, codes)
        codes = jnp.where(lane == ori + o, label >> 8, codes)
    about = codes.astype(jnp.float32)
    place = 2 * ori
    for scalar_ref in (defocus_ref, noise_ref):
        for part in three_parts(jnp.full((8, META), scalar_ref[0], jnp.float32)):
            about = jnp.where(lane == place, part, about)
            place += 1
    out_ref[:, 2 * npix :] = jnp.broadcast_to(about[:1], (npix, META)).astype(jnp.bfloat16)
    for start in range(0, npix, chunk):
        real = jnp.dot(
            image_ref[...], table_ref[:, start : start + chunk], preferred_element_type=jnp.float32
        ).astype(jnp.bfloat16)
        both_ref[:npix, start : start + chunk] = real
        both_ref[npix:, npix + start : npix + start + chunk] = -real
        imag = -jnp.dot(
            image_ref[...],
            table_ref[:, npix + start : npix + start + chunk],
            preferred_element_type=jnp.float32,
        ).astype(jnp.bfloat16)
        both_ref[:npix, npix + start : npix + start + chunk] = imag
        both_ref[npix:, start : start + chunk] = imag
    for start in range(0, 2 * npix, chunk):
        out_ref[:, start : start + chunk] = jnp.dot(
            table_ref[...], both_ref[:, start : start + chunk], preferred_element_type=jnp.float32
        ).astype(jnp.bfloat16)


def transform(orient, defocus, noise, image, table):
    npix = image.shape[0]
    return pl.pallas_call(
        functools.partial(transform_kernel, 256),
        in_specs=[scalar(), scalar(), scalar(), whole(), whole()],
        out_specs=whole(),
        out_shape=jax.ShapeDtypeStruct((npix, 2 * npix + META), jnp.bfloat16),
        scratch_shapes=[pltpu.VMEM((2 * npix, 2 * npix), jnp.bfloat16)],
        compiler_params=params(),
        cost_estimate=cost(12 * npix**3, 10 * npix * npix),
        name="transform",
    )(orient, defocus, noise, image, table)


def prepare_kernel(planes_ref, weights_ref, lookup_ref):
    deep, labels = lookup_ref.shape
    rows = planes_ref.shape[1]
    level = lax.broadcasted_iota(jnp.int32, (deep // rows, rows, labels), 0)
    total = jnp.zeros((deep // rows, rows, labels), jnp.float32)
    for k in range(2):
        weight = weights_ref[k].astype(jnp.float32)
        total = total + jnp.where(level == planes_ref[k][None], weight[None], 0.0)
    lookup_ref[...] = total.reshape(deep, labels).astype(jnp.bfloat16)


def prepare(planes, weights, deep):
    labels = planes.shape[2]
    return pl.pallas_call(
        prepare_kernel,
        in_specs=[whole(), whole()],
        out_specs=whole(),
        out_shape=jax.ShapeDtypeStruct((deep, labels), jnp.bfloat16),
        compiler_params=params(SMALL),
        cost_estimate=cost(1 << 22, 1 << 20),
        name="prepare",
    )(planes, weights)


def contrast(defocus, row_square, npix):
    column = lax.broadcasted_iota(jnp.int32, (1, npix), 1)
    freq_x = frequency(column, npix)
    chi = defocus * (row_square + freq_x * freq_x)
    turns = jnp.floor((chi + TILT) * (1.0 / math.pi) + 0.5)
    angle = ((chi - turns * PI_HIGH) - turns * PI_LOW) + TILT
    half = turns * 0.5
    sign = 4.0 * (half - jnp.floor(half)) - 1.0
    square = angle * angle
    series = -1.0 / 39916800.0
    for term in (1.0 / 362880.0, -1.0 / 5040.0, 1.0 / 120.0, -1.0 / 6.0, 1.0):
        series = series * square + term
    return sign * (series * angle)


def compare_kernel(ori, rows, slot_ref, fourier_ref, lookup_ref, volume_ref, filtered_ref, square_ref, picks_ref, part_ref, noise_ref, mix_ref, total_ref, defocus_ref):
    many, npix = square_ref.shape
    deep = volume_ref.shape[0]
    images = many // rows
    batches, block, _ = mix_ref.shape
    lines = block // ori
    group = lines // rows

    meta = fourier_ref[:, 2 * npix :]
    here = lax.broadcasted_iota(jnp.int32, (images, many), 0) * rows
    there = lax.broadcasted_iota(jnp.int32, (images, many), 1)
    pick = jnp.where(here == there, 1.0, 0.0).astype(jnp.bfloat16)
    about = jnp.dot(pick, meta, preferred_element_type=jnp.float32)
    label = lax.broadcasted_iota(jnp.int32, (images, lookup_ref.shape[1]), 1).astype(jnp.float32)
    owner = lax.broadcasted_iota(jnp.int32, (many, images), 0) // rows
    image = lax.broadcasted_iota(jnp.int32, (many, images), 1)
    spread = jnp.where(owner == image, 1.0, 0.0).astype(jnp.bfloat16)
    row = lax.broadcasted_iota(jnp.int32, (many, deep), 0) % rows
    at_row = row == lax.broadcasted_iota(jnp.int32, (many, deep), 1) % rows
    for o in range(ori):
        mine = about[:, o : o + 1] + 256.0 * about[:, ori + o : ori + o + 1]
        found = same(jnp.where(label == mine, 1.0, 0.0).astype(jnp.bfloat16), lookup_ref[...])
        found = found.astype(jnp.bfloat16)
        picks_ref[o * images : (o + 1) * images, :] = found
        every = jnp.dot(spread, found, preferred_element_type=jnp.float32)
        every = jnp.where(at_row, every, 0.0).astype(jnp.bfloat16)
        for batch in range(batches):
            mix_ref[batch, o * lines : (o + 1) * lines, :] = every[batch * lines : (batch + 1) * lines]
    place = 2 * ori
    defocus = meta.astype(jnp.float32)
    defocus_ref[...] = (
        defocus[:, place : place + 1]
        + defocus[:, place + 1 : place + 2]
        + defocus[:, place + 2 : place + 3]
    )
    turned = jnp.transpose(jnp.concatenate([about, about], 0))
    noise_ref[...] = (
        turned[place + 3 : place + 4] + turned[place + 4 : place + 5] + turned[place + 5 : place + 6]
    )
    index = lax.broadcasted_iota(jnp.int32, (lines, 1), 0) % rows + slot_ref[0] * rows
    freq_y = frequency(index, npix)

    @pl.loop(0, batches)
    def _(batch):
        at = pl.multiple_of(batch * lines, lines)
        section = jnp.dot(mix_ref[batch], volume_ref[...], preferred_element_type=jnp.float32)
        ctf = contrast(defocus_ref[pl.ds(at, lines), :], freq_y * freq_y, npix)
        for part in range(2):
            fourier = fourier_ref[pl.ds(at, lines), part * npix : (part + 1) * npix]
            filtered_ref[pl.ds(at, lines), part * npix : (part + 1) * npix] = (
                ctf * fourier.astype(jnp.float32)
            ).astype(jnp.bfloat16)
        square = ctf * ctf
        square_ref[pl.ds(at, lines), :] = square.astype(jnp.bfloat16)
        for o in range(ori):
            real = section[o * lines : (o + 1) * lines, :npix]
            imag = section[o * lines : (o + 1) * lines, npix:]
            power = square * (real * real + imag * imag)
            lanes = power[:, :128]
            for chunk in range(1, npix // 128):
                lanes = lanes + power[:, chunk * 128 : (chunk + 1) * 128]
            sums = jnp.sum(lanes.reshape(group, rows, 128), axis=1)
            first = pl.multiple_of(o * images + batch * group, group)
            total_ref[pl.ds(first, group), :] = sums

    found = jnp.where(at_row, same(filtered_ref[...], volume_ref[...]), 0.0)
    found = jnp.sum(found.reshape(images, rows, deep), axis=1)
    halves = []
    for o in range(ori):
        cross = found * picks_ref[o * images : (o + 1) * images, :].astype(jnp.float32)
        lanes = cross[:, :128]
        for chunk in range(1, deep // 128):
            lanes = lanes + cross[:, chunk * 128 : (chunk + 1) * 128]
        halves.append(lanes - 0.5 * total_ref[o * images : (o + 1) * images, :])
    upper = jnp.concatenate(halves[: ori // 2], 0)
    lower = jnp.concatenate(halves[ori // 2 :], 0)
    upper = jnp.sum(jnp.transpose(upper), axis=0, keepdims=True)
    lower = jnp.sum(jnp.transpose(lower), axis=0, keepdims=True)
    even = lax.broadcasted_iota(jnp.int32, part_ref.shape, 0) % 2 == 0
    part_ref[...] = jnp.where(even, upper, lower)


def compare(slot, fourier, lookup, volume, ori, rows, copies):
    many = fourier.shape[0]
    deep, wide = volume.shape
    images = many // rows
    lines = 8 * rows
    return pl.pallas_call(
        functools.partial(compare_kernel, ori, rows),
        in_specs=[scalar()] + [whole()] * 3,
        out_specs=(whole(),) * 5,
        out_shape=(
            jax.ShapeDtypeStruct((many, wide), jnp.bfloat16),
            jax.ShapeDtypeStruct((many, wide // 2), jnp.bfloat16),
            jax.ShapeDtypeStruct((ori * images, deep), jnp.bfloat16),
            jax.ShapeDtypeStruct((copies * 2, 2 * images), jnp.float32),
            jax.ShapeDtypeStruct((1, 2 * images), jnp.float32),
        ),
        scratch_shapes=[
            pltpu.VMEM((many // lines, ori * lines, deep), jnp.bfloat16),
            pltpu.VMEM((ori * images, 128), jnp.float32),
            pltpu.VMEM((many, 1), jnp.float32),
        ],
        compiler_params=params(LARGE),
        cost_estimate=cost(1 << 31, 5 << 20),
        name="compare",
    )(slot, fourier, lookup, volume)


def project_kernel(rows, ori, core_ref, part_ref, noise_ref, picks_ref, filtered_ref, square_ref, probs_ref, keep_ref, send_ref):
    many, wide = filtered_ref.shape
    deep = picks_ref.shape[1]
    lanes = part_ref.shape[1]
    images = lanes // 2
    sums = jnp.sum(part_ref[...].reshape(part_ref.shape[0] // 8, 8, lanes), axis=0)
    sums = sums + pltpu.roll(sums, 4, 0)
    sums = sums + pltpu.roll(sums, 2, 0)
    score = sums / noise_ref[...]
    top = jnp.maximum(score, pltpu.roll(score, 1, 0))
    top = jnp.maximum(top, pltpu.roll(top, images, 1))
    power = jnp.exp(score - top)
    total = power + pltpu.roll(power, 1, 0)
    total = total + pltpu.roll(total, images, 1)
    probs = power / total
    probs_ref[...] = probs
    column = jnp.transpose(jnp.concatenate([probs] * (lanes // 8), 0))
    share = jnp.zeros((images, deep), jnp.float32)
    for o in range(ori):
        half = o % 2
        chance = column[half * images : (half + 1) * images, o // 2 : o // 2 + 1]
        share = share + chance * picks_ref[o * images : (o + 1) * images, :].astype(jnp.float32)
    image = lax.broadcasted_iota(jnp.int32, (images, many), 0)
    owner = lax.broadcasted_iota(jnp.int32, (images, many), 1) // rows
    spread = jnp.where(owner == image, 1.0, 0.0).astype(jnp.bfloat16)
    row = lax.broadcasted_iota(jnp.int32, (deep, many), 0) % rows
    at_row = row == lax.broadcasted_iota(jnp.int32, (deep, many), 1) % rows
    share = jnp.dot(
        jnp.transpose(share).astype(jnp.bfloat16), spread, preferred_element_type=jnp.float32
    )
    share = jnp.where(at_row, share, 0.0).astype(jnp.bfloat16)
    first = core_ref[0] == 0
    for source_ref, start, size in ((filtered_ref, 0, wide), (square_ref, wide, wide // 2)):
        sums = jnp.dot(share, source_ref[...], preferred_element_type=jnp.float32)
        sums = sums.reshape(keep_ref.shape[0], 2, keep_ref.shape[1], size)
        keep_ref[:, :, start : start + size] = jnp.where(first, sums[:, 0], sums[:, 1]).astype(jnp.bfloat16)
        send_ref[:, :, start : start + size] = jnp.where(first, sums[:, 1], sums[:, 0]).astype(jnp.bfloat16)


def project(core, part, noise, picks, filtered, square, rows, ori, pairs):
    many, wide = filtered.shape
    deep = picks.shape[1]
    half = jax.ShapeDtypeStruct((pairs, deep // (2 * pairs), wide + wide // 2), jnp.bfloat16)
    return pl.pallas_call(
        functools.partial(project_kernel, rows, ori),
        in_specs=[scalar()] + [whole()] * 5,
        out_specs=(whole(), whole(), whole()),
        out_shape=(jax.ShapeDtypeStruct((8, part.shape[1]), jnp.float32), half, half),
        compiler_params=params(LARGE),
        cost_estimate=cost(1 << 29, 4 << 20),
        name="project",
    )(core, part, noise, picks, filtered, square)


def middle_kernel(high_ref, keep_ref, got_ref, own_ref, *send_refs):
    pairs = keep_ref.shape[0]
    for ahead in range(pairs):
        at = (high_ref[0] + ahead) % pairs
        total = keep_ref[at].astype(jnp.float32) + got_ref[at].astype(jnp.float32)
        if ahead == 0:
            own_ref[...] = total
        else:
            send_refs[ahead - 1][...] = total.astype(jnp.bfloat16)


def middle(high, keep, got):
    pairs, slab, wide = keep.shape
    return pl.pallas_call(
        middle_kernel,
        in_specs=[scalar(), whole(), whole()],
        out_specs=(whole(),) * pairs,
        out_shape=(jax.ShapeDtypeStruct((slab, wide), jnp.float32),)
        + (jax.ShapeDtypeStruct((slab, wide), jnp.bfloat16),) * (pairs - 1),
        compiler_params=params(SMALL),
        cost_estimate=cost(1 << 20, 2 << 20),
        name="middle",
    )(high, keep, got)


def finish_kernel(own_ref, *refs):
    data_ref, weight_ref, data_out, weight_out = refs[-4:]
    wide = data_ref.shape[1]
    total = own_ref[...]
    for part_ref in refs[:-4]:
        total = total + part_ref[...].astype(jnp.float32)
    data_out[...] = data_ref[...] + total[:, :wide]
    weight_out[...] = weight_ref[...] + total[:, wide:]


def finish(own, parts, data_old, weight_old):
    return pl.pallas_call(
        finish_kernel,
        out_shape=(
            jax.ShapeDtypeStruct(data_old.shape, jnp.float32),
            jax.ShapeDtypeStruct(weight_old.shape, jnp.float32),
        ),
        compiler_params=params(SMALL),
        cost_estimate=cost(1 << 20, 2 << 20),
        name="finish",
    )(own, *parts, data_old, weight_old)


def on_device(images, defocus, noise, orient, planes, weights, volume, data_old, weight_old):
    npix = images.shape[1]
    ori = orient.shape[1]
    n_img = lax.axis_size("img")
    n_vol = lax.axis_size("vol")
    rows = npix // n_img
    slab = volume.shape[0]
    deep = n_vol * slab * rows
    many = n_img * rows
    pairs = n_vol // 2
    slot = lax.axis_index("img").astype(jnp.int32).reshape(1)
    place = lax.axis_index("vol").astype(jnp.int32)

    fourier = transform(orient, defocus, noise, images[0], jnp.asarray(dft_table(npix)))
    fourier = lax.all_to_all(
        fourier.reshape(n_img, rows, 2 * npix + META), "img", split_axis=0, concat_axis=0, tiled=True
    ).reshape(many, 2 * npix + META)
    vol_rows = lax.all_gather(volume.reshape(slab * rows, 2 * npix), "vol", axis=0, tiled=True)
    lookup = prepare(jnp.swapaxes(planes, 1, 2), jnp.swapaxes(weights, 1, 2), deep)
    filtered, square, picks, part, noise_all = compare(
        slot, fourier, lookup, vol_rows, ori, rows, n_img
    )
    part = lax.all_to_all(
        part.reshape(n_img, 2, 2 * n_img), "img", split_axis=0, concat_axis=0, tiled=True
    ).reshape(2 * n_img, 2 * n_img)
    probs, keep, send = project(
        (place % 2).reshape(1), part, noise_all, picks, filtered, square, rows, ori, pairs
    )
    mine = lax.dynamic_slice_in_dim(
        probs[:2].reshape(2 * 2, n_img), lax.axis_index("img"), 1, 1
    ).reshape(1, ori)
    got = lax.ppermute(send, "vol", [(v, v ^ 1) for v in range(n_vol)])
    own, *sends = middle((place // 2).reshape(1), keep, got)
    parts = [
        lax.ppermute(part, "vol", [(v, (v + 2 * ahead) % n_vol) for v in range(n_vol)])
        for ahead, part in enumerate(sends, 1)
    ]
    data, weight = finish(
        own,
        parts,
        data_old.reshape(slab * rows, 2 * npix),
        weight_old.reshape(slab * rows, npix),
    )
    return (mine, data.reshape(data_old.shape), weight.reshape(weight_old.shape))


def solution(mesh):
    placed = (
        P(("img", "vol"), None, None),
        P(("img", "vol")),
        P(("img", "vol")),
        P(("img", "vol"), None),
        P(None, None, "img"),
        P(None, None, "img"),
        P("vol", "img", None),
        P("vol", "img", None),
        P("vol", "img", None),
    )
    return jax.shard_map(
        on_device,
        mesh=mesh,
        in_specs=placed,
        out_specs=(P(("img", "vol"), None), P("vol", "img", None), P("vol", "img", None)),
        check_vma=False,
    )
```

```python
import functools
import math

import jax
import jax.numpy as jnp
import ml_dtypes
import numpy as np
from jax import lax
from jax.experimental import pallas as pl
from jax.experimental.pallas import tpu as pltpu
from jax.sharding import PartitionSpec as P

AMP = 0.1
TILT = math.asin(AMP)
TURN = 2.0 * math.pi
TURN_HIGH = math.floor(TURN * 4096) / 4096
TURN_LOW = TURN - TURN_HIGH
SINE = tuple(
    factor / TURN ** (2 * power + 1)
    for power, factor in enumerate(
        (
            6.283185272722434,
            -41.341697068956265,
            81.60502462257806,
            -76.70155117622761,
            42.01616582127327,
            -14.868610992503873,
            3.199693654235983,
        )
    )
)
LARGE = 32 * 1024 * 1024
SMALL = 16 * 1024 * 1024
META = 128


def dft_table(npix):
    index = np.arange(npix)
    angle = (index[:, None] * index[None, :] % npix) * (2.0 * math.pi / npix)
    scale = 1.0 / math.sqrt(npix)
    both = np.concatenate([np.cos(angle) * scale, np.sin(angle) * scale], 1)
    return both.astype(np.float32).astype(ml_dtypes.bfloat16)


def frequency(index, npix):
    return ((index + npix // 2) % npix - npix // 2).astype(jnp.float32) / npix


def params(size):
    return pltpu.CompilerParams(vmem_limit_bytes=size)


def cost(flops, size):
    return pl.CostEstimate(flops=flops, bytes_accessed=size, transcendentals=0)


def whole():
    return pl.BlockSpec(memory_space=pltpu.VMEM)


def scalar():
    return pl.BlockSpec(memory_space=pltpu.SMEM)


def same(a, b):
    return lax.dot_general(a, b, (((1,), (1,)), ((), ())), preferred_element_type=jnp.float32)


def three_parts(value):
    parts = []
    for _ in range(3):
        part = value.astype(jnp.bfloat16).astype(jnp.float32)
        parts.append(part)
        value = value - part
    return parts


def bits(rows):
    assert rows & (rows - 1) == 0
    return rows.bit_length() - 1


def spread_over(rows, shape, image_axis):
    image = lax.broadcasted_iota(jnp.int32, shape, image_axis)
    owner = lax.broadcasted_iota(jnp.int32, shape, 1 - image_axis) >> bits(rows)
    return jnp.where(owner == image, 1.0, 0.0).astype(jnp.bfloat16)


def own_row(values, rows):
    height, width = values.shape
    sublane = lax.broadcasted_iota(jnp.int32, (rows, width), 0)
    lane = lax.broadcasted_iota(jnp.int32, (rows, width), 1) & (rows - 1)
    return jnp.where((sublane == lane)[None], values.reshape(height // rows, rows, width), 0.0)


def transform_kernel(chunk, orient_ref, defocus_ref, noise_ref, image_ref, table_hbm, out_hbm, table_ref, both_ref, out_ref, in_sems, out_sems):
    npix = image_ref.shape[0]
    ori = orient_ref.shape[1]
    starts = list(range(0, 2 * npix, chunk))
    loads = []
    for number, start in enumerate(starts):
        at = pl.ds(start, chunk)
        load = pltpu.make_async_copy(table_hbm.at[:, at], table_ref.at[:, at], in_sems.at[number])
        load.start()
        loads.append(load)
    lane = lax.broadcasted_iota(jnp.int32, (8, META), 1)
    codes = jnp.zeros((8, META), jnp.int32)
    for o in range(ori):
        label = orient_ref[0, o]
        codes = jnp.where(lane == o, label & 255, codes)
        codes = jnp.where(lane == ori + o, label >> 8, codes)
    about = codes.astype(jnp.float32)
    place = 2 * ori
    for scalar_ref in (defocus_ref, noise_ref):
        for part in three_parts(jnp.full((8, META), scalar_ref[0, 0], jnp.float32)):
            about = jnp.where(lane == place, part, about)
            place += 1
    out_ref[:, 2 * npix :] = jnp.broadcast_to(about[:1], (npix, META)).astype(jnp.bfloat16)
    saves = []

    def save(start, size):
        at = pl.ds(start, size)
        copy = pltpu.make_async_copy(out_ref.at[:, at], out_hbm.at[:, at], out_sems.at[len(saves)])
        copy.start()
        saves.append(copy)

    save(2 * npix, META)
    for number, start in enumerate(starts):
        loads[number].wait()
        first = jnp.dot(
            image_ref[...], table_ref[:, start : start + chunk], preferred_element_type=jnp.float32
        ).astype(jnp.bfloat16)
        if start < npix:
            both_ref[:npix, start : start + chunk] = first
            both_ref[npix:, npix + start : npix + start + chunk] = -first
        else:
            both_ref[:npix, start : start + chunk] = -first
            both_ref[npix:, start - npix : start - npix + chunk] = -first
    for start in starts:
        out_ref[:, start : start + chunk] = jnp.dot(
            table_ref[...], both_ref[:, start : start + chunk], preferred_element_type=jnp.float32
        ).astype(jnp.bfloat16)
        save(start, chunk)
    for copy in saves:
        copy.wait()


def transform(orient, defocus, noise, image, table):
    npix = image.shape[0]
    chunk = 256
    pieces = 2 * npix // chunk
    return pl.pallas_call(
        functools.partial(transform_kernel, chunk),
        in_specs=[scalar(), scalar(), scalar(), whole(), pl.BlockSpec(memory_space=pl.ANY)],
        out_specs=pl.BlockSpec(memory_space=pl.ANY),
        out_shape=jax.ShapeDtypeStruct((npix, 2 * npix + META), jnp.bfloat16),
        scratch_shapes=[
            pltpu.VMEM((npix, 2 * npix), jnp.bfloat16),
            pltpu.VMEM((2 * npix, 2 * npix), jnp.bfloat16),
            pltpu.VMEM((npix, 2 * npix + META), jnp.bfloat16),
            pltpu.SemaphoreType.DMA((pieces,)),
            pltpu.SemaphoreType.DMA((pieces + 1,)),
        ],
        compiler_params=params(LARGE),
        cost_estimate=cost(12 * npix**3, 10 * npix * npix),
        name="transform",
    )(orient, defocus, noise, image, table)


def prepare_kernel(planes_ref, weights_ref, lookup_ref):
    deep, labels = lookup_ref.shape
    rows = planes_ref.shape[1]
    level = lax.broadcasted_iota(jnp.int32, (deep // rows, rows, labels), 0)
    total = jnp.zeros((deep // rows, rows, labels), jnp.float32)
    for k in range(2):
        weight = weights_ref[k].astype(jnp.float32)
        total = total + jnp.where(level == planes_ref[k][None], weight[None], 0.0)
    lookup_ref[...] = total.reshape(deep, labels).astype(jnp.bfloat16)


def prepare(planes, weights, deep):
    labels = planes.shape[2]
    return pl.pallas_call(
        prepare_kernel,
        in_specs=[whole(), whole()],
        out_specs=whole(),
        out_shape=jax.ShapeDtypeStruct((deep, labels), jnp.bfloat16),
        compiler_params=params(SMALL),
        cost_estimate=cost(1 << 22, 1 << 20),
        name="prepare",
    )(planes, weights)


def contrast(defocus, row_square, start, width, npix):
    column = start + lax.broadcasted_iota(jnp.int32, (1, width), 1)
    freq_x = frequency(column, npix)
    chi = defocus * (row_square + freq_x * freq_x)
    turns = jnp.floor(chi * (1.0 / TURN) + (TILT / TURN + 0.5))
    angle = ((chi - turns * TURN_HIGH) - turns * TURN_LOW) + TILT
    square = angle * angle
    series = -SINE[-1]
    for term in SINE[-2::-1]:
        series = series * square - term
    return series * angle


def line_geometry(meta, ori, rows, many, npix, slot):
    place = 2 * ori
    defocus = meta[:, place : place + 1] + meta[:, place + 1 : place + 2] + meta[:, place + 2 : place + 3]
    index = (lax.broadcasted_iota(jnp.int32, (many, 1), 0) & (rows - 1)) + slot * rows
    freq_y = jnp.where(index < npix // 2, index, index - npix).astype(jnp.float32) / npix
    return defocus, freq_y * freq_y


def compare_kernel(ori, rows, slot_ref, fourier_ref, lookup_ref, volume_ref, filtered_ref, picks_ref, part_ref, about_ref, mix_ref, section_ref, power_ref):
    many, wide = filtered_ref.shape
    npix = wide // 2
    deep = volume_ref.shape[0]
    images = many // rows

    meta = fourier_ref[:, wide:]
    here = lax.broadcasted_iota(jnp.int32, (images, many), 0) << bits(rows)
    there = lax.broadcasted_iota(jnp.int32, (images, many), 1)
    pick = jnp.where(here == there, 1.0, 0.0).astype(jnp.bfloat16)
    about = jnp.dot(pick, meta, preferred_element_type=jnp.float32)
    about_ref[...] = about
    label = lax.broadcasted_iota(jnp.int32, (images, lookup_ref.shape[1]), 1).astype(jnp.float32)
    found = []
    for o in range(ori):
        mine = about[:, o : o + 1] + 256.0 * about[:, ori + o : ori + o + 1]
        found.append(jnp.where(label == mine, 1.0, 0.0).astype(jnp.bfloat16))
    found = same(jnp.concatenate(found, 0), lookup_ref[...]).astype(jnp.bfloat16)
    picks_ref[...] = found
    spread = spread_over(rows, (many, images), 1)
    for o in range(ori):
        every = jnp.dot(
            spread, found[o * images : (o + 1) * images], preferred_element_type=jnp.float32
        )
        mix_ref[o * many : (o + 1) * many, :] = (
            own_row(every, rows).reshape(many, deep).astype(jnp.bfloat16)
        )
    defocus, row_square = line_geometry(meta.astype(jnp.float32), ori, rows, many, npix, slot_ref[0])
    for number, start in enumerate(range(0, npix, 128)):
        real = slice(start, start + 128)
        imag = slice(npix + start, npix + start + 128)
        slot = number % 2
        section_ref[slot] = jnp.dot(
            mix_ref[...],
            jnp.concatenate([volume_ref[:, real], volume_ref[:, imag]], 1),
            preferred_element_type=jnp.float32,
        )
        ctf = contrast(defocus, row_square, start, 128, npix)
        for part in (real, imag):
            filtered_ref[:, part] = (ctf * fourier_ref[:, part].astype(jnp.float32)).astype(jnp.bfloat16)
        square = ctf * ctf
        for o in range(ori):
            s_real = section_ref[slot, o * many : (o + 1) * many, :128]
            s_imag = section_ref[slot, o * many : (o + 1) * many, 128:]
            power = square * (s_real * s_real + s_imag * s_imag)
            if number:
                power = power + power_ref[o]
            power_ref[o] = power

    found = own_row(same(filtered_ref[...], volume_ref[...]), rows)
    found = jnp.sum(found, axis=1)
    halves = []
    for o in range(ori):
        cross = found * picks_ref[o * images : (o + 1) * images, :].astype(jnp.float32)
        lanes = cross[:, :128]
        for start in range(128, deep, 128):
            lanes = lanes + cross[:, start : start + 128]
        power = jnp.sum(power_ref[o].reshape(images, rows, 128), axis=1)
        halves.append(lanes - 0.5 * power)
    upper = jnp.concatenate(halves[: ori // 2], 0)
    lower = jnp.concatenate(halves[ori // 2 :], 0)
    upper = jnp.sum(jnp.transpose(upper), axis=0, keepdims=True)
    lower = jnp.sum(jnp.transpose(lower), axis=0, keepdims=True)
    even = (lax.broadcasted_iota(jnp.int32, part_ref.shape, 0) & 1) == 0
    part_ref[...] = jnp.where(even, upper, lower)


def compare(slot, fourier, lookup, volume, ori, rows, copies):
    many = fourier.shape[0]
    deep, wide = volume.shape
    images = many // rows
    return pl.pallas_call(
        functools.partial(compare_kernel, ori, rows),
        in_specs=[scalar()] + [whole()] * 3,
        out_specs=(whole(),) * 4,
        out_shape=(
            jax.ShapeDtypeStruct((many, wide), jnp.bfloat16),
            jax.ShapeDtypeStruct((ori * images, deep), jnp.bfloat16),
            jax.ShapeDtypeStruct((copies * 2, 2 * images), jnp.float32),
            jax.ShapeDtypeStruct((images, META), jnp.float32),
        ),
        scratch_shapes=[
            pltpu.VMEM((ori * many, deep), jnp.bfloat16),
            pltpu.VMEM((2, ori * many, 256), jnp.float32),
            pltpu.VMEM((ori, many, 128), jnp.float32),
        ],
        compiler_params=params(LARGE),
        cost_estimate=cost(1 << 31, 5 << 20),
        name="compare",
    )(slot, fourier, lookup, volume)


def squares_kernel(ori, rows, slot_ref, about_ref, square_ref, noise_ref):
    many, npix = square_ref.shape
    images = many // rows
    about = about_ref[...]
    meta = jnp.dot(
        spread_over(rows, (many, images), 1),
        about.astype(jnp.bfloat16),
        preferred_element_type=jnp.float32,
    )
    defocus, row_square = line_geometry(meta, ori, rows, many, npix, slot_ref[0])
    for start in range(0, npix, 128):
        ctf = contrast(defocus, row_square, start, 128, npix)
        square_ref[:, start : start + 128] = (ctf * ctf).astype(jnp.bfloat16)
    place = 2 * ori + 3
    turned = jnp.transpose(jnp.concatenate([about, about], 0))
    noise_ref[...] = turned[place : place + 1] + turned[place + 1 : place + 2] + turned[place + 2 : place + 3]


def squares(slot, about, ori, rows, npix):
    images = about.shape[0]
    return pl.pallas_call(
        functools.partial(squares_kernel, ori, rows),
        in_specs=[scalar(), whole()],
        out_specs=(whole(), whole()),
        out_shape=(
            jax.ShapeDtypeStruct((images * rows, npix), jnp.bfloat16),
            jax.ShapeDtypeStruct((1, 2 * images), jnp.float32),
        ),
        compiler_params=params(SMALL),
        cost_estimate=cost(1 << 27, 1 << 20),
        name="squares",
    )(slot, about)


def project_kernel(rows, ori, core_ref, part_ref, noise_ref, picks_ref, filtered_ref, square_ref, probs_ref, keep_ref, send_ref):
    many, wide = filtered_ref.shape
    deep = picks_ref.shape[1]
    lanes = part_ref.shape[1]
    images = lanes // 2
    sums = jnp.sum(part_ref[...].reshape(part_ref.shape[0] // 8, 8, lanes), axis=0)
    sums = sums + pltpu.roll(sums, 4, 0)
    sums = sums + pltpu.roll(sums, 2, 0)
    score = sums / noise_ref[...]
    top = jnp.maximum(score, pltpu.roll(score, 1, 0))
    top = jnp.maximum(top, pltpu.roll(top, images, 1))
    power = jnp.exp(score - top)
    total = power + pltpu.roll(power, 1, 0)
    total = total + pltpu.roll(total, images, 1)
    probs = power / total
    probs_ref[...] = probs
    column = jnp.transpose(jnp.concatenate([probs] * (lanes // 8), 0))
    share = jnp.zeros((images, deep), jnp.float32)
    for o in range(ori):
        half = o % 2
        chance = column[half * images : (half + 1) * images, o // 2 : o // 2 + 1]
        share = share + chance * picks_ref[o * images : (o + 1) * images, :].astype(jnp.float32)
    share = jnp.dot(
        jnp.transpose(share).astype(jnp.bfloat16),
        spread_over(rows, (images, many), 0),
        preferred_element_type=jnp.float32,
    )
    share = own_row(share, rows).reshape(deep, many).astype(jnp.bfloat16)
    first = core_ref[0] == 0
    for source_ref, start, size in ((filtered_ref, 0, wide), (square_ref, wide, wide // 2)):
        sums = jnp.dot(share, source_ref[...], preferred_element_type=jnp.float32)
        sums = sums.reshape(keep_ref.shape[0], 2, keep_ref.shape[1], size)
        keep_ref[:, :, start : start + size] = jnp.where(first, sums[:, 0], sums[:, 1]).astype(jnp.bfloat16)
        send_ref[:, :, start : start + size] = jnp.where(first, sums[:, 1], sums[:, 0]).astype(jnp.bfloat16)


def project(core, part, noise, picks, filtered, square, rows, ori, pairs):
    many, wide = filtered.shape
    deep = picks.shape[1]
    half = jax.ShapeDtypeStruct((pairs, deep // (2 * pairs), wide + wide // 2), jnp.bfloat16)
    return pl.pallas_call(
        functools.partial(project_kernel, rows, ori),
        in_specs=[scalar()] + [whole()] * 5,
        out_specs=(whole(), whole(), whole()),
        out_shape=(jax.ShapeDtypeStruct((8, part.shape[1]), jnp.float32), half, half),
        compiler_params=params(LARGE),
        cost_estimate=cost(1 << 29, 4 << 20),
        name="project",
    )(core, part, noise, picks, filtered, square)


def middle_kernel(keep_ref, got_ref, out_ref):
    out_ref[...] = (keep_ref[...].astype(jnp.float32) + got_ref[...].astype(jnp.float32)).astype(jnp.bfloat16)


def middle(keep, got):
    return pl.pallas_call(
        middle_kernel,
        out_shape=jax.ShapeDtypeStruct(keep.shape, jnp.bfloat16),
        compiler_params=params(SMALL),
        cost_estimate=cost(1 << 20, 2 << 20),
        name="middle",
    )(keep, got)


def finish_kernel(parts_ref, data_ref, weight_ref, data_out, weight_out):
    wide = data_ref.shape[1]
    total = parts_ref[0].astype(jnp.float32)
    for source in range(1, parts_ref.shape[0]):
        total = total + parts_ref[source].astype(jnp.float32)
    data_out[...] = data_ref[...] + total[:, :wide]
    weight_out[...] = weight_ref[...] + total[:, wide:]


def finish(parts, data_old, weight_old):
    return pl.pallas_call(
        finish_kernel,
        out_shape=(
            jax.ShapeDtypeStruct(data_old.shape, jnp.float32),
            jax.ShapeDtypeStruct(weight_old.shape, jnp.float32),
        ),
        compiler_params=params(SMALL),
        cost_estimate=cost(1 << 20, 2 << 20),
        name="finish",
    )(parts, data_old, weight_old)


def on_device(images, defocus, noise, orient, planes, weights, volume, data_old, weight_old):
    npix = images.shape[1]
    ori = orient.shape[1]
    n_img = lax.axis_size("img")
    n_vol = lax.axis_size("vol")
    rows = npix // n_img
    slab = volume.shape[0]
    deep = n_vol * slab * rows
    many = n_img * rows
    pairs = n_vol // 2
    slot = lax.axis_index("img").astype(jnp.int32).reshape(1)
    place = lax.axis_index("vol").astype(jnp.int32)

    fourier = transform(
        orient, defocus.reshape(1, 1), noise.reshape(1, 1), images[0], jnp.asarray(dft_table(npix))
    )
    fourier = lax.all_to_all(
        fourier.reshape(n_img, rows, 2 * npix + META), "img", split_axis=0, concat_axis=0, tiled=True
    ).reshape(many, 2 * npix + META)
    vol_rows = lax.all_gather(volume.reshape(slab * rows, 2 * npix), "vol", axis=0, tiled=True)
    lookup = prepare(jnp.swapaxes(planes, 1, 2), jnp.swapaxes(weights, 1, 2), deep)
    filtered, picks, part, about = compare(slot, fourier, lookup, vol_rows, ori, rows, n_img)
    square, noise_all = squares(slot, about, ori, rows, npix)
    part = lax.all_to_all(
        part.reshape(n_img, 2, 2 * n_img), "img", split_axis=0, concat_axis=0, tiled=True
    ).reshape(2 * n_img, 2 * n_img)
    probs, keep, send = project(
        (place % 2).reshape(1), part, noise_all, picks, filtered, square, rows, ori, pairs
    )
    mine = lax.dynamic_slice_in_dim(
        probs[:2].reshape(2 * 2, n_img), lax.axis_index("img"), 1, 1
    ).reshape(1, ori)
    got = lax.ppermute(send, "vol", [(v, v ^ 1) for v in range(n_vol)])
    parts = lax.all_to_all(
        middle(keep, got),
        "vol",
        split_axis=0,
        concat_axis=0,
        axis_index_groups=[list(range(core, n_vol, 2)) for core in range(2)],
        tiled=True,
    )
    data, weight = finish(
        parts,
        data_old.reshape(slab * rows, 2 * npix),
        weight_old.reshape(slab * rows, npix),
    )
    return (mine, data.reshape(data_old.shape), weight.reshape(weight_old.shape))


def solution(mesh):
    placed = (
        P(("img", "vol"), None, None),
        P(("img", "vol")),
        P(("img", "vol")),
        P(("img", "vol"), None),
        P(None, None, "img"),
        P(None, None, "img"),
        P("vol", "img", None),
        P("vol", "img", None),
        P("vol", "img", None),
    )
    return jax.shard_map(
        on_device,
        mesh=mesh,
        in_specs=placed,
        out_specs=(P(("img", "vol"), None), P("vol", "img", None), P("vol", "img", None)),
        check_vma=False,
    )
```

```python
import functools
import math

import jax
import jax.numpy as jnp
import ml_dtypes
import numpy as np
from jax import lax
from jax.experimental import pallas as pl
from jax.experimental.pallas import tpu as pltpu
from jax.sharding import PartitionSpec as P

AMP = 0.1
TILT = math.asin(AMP)
TURN = 2.0 * math.pi
TURN_HIGH = math.floor(TURN * 4096) / 4096
TURN_LOW = TURN - TURN_HIGH
SINE = tuple(
    factor / TURN ** (2 * power + 1)
    for power, factor in enumerate(
        (
            6.283185272722434,
            -41.341697068956265,
            81.60502462257806,
            -76.70155117622761,
            42.01616582127327,
            -14.868610992503873,
            3.199693654235983,
        )
    )
)
HUGE = 56 * 1024 * 1024
LARGE = 32 * 1024 * 1024
SMALL = 16 * 1024 * 1024
META = 128


def dft_table(npix):
    index = np.arange(npix)
    angle = (index[:, None] * index[None, :] % npix) * (2.0 * math.pi / npix)
    scale = 1.0 / math.sqrt(npix)
    both = np.concatenate([np.cos(angle) * scale, np.sin(angle) * scale], 1)
    return both.astype(np.float32).astype(ml_dtypes.bfloat16)


def frequency(index, npix):
    return ((index + npix // 2) % npix - npix // 2).astype(jnp.float32) / npix


def params(size):
    return pltpu.CompilerParams(vmem_limit_bytes=size)


def cost(flops, size):
    return pl.CostEstimate(flops=flops, bytes_accessed=size, transcendentals=0)


def whole():
    return pl.BlockSpec(memory_space=pltpu.VMEM)


def scalar():
    return pl.BlockSpec(memory_space=pltpu.SMEM)


def same(a, b):
    return lax.dot_general(a, b, (((1,), (1,)), ((), ())), preferred_element_type=jnp.float32)


def three_parts(value):
    parts = []
    for _ in range(3):
        part = value.astype(jnp.bfloat16).astype(jnp.float32)
        parts.append(part)
        value = value - part
    return parts


def bits(rows):
    assert rows & (rows - 1) == 0
    return rows.bit_length() - 1


def spread_over(rows, shape, image_axis):
    image = lax.broadcasted_iota(jnp.int32, shape, image_axis)
    owner = lax.broadcasted_iota(jnp.int32, shape, 1 - image_axis) >> bits(rows)
    return jnp.where(owner == image, 1.0, 0.0).astype(jnp.bfloat16)


def own_row(values, rows):
    height, width = values.shape
    sublane = lax.broadcasted_iota(jnp.int32, (rows, width), 0)
    lane = lax.broadcasted_iota(jnp.int32, (rows, width), 1) & (rows - 1)
    return jnp.where((sublane == lane)[None], values.reshape(height // rows, rows, width), 0.0)


def transform_kernel(chunk, orient_hbm, defocus_hbm, noise_hbm, image_hbm, table_hbm, out_hbm, orient_ref, defocus_ref, noise_ref, image_ref, table_ref, both_ref, out_ref, in_sems, out_sems):
    npix = image_ref.shape[0]
    ori = orient_ref.shape[1]
    starts = list(range(0, 2 * npix, chunk))
    pairs = [(image_hbm, image_ref)]
    pairs += [(table_hbm.at[:, pl.ds(start, chunk)], table_ref.at[:, pl.ds(start, chunk)]) for start in starts]
    pairs += [(orient_hbm, orient_ref), (defocus_hbm, defocus_ref), (noise_hbm, noise_ref)]
    loads = []
    for number, (source, target) in enumerate(pairs):
        load = pltpu.make_async_copy(source, target, in_sems.at[number])
        load.start()
        loads.append(load)
    loads[0].wait()
    for number, start in enumerate(starts):
        loads[1 + number].wait()
        first = jnp.dot(
            image_ref[...], table_ref[:, start : start + chunk], preferred_element_type=jnp.float32
        ).astype(jnp.bfloat16)
        if start < npix:
            both_ref[:npix, start : start + chunk] = first
            both_ref[npix:, npix + start : npix + start + chunk] = -first
        else:
            both_ref[:npix, start : start + chunk] = -first
            both_ref[npix:, start - npix : start - npix + chunk] = -first
    for load in loads[1 + len(starts) :]:
        load.wait()
    saves = []

    def save(start, size):
        at = pl.ds(start, size)
        copy = pltpu.make_async_copy(out_ref.at[:, at], out_hbm.at[:, at], out_sems.at[len(saves)])
        copy.start()
        saves.append(copy)

    lane = lax.broadcasted_iota(jnp.int32, (8, META), 1)
    codes = jnp.zeros((8, META), jnp.int32)
    for o in range(ori):
        label = orient_ref[0, o]
        codes = jnp.where(lane == o, label & 255, codes)
        codes = jnp.where(lane == ori + o, label >> 8, codes)
    about = codes.astype(jnp.float32)
    place = 2 * ori
    for scalar_ref in (defocus_ref, noise_ref):
        for part in three_parts(jnp.full((8, META), scalar_ref[0], jnp.float32)):
            about = jnp.where(lane == place, part, about)
            place += 1
    out_ref[:, 2 * npix :] = jnp.broadcast_to(about[:1], (npix, META)).astype(jnp.bfloat16)
    save(2 * npix, META)
    for start in starts:
        out_ref[:, start : start + chunk] = jnp.dot(
            table_ref[...], both_ref[:, start : start + chunk], preferred_element_type=jnp.float32
        ).astype(jnp.bfloat16)
        save(start, chunk)
    for copy in saves:
        copy.wait()


def transform(orient, defocus, noise, image, table):
    npix = image.shape[0]
    chunk = npix
    pieces = 2 * npix // chunk
    return pl.pallas_call(
        functools.partial(transform_kernel, chunk),
        in_specs=[pl.BlockSpec(memory_space=pl.ANY)] * 5,
        out_specs=pl.BlockSpec(memory_space=pl.ANY),
        out_shape=jax.ShapeDtypeStruct((npix, 2 * npix + META), jnp.bfloat16),
        scratch_shapes=[
            pltpu.SMEM(orient.shape, jnp.int32),
            pltpu.SMEM(defocus.shape, jnp.float32),
            pltpu.SMEM(noise.shape, jnp.float32),
            pltpu.VMEM((npix, npix), jnp.bfloat16),
            pltpu.VMEM((npix, 2 * npix), jnp.bfloat16),
            pltpu.VMEM((2 * npix, 2 * npix), jnp.bfloat16),
            pltpu.VMEM((npix, 2 * npix + META), jnp.bfloat16),
            pltpu.SemaphoreType.DMA((pieces + 4,)),
            pltpu.SemaphoreType.DMA((pieces + 1,)),
        ],
        compiler_params=params(HUGE),
        cost_estimate=cost(12 * npix**3, 10 * npix * npix),
        name="transform",
    )(orient, defocus, noise, image, table)


def prepare_kernel(planes_ref, weights_ref, lookup_ref):
    deep, labels = lookup_ref.shape
    rows = planes_ref.shape[1]
    level = lax.broadcasted_iota(jnp.int32, (deep // rows, rows, labels), 0)
    total = jnp.zeros((deep // rows, rows, labels), jnp.float32)
    for k in range(2):
        weight = weights_ref[k].astype(jnp.float32)
        total = total + jnp.where(level == planes_ref[k][None], weight[None], 0.0)
    lookup_ref[...] = total.reshape(deep, labels).astype(jnp.bfloat16)


def prepare(planes, weights, deep):
    labels = planes.shape[2]
    return pl.pallas_call(
        prepare_kernel,
        in_specs=[whole(), whole()],
        out_specs=whole(),
        out_shape=jax.ShapeDtypeStruct((deep, labels), jnp.bfloat16),
        compiler_params=params(SMALL),
        cost_estimate=cost(1 << 22, 1 << 20),
        name="prepare",
    )(planes, weights)


def contrast(defocus, row_square, start, width, npix):
    column = start + lax.broadcasted_iota(jnp.int32, (1, width), 1)
    freq_x = frequency(column, npix)
    chi = defocus * (row_square + freq_x * freq_x)
    turns = jnp.floor(chi * (1.0 / TURN) + (TILT / TURN + 0.5))
    angle = ((chi - turns * TURN_HIGH) - turns * TURN_LOW) + TILT
    square = angle * angle
    series = -SINE[-1]
    for term in SINE[-2::-1]:
        series = series * square - term
    return series * angle


def line_geometry(meta, ori, rows, many, npix, slot):
    place = 2 * ori
    defocus = meta[:, place : place + 1] + meta[:, place + 1 : place + 2] + meta[:, place + 2 : place + 3]
    index = (lax.broadcasted_iota(jnp.int32, (many, 1), 0) & (rows - 1)) + slot * rows
    freq_y = jnp.where(index < npix // 2, index, index - npix).astype(jnp.float32) / npix
    return defocus, freq_y * freq_y


def compare_kernel(ori, rows, slot_ref, fourier_ref, lookup_ref, volume_ref, filtered_ref, picks_ref, part_ref, about_ref, mix_ref, section_ref, power_ref):
    many, wide = filtered_ref.shape
    npix = wide // 2
    deep = volume_ref.shape[0]
    images = many // rows

    meta = fourier_ref[:, wide:]
    here = lax.broadcasted_iota(jnp.int32, (images, many), 0) << bits(rows)
    there = lax.broadcasted_iota(jnp.int32, (images, many), 1)
    pick = jnp.where(here == there, 1.0, 0.0).astype(jnp.bfloat16)
    about = jnp.dot(pick, meta, preferred_element_type=jnp.float32)
    about_ref[...] = about
    label = lax.broadcasted_iota(jnp.int32, (images, lookup_ref.shape[1]), 1).astype(jnp.float32)
    found = []
    for o in range(ori):
        mine = about[:, o : o + 1] + 256.0 * about[:, ori + o : ori + o + 1]
        found.append(jnp.where(label == mine, 1.0, 0.0).astype(jnp.bfloat16))
    found = same(jnp.concatenate(found, 0), lookup_ref[...]).astype(jnp.bfloat16)
    picks_ref[...] = found
    spread = spread_over(rows, (many, images), 1)
    for o in range(ori):
        every = jnp.dot(
            spread, found[o * images : (o + 1) * images], preferred_element_type=jnp.float32
        )
        mix_ref[o * many : (o + 1) * many, :] = (
            own_row(every, rows).reshape(many, deep).astype(jnp.bfloat16)
        )
    defocus, row_square = line_geometry(meta.astype(jnp.float32), ori, rows, many, npix, slot_ref[0])
    for number, start in enumerate(range(0, npix, 128)):
        real = slice(start, start + 128)
        imag = slice(npix + start, npix + start + 128)
        slot = number % 2
        section_ref[slot] = jnp.dot(
            mix_ref[...],
            jnp.concatenate([volume_ref[:, real], volume_ref[:, imag]], 1),
            preferred_element_type=jnp.float32,
        )
        ctf = contrast(defocus, row_square, start, 128, npix)
        for part in (real, imag):
            filtered_ref[:, part] = (ctf * fourier_ref[:, part].astype(jnp.float32)).astype(jnp.bfloat16)
        square = ctf * ctf
        for o in range(ori):
            s_real = section_ref[slot, o * many : (o + 1) * many, :128]
            s_imag = section_ref[slot, o * many : (o + 1) * many, 128:]
            power = square * (s_real * s_real + s_imag * s_imag)
            if number:
                power = power + power_ref[o]
            power_ref[o] = power

    found = own_row(same(filtered_ref[...], volume_ref[...]), rows)
    found = jnp.sum(found, axis=1)
    halves = []
    for o in range(ori):
        cross = found * picks_ref[o * images : (o + 1) * images, :].astype(jnp.float32)
        lanes = cross[:, :128]
        for start in range(128, deep, 128):
            lanes = lanes + cross[:, start : start + 128]
        power = jnp.sum(power_ref[o].reshape(images, rows, 128), axis=1)
        halves.append(lanes - 0.5 * power)
    upper = jnp.concatenate(halves[: ori // 2], 0)
    lower = jnp.concatenate(halves[ori // 2 :], 0)
    upper = jnp.sum(jnp.transpose(upper), axis=0, keepdims=True)
    lower = jnp.sum(jnp.transpose(lower), axis=0, keepdims=True)
    even = (lax.broadcasted_iota(jnp.int32, part_ref.shape, 0) & 1) == 0
    part_ref[...] = jnp.where(even, upper, lower)


def compare(slot, fourier, lookup, volume, ori, rows, copies):
    many = fourier.shape[0]
    deep, wide = volume.shape
    images = many // rows
    return pl.pallas_call(
        functools.partial(compare_kernel, ori, rows),
        in_specs=[scalar()] + [whole()] * 3,
        out_specs=(whole(),) * 4,
        out_shape=(
            jax.ShapeDtypeStruct((many, wide), jnp.bfloat16),
            jax.ShapeDtypeStruct((ori * images, deep), jnp.bfloat16),
            jax.ShapeDtypeStruct((copies * 2, 2 * images), jnp.float32),
            jax.ShapeDtypeStruct((images, META), jnp.float32),
        ),
        scratch_shapes=[
            pltpu.VMEM((ori * many, deep), jnp.bfloat16),
            pltpu.VMEM((2, ori * many, 256), jnp.float32),
            pltpu.VMEM((ori, many, 128), jnp.float32),
        ],
        compiler_params=params(LARGE),
        cost_estimate=cost(1 << 31, 5 << 20),
        name="compare",
    )(slot, fourier, lookup, volume)


def squares_kernel(ori, rows, slot_ref, about_ref, square_ref, noise_ref):
    many, npix = square_ref.shape
    images = many // rows
    about = about_ref[...]
    meta = jnp.dot(
        spread_over(rows, (many, images), 1),
        about.astype(jnp.bfloat16),
        preferred_element_type=jnp.float32,
    )
    defocus, row_square = line_geometry(meta, ori, rows, many, npix, slot_ref[0])
    for start in range(0, npix, 128):
        ctf = contrast(defocus, row_square, start, 128, npix)
        square_ref[:, start : start + 128] = (ctf * ctf).astype(jnp.bfloat16)
    place = 2 * ori + 3
    turned = jnp.transpose(jnp.concatenate([about, about], 0))
    noise_ref[...] = turned[place : place + 1] + turned[place + 1 : place + 2] + turned[place + 2 : place + 3]


def squares(slot, about, ori, rows, npix):
    images = about.shape[0]
    return pl.pallas_call(
        functools.partial(squares_kernel, ori, rows),
        in_specs=[scalar(), whole()],
        out_specs=(whole(), whole()),
        out_shape=(
            jax.ShapeDtypeStruct((images * rows, npix), jnp.bfloat16),
            jax.ShapeDtypeStruct((1, 2 * images), jnp.float32),
        ),
        compiler_params=params(SMALL),
        cost_estimate=cost(1 << 27, 1 << 20),
        name="squares",
    )(slot, about)


def project_kernel(rows, ori, core_ref, part_ref, noise_ref, picks_ref, filtered_ref, square_ref, probs_ref, keep_ref, send_ref):
    many, wide = filtered_ref.shape
    deep = picks_ref.shape[1]
    lanes = part_ref.shape[1]
    images = lanes // 2
    sums = jnp.sum(part_ref[...].reshape(part_ref.shape[0] // 8, 8, lanes), axis=0)
    sums = sums + pltpu.roll(sums, 4, 0)
    sums = sums + pltpu.roll(sums, 2, 0)
    score = sums / noise_ref[...]
    top = jnp.maximum(score, pltpu.roll(score, 1, 0))
    top = jnp.maximum(top, pltpu.roll(top, images, 1))
    power = jnp.exp(score - top)
    total = power + pltpu.roll(power, 1, 0)
    total = total + pltpu.roll(total, images, 1)
    probs = power / total
    probs_ref[...] = probs
    column = jnp.transpose(jnp.concatenate([probs] * (lanes // 8), 0))
    share = jnp.zeros((images, deep), jnp.float32)
    for o in range(ori):
        half = o % 2
        chance = column[half * images : (half + 1) * images, o // 2 : o // 2 + 1]
        share = share + chance * picks_ref[o * images : (o + 1) * images, :].astype(jnp.float32)
    share = jnp.dot(
        jnp.transpose(share).astype(jnp.bfloat16),
        spread_over(rows, (images, many), 0),
        preferred_element_type=jnp.float32,
    )
    share = own_row(share, rows).reshape(deep, many).astype(jnp.bfloat16)
    first = core_ref[0] == 0
    for source_ref, start, size in ((filtered_ref, 0, wide), (square_ref, wide, wide // 2)):
        sums = jnp.dot(share, source_ref[...], preferred_element_type=jnp.float32)
        sums = sums.reshape(keep_ref.shape[0], 2, keep_ref.shape[1], size)
        keep_ref[:, :, start : start + size] = jnp.where(first, sums[:, 0], sums[:, 1]).astype(jnp.bfloat16)
        send_ref[:, :, start : start + size] = jnp.where(first, sums[:, 1], sums[:, 0]).astype(jnp.bfloat16)


def project(core, part, noise, picks, filtered, square, rows, ori, pairs):
    many, wide = filtered.shape
    deep = picks.shape[1]
    half = jax.ShapeDtypeStruct((pairs, deep // (2 * pairs), wide + wide // 2), jnp.bfloat16)
    return pl.pallas_call(
        functools.partial(project_kernel, rows, ori),
        in_specs=[scalar()] + [whole()] * 5,
        out_specs=(whole(), whole(), whole()),
        out_shape=(jax.ShapeDtypeStruct((8, part.shape[1]), jnp.float32), half, half),
        compiler_params=params(LARGE),
        cost_estimate=cost(1 << 29, 4 << 20),
        name="project",
    )(core, part, noise, picks, filtered, square)


def middle_kernel(high_ref, keep_ref, got_ref, own_ref, *send_refs):
    pairs = keep_ref.shape[0]
    for ahead in range(pairs):
        at = (high_ref[0] + ahead) % pairs
        total = keep_ref[at].astype(jnp.float32) + got_ref[at].astype(jnp.float32)
        if ahead == 0:
            own_ref[...] = total
        else:
            send_refs[ahead - 1][...] = total.astype(jnp.bfloat16)


def middle(high, keep, got):
    pairs, slab, wide = keep.shape
    return pl.pallas_call(
        middle_kernel,
        in_specs=[scalar(), whole(), whole()],
        out_specs=(whole(),) * pairs,
        out_shape=(jax.ShapeDtypeStruct((slab, wide), jnp.float32),)
        + (jax.ShapeDtypeStruct((slab, wide), jnp.bfloat16),) * (pairs - 1),
        compiler_params=params(SMALL),
        cost_estimate=cost(1 << 20, 2 << 20),
        name="middle",
    )(high, keep, got)


def finish_kernel(own_ref, *refs):
    data_ref, weight_ref, data_out, weight_out = refs[-4:]
    wide = data_ref.shape[1]
    total = own_ref[...]
    for part_ref in refs[:-4]:
        total = total + part_ref[...].astype(jnp.float32)
    data_out[...] = data_ref[...] + total[:, :wide]
    weight_out[...] = weight_ref[...] + total[:, wide:]


def finish(own, parts, data_old, weight_old):
    return pl.pallas_call(
        finish_kernel,
        out_shape=(
            jax.ShapeDtypeStruct(data_old.shape, jnp.float32),
            jax.ShapeDtypeStruct(weight_old.shape, jnp.float32),
        ),
        compiler_params=params(SMALL),
        cost_estimate=cost(1 << 20, 2 << 20),
        name="finish",
    )(own, *parts, data_old, weight_old)


def on_device(images, defocus, noise, orient, planes, weights, volume, data_old, weight_old):
    npix = images.shape[1]
    ori = orient.shape[1]
    n_img = lax.axis_size("img")
    n_vol = lax.axis_size("vol")
    rows = npix // n_img
    slab = volume.shape[0]
    deep = n_vol * slab * rows
    many = n_img * rows
    pairs = n_vol // 2
    slot = lax.axis_index("img").astype(jnp.int32).reshape(1)
    place = lax.axis_index("vol").astype(jnp.int32)

    fourier = transform(orient, defocus, noise, images[0], jnp.asarray(dft_table(npix)))
    fourier = lax.all_to_all(
        fourier.reshape(n_img, rows, 2 * npix + META), "img", split_axis=0, concat_axis=0, tiled=True
    ).reshape(many, 2 * npix + META)
    vol_rows = lax.all_gather(volume.reshape(slab * rows, 2 * npix), "vol", axis=0, tiled=True)
    lookup = prepare(jnp.swapaxes(planes, 1, 2), jnp.swapaxes(weights, 1, 2), deep)
    filtered, picks, part, about = compare(slot, fourier, lookup, vol_rows, ori, rows, n_img)
    square, noise_all = squares(slot, about, ori, rows, npix)
    part = lax.all_to_all(
        part.reshape(n_img, 2, 2 * n_img), "img", split_axis=0, concat_axis=0, tiled=True
    ).reshape(2 * n_img, 2 * n_img)
    probs, keep, send = project(
        (place % 2).reshape(1), part, noise_all, picks, filtered, square, rows, ori, pairs
    )
    mine = lax.dynamic_slice_in_dim(
        probs[:2].reshape(2 * 2, n_img), lax.axis_index("img"), 1, 1
    ).reshape(1, ori)
    got = lax.ppermute(send, "vol", [(v, v ^ 1) for v in range(n_vol)])
    own, *sends = middle((place // 2).reshape(1), keep, got)
    parts = [
        lax.ppermute(part, "vol", [(v, (v + 2 * ahead) % n_vol) for v in range(n_vol)])
        for ahead, part in enumerate(sends, 1)
    ]
    data, weight = finish(
        own,
        parts,
        data_old.reshape(slab * rows, 2 * npix),
        weight_old.reshape(slab * rows, npix),
    )
    return (mine, data.reshape(data_old.shape), weight.reshape(weight_old.shape))


def solution(mesh):
    placed = (
        P(("img", "vol"), None, None),
        P(("img", "vol")),
        P(("img", "vol")),
        P(("img", "vol"), None),
        P(None, None, "img"),
        P(None, None, "img"),
        P("vol", "img", None),
        P("vol", "img", None),
        P("vol", "img", None),
    )
    return jax.shard_map(
        on_device,
        mesh=mesh,
        in_specs=placed,
        out_specs=(P(("img", "vol"), None), P("vol", "img", None), P("vol", "img", None)),
        check_vma=False,
    )
```

```python
import functools
import math

import jax
import jax.numpy as jnp
import ml_dtypes
import numpy as np
from jax import lax
from jax.experimental import pallas as pl
from jax.experimental.pallas import tpu as pltpu
from jax.sharding import PartitionSpec as P

AMP = 0.1
TILT = math.asin(AMP)
TURN = 2.0 * math.pi
TURN_HIGH = math.floor(TURN * 4096) / 4096
TURN_LOW = TURN - TURN_HIGH
SINE = tuple(
    factor / TURN ** (2 * power + 1)
    for power, factor in enumerate(
        (
            6.283185272722434,
            -41.341697068956265,
            81.60502462257806,
            -76.70155117622761,
            42.01616582127327,
            -14.868610992503873,
            3.199693654235983,
        )
    )
)
HUGE = 56 * 1024 * 1024
LARGE = 32 * 1024 * 1024
SMALL = 16 * 1024 * 1024
META = 128


def dft_tables(npix):
    index = np.arange(npix)
    angle = (index[:, None] * index[None, :] % npix) * (2.0 * math.pi / npix)
    scale = 1.0 / math.sqrt(npix)
    parts = [np.cos(angle) * scale, np.sin(angle) * scale]
    halves = [part[: npix // 2, parity::2] for parity in range(2) for part in parts]
    return tuple(
        jnp.asarray(np.concatenate(table, 1).astype(np.float32).astype(ml_dtypes.bfloat16))
        for table in (parts, halves)
    )


def frequency(index, npix):
    return ((index + npix // 2) % npix - npix // 2).astype(jnp.float32) / npix


def params(size):
    return pltpu.CompilerParams(vmem_limit_bytes=size)


def cost(flops, size):
    return pl.CostEstimate(flops=flops, bytes_accessed=size, transcendentals=0)


def whole():
    return pl.BlockSpec(memory_space=pltpu.VMEM)


def scalar():
    return pl.BlockSpec(memory_space=pltpu.SMEM)


def same(a, b):
    return lax.dot_general(a, b, (((1,), (1,)), ((), ())), preferred_element_type=jnp.float32)


def three_parts(value):
    parts = []
    for _ in range(3):
        part = value.astype(jnp.bfloat16).astype(jnp.float32)
        parts.append(part)
        value = value - part
    return parts


def bits(rows):
    assert rows & (rows - 1) == 0
    return rows.bit_length() - 1


def spread_over(rows, shape, image_axis):
    image = lax.broadcasted_iota(jnp.int32, shape, image_axis)
    owner = lax.broadcasted_iota(jnp.int32, shape, 1 - image_axis) >> bits(rows)
    return jnp.where(owner == image, 1.0, 0.0).astype(jnp.bfloat16)


def own_row(values, rows):
    height, width = values.shape
    sublane = lax.broadcasted_iota(jnp.int32, (rows, width), 0)
    lane = lax.broadcasted_iota(jnp.int32, (rows, width), 1) & (rows - 1)
    return jnp.where((sublane == lane)[None], values.reshape(height // rows, rows, width), 0.0)


def transform_kernel(chunk, orient_hbm, defocus_hbm, noise_hbm, image_hbm, table_hbm, halves_hbm, out_hbm, orient_ref, defocus_ref, noise_ref, image_ref, wide_ref, table_ref, halves_ref, both_ref, out_ref, in_sems, out_sems):
    npix = image_ref.shape[0]
    half = npix // 2
    ori = orient_ref.shape[1]
    starts = list(range(0, 2 * npix, chunk))
    pairs = [(image_hbm, image_ref)]
    pairs += [(table_hbm.at[:, pl.ds(start, chunk)], table_ref.at[:, pl.ds(start, chunk)]) for start in starts]
    pairs += [(halves_hbm, halves_ref), (orient_hbm, orient_ref), (defocus_hbm, defocus_ref), (noise_hbm, noise_ref)]
    loads = []
    for number, (source, target) in enumerate(pairs):
        load = pltpu.make_async_copy(source, target, in_sems.at[number])
        load.start()
        loads.append(load)
    loads[0].wait()
    tiles = range(npix // 128)
    for tile in tiles:
        wide_ref[tile] = image_ref[:, tile * 128 : (tile + 1) * 128].astype(jnp.float32)
    image = jnp.concatenate(
        [
            jnp.concatenate([wide_ref[tile, pl.ds(parity, half, 2), :] for tile in tiles], 1)
            for parity in range(2)
        ],
        0,
    ).astype(jnp.bfloat16)
    for number, start in enumerate(starts):
        loads[1 + number].wait()
        first = jnp.dot(
            image, table_ref[:, start : start + chunk], preferred_element_type=jnp.float32
        ).astype(jnp.bfloat16)
        for parity in range(2):
            part = first[parity * half : (parity + 1) * half]
            upper = slice(parity * npix, parity * npix + half)
            lower = slice(parity * npix + half, (parity + 1) * npix)
            if start < npix:
                both_ref[upper, start : start + chunk] = part
                both_ref[lower, npix + start : npix + start + chunk] = -part
            else:
                both_ref[upper, start : start + chunk] = -part
                both_ref[lower, start - npix : start - npix + chunk] = -part
    for load in loads[1 + len(starts) :]:
        load.wait()
    saves = []

    def save(start, size):
        at = pl.ds(start, size)
        copy = pltpu.make_async_copy(out_ref.at[:, at], out_hbm.at[:, at], out_sems.at[len(saves)])
        copy.start()
        saves.append(copy)

    lane = lax.broadcasted_iota(jnp.int32, (8, META), 1)
    codes = jnp.zeros((8, META), jnp.int32)
    for o in range(ori):
        label = orient_ref[0, o]
        codes = jnp.where(lane == o, label & 255, codes)
        codes = jnp.where(lane == ori + o, label >> 8, codes)
    about = codes.astype(jnp.float32)
    place = 2 * ori
    for scalar_ref in (defocus_ref, noise_ref):
        for part in three_parts(jnp.full((8, META), scalar_ref[0], jnp.float32)):
            about = jnp.where(lane == place, part, about)
            place += 1
    out_ref[:, 2 * npix :] = jnp.broadcast_to(about[:1], (npix, META)).astype(jnp.bfloat16)
    save(2 * npix, META)
    for start in starts:
        even, odd = (
            jnp.dot(
                halves_ref[:, parity * npix : (parity + 1) * npix],
                both_ref[parity * npix : (parity + 1) * npix, start : start + chunk],
                preferred_element_type=jnp.float32,
            )
            for parity in range(2)
        )
        out_ref[:half, start : start + chunk] = (even + odd).astype(jnp.bfloat16)
        out_ref[half:, start : start + chunk] = (even - odd).astype(jnp.bfloat16)
        save(start, chunk)
    for copy in saves:
        copy.wait()


def transform(orient, defocus, noise, image, table, halves):
    npix = image.shape[0]
    chunk = npix
    pieces = 2 * npix // chunk
    return pl.pallas_call(
        functools.partial(transform_kernel, chunk),
        in_specs=[pl.BlockSpec(memory_space=pl.ANY)] * 6,
        out_specs=pl.BlockSpec(memory_space=pl.ANY),
        out_shape=jax.ShapeDtypeStruct((npix, 2 * npix + META), jnp.bfloat16),
        scratch_shapes=[
            pltpu.SMEM(orient.shape, jnp.int32),
            pltpu.SMEM(defocus.shape, jnp.float32),
            pltpu.SMEM(noise.shape, jnp.float32),
            pltpu.VMEM((npix, npix), jnp.bfloat16),
            pltpu.VMEM((npix // 128, npix, 128), jnp.float32),
            pltpu.VMEM((npix, 2 * npix), jnp.bfloat16),
            pltpu.VMEM((npix // 2, 2 * npix), jnp.bfloat16),
            pltpu.VMEM((2 * npix, 2 * npix), jnp.bfloat16),
            pltpu.VMEM((npix, 2 * npix + META), jnp.bfloat16),
            pltpu.SemaphoreType.DMA((pieces + 5,)),
            pltpu.SemaphoreType.DMA((pieces + 1,)),
        ],
        compiler_params=params(HUGE),
        cost_estimate=cost(12 * npix**3, 10 * npix * npix),
        name="transform",
    )(orient, defocus, noise, image, table, halves)


def prepare_kernel(planes_ref, weights_ref, lookup_ref):
    deep, labels = lookup_ref.shape
    rows = planes_ref.shape[1]
    level = lax.broadcasted_iota(jnp.int32, (deep // rows, rows, labels), 0)
    total = jnp.zeros((deep // rows, rows, labels), jnp.float32)
    for k in range(2):
        weight = weights_ref[k].astype(jnp.float32)
        total = total + jnp.where(level == planes_ref[k][None], weight[None], 0.0)
    lookup_ref[...] = total.reshape(deep, labels).astype(jnp.bfloat16)


def prepare(planes, weights, deep):
    labels = planes.shape[2]
    return pl.pallas_call(
        prepare_kernel,
        in_specs=[whole(), whole()],
        out_specs=whole(),
        out_shape=jax.ShapeDtypeStruct((deep, labels), jnp.bfloat16),
        compiler_params=params(SMALL),
        cost_estimate=cost(1 << 22, 1 << 20),
        name="prepare",
    )(planes, weights)


def contrast(defocus, row_square, start, width, npix):
    column = start + lax.broadcasted_iota(jnp.int32, (1, width), 1)
    freq_x = frequency(column, npix)
    chi = defocus * (row_square + freq_x * freq_x)
    turns = jnp.floor(chi * (1.0 / TURN) + (TILT / TURN + 0.5))
    angle = ((chi - turns * TURN_HIGH) - turns * TURN_LOW) + TILT
    square = angle * angle
    series = -SINE[-1]
    for term in SINE[-2::-1]:
        series = series * square - term
    return series * angle


def line_geometry(meta, ori, rows, many, npix, slot):
    place = 2 * ori
    defocus = meta[:, place : place + 1] + meta[:, place + 1 : place + 2] + meta[:, place + 2 : place + 3]
    index = (lax.broadcasted_iota(jnp.int32, (many, 1), 0) & (rows - 1)) + slot * rows
    freq_y = jnp.where(index < npix // 2, index, index - npix).astype(jnp.float32) / npix
    return defocus, freq_y * freq_y


def compare_kernel(ori, rows, slot_ref, fourier_ref, lookup_ref, volume_ref, filtered_ref, picks_ref, part_ref, about_ref, mix_ref, section_ref, power_ref):
    many, wide = filtered_ref.shape
    npix = wide // 2
    deep = volume_ref.shape[0]
    images = many // rows

    meta = fourier_ref[:, wide:]
    here = lax.broadcasted_iota(jnp.int32, (images, many), 0) << bits(rows)
    there = lax.broadcasted_iota(jnp.int32, (images, many), 1)
    pick = jnp.where(here == there, 1.0, 0.0).astype(jnp.bfloat16)
    about = jnp.dot(pick, meta, preferred_element_type=jnp.float32)
    about_ref[...] = about
    label = lax.broadcasted_iota(jnp.int32, (images, lookup_ref.shape[1]), 1).astype(jnp.float32)
    found = []
    for o in range(ori):
        mine = about[:, o : o + 1] + 256.0 * about[:, ori + o : ori + o + 1]
        found.append(jnp.where(label == mine, 1.0, 0.0).astype(jnp.bfloat16))
    found = same(jnp.concatenate(found, 0), lookup_ref[...]).astype(jnp.bfloat16)
    picks_ref[...] = found
    spread = spread_over(rows, (many, images), 1)
    for o in range(ori):
        every = jnp.dot(
            spread, found[o * images : (o + 1) * images], preferred_element_type=jnp.float32
        )
        mix_ref[o * many : (o + 1) * many, :] = (
            own_row(every, rows).reshape(many, deep).astype(jnp.bfloat16)
        )
    defocus, row_square = line_geometry(meta.astype(jnp.float32), ori, rows, many, npix, slot_ref[0])
    for number, start in enumerate(range(0, npix, 128)):
        real = slice(start, start + 128)
        imag = slice(npix + start, npix + start + 128)
        slot = number % 2
        section_ref[slot] = jnp.dot(
            mix_ref[...],
            jnp.concatenate([volume_ref[:, real], volume_ref[:, imag]], 1),
            preferred_element_type=jnp.float32,
        )
        ctf = contrast(defocus, row_square, start, 128, npix)
        for part in (real, imag):
            filtered_ref[:, part] = (ctf * fourier_ref[:, part].astype(jnp.float32)).astype(jnp.bfloat16)
        square = ctf * ctf
        for o in range(ori):
            s_real = section_ref[slot, o * many : (o + 1) * many, :128]
            s_imag = section_ref[slot, o * many : (o + 1) * many, 128:]
            power = square * (s_real * s_real + s_imag * s_imag)
            if number:
                power = power + power_ref[o]
            power_ref[o] = power

    found = own_row(same(filtered_ref[...], volume_ref[...]), rows)
    found = jnp.sum(found, axis=1)
    halves = []
    for o in range(ori):
        cross = found * picks_ref[o * images : (o + 1) * images, :].astype(jnp.float32)
        lanes = cross[:, :128]
        for start in range(128, deep, 128):
            lanes = lanes + cross[:, start : start + 128]
        power = jnp.sum(power_ref[o].reshape(images, rows, 128), axis=1)
        halves.append(lanes - 0.5 * power)
    upper = jnp.concatenate(halves[: ori // 2], 0)
    lower = jnp.concatenate(halves[ori // 2 :], 0)
    upper = jnp.sum(jnp.transpose(upper), axis=0, keepdims=True)
    lower = jnp.sum(jnp.transpose(lower), axis=0, keepdims=True)
    even = (lax.broadcasted_iota(jnp.int32, part_ref.shape, 0) & 1) == 0
    part_ref[...] = jnp.where(even, upper, lower)


def compare(slot, fourier, lookup, volume, ori, rows, copies):
    many = fourier.shape[0]
    deep, wide = volume.shape
    images = many // rows
    return pl.pallas_call(
        functools.partial(compare_kernel, ori, rows),
        in_specs=[scalar()] + [whole()] * 3,
        out_specs=(whole(),) * 4,
        out_shape=(
            jax.ShapeDtypeStruct((many, wide), jnp.bfloat16),
            jax.ShapeDtypeStruct((ori * images, deep), jnp.bfloat16),
            jax.ShapeDtypeStruct((copies * 2, 2 * images), jnp.float32),
            jax.ShapeDtypeStruct((images, META), jnp.float32),
        ),
        scratch_shapes=[
            pltpu.VMEM((ori * many, deep), jnp.bfloat16),
            pltpu.VMEM((2, ori * many, 256), jnp.float32),
            pltpu.VMEM((ori, many, 128), jnp.float32),
        ],
        compiler_params=params(LARGE),
        cost_estimate=cost(1 << 31, 5 << 20),
        name="compare",
    )(slot, fourier, lookup, volume)


def squares_kernel(ori, rows, npix, slot_ref, about_ref, square_ref, noise_ref):
    many = square_ref.shape[0]
    images = many // rows
    about = about_ref[...]
    meta = jnp.dot(
        spread_over(rows, (many, images), 1),
        about.astype(jnp.bfloat16),
        preferred_element_type=jnp.float32,
    )
    defocus, row_square = line_geometry(meta, ori, rows, many, npix, slot_ref[0])
    for start in range(0, square_ref.shape[1], 128):
        ctf = contrast(defocus, row_square, start, 128, npix)
        square_ref[:, start : start + 128] = (ctf * ctf).astype(jnp.bfloat16)
    place = 2 * ori + 3
    turned = jnp.transpose(jnp.concatenate([about, about], 0))
    noise_ref[...] = turned[place : place + 1] + turned[place + 1 : place + 2] + turned[place + 2 : place + 3]


def squares(slot, about, ori, rows, npix):
    images = about.shape[0]
    return pl.pallas_call(
        functools.partial(squares_kernel, ori, rows, npix),
        in_specs=[scalar(), whole()],
        out_specs=(whole(), whole()),
        out_shape=(
            jax.ShapeDtypeStruct((images * rows, npix // 2 + 128), jnp.bfloat16),
            jax.ShapeDtypeStruct((1, 2 * images), jnp.float32),
        ),
        compiler_params=params(SMALL),
        cost_estimate=cost(1 << 27, 1 << 20),
        name="squares",
    )(slot, about)


def project_kernel(rows, ori, core_ref, part_ref, noise_ref, picks_ref, filtered_ref, square_ref, probs_ref, keep_ref, send_ref):
    many, wide = filtered_ref.shape
    deep = picks_ref.shape[1]
    lanes = part_ref.shape[1]
    images = lanes // 2
    sums = jnp.sum(part_ref[...].reshape(part_ref.shape[0] // 8, 8, lanes), axis=0)
    sums = sums + pltpu.roll(sums, 4, 0)
    sums = sums + pltpu.roll(sums, 2, 0)
    score = sums / noise_ref[...]
    top = jnp.maximum(score, pltpu.roll(score, 1, 0))
    top = jnp.maximum(top, pltpu.roll(top, images, 1))
    power = jnp.exp(score - top)
    total = power + pltpu.roll(power, 1, 0)
    total = total + pltpu.roll(total, images, 1)
    probs = power / total
    probs_ref[...] = probs
    column = jnp.transpose(jnp.concatenate([probs] * (lanes // 8), 0))
    share = jnp.zeros((images, deep), jnp.float32)
    for o in range(ori):
        half = o % 2
        chance = column[half * images : (half + 1) * images, o // 2 : o // 2 + 1]
        share = share + chance * picks_ref[o * images : (o + 1) * images, :].astype(jnp.float32)
    share = jnp.dot(
        jnp.transpose(share).astype(jnp.bfloat16),
        spread_over(rows, (images, many), 0),
        preferred_element_type=jnp.float32,
    )
    share = own_row(share, rows).reshape(deep, many).astype(jnp.bfloat16)
    first = core_ref[0] == 0
    pairs = keep_ref.shape[0]
    slab = deep // (2 * pairs)
    tiles = (wide + square_ref.shape[1]) // 128 - 1
    for source_ref, start in ((filtered_ref, 0), (square_ref, wide // 128)):
        sums = jnp.dot(share, source_ref[...], preferred_element_type=jnp.float32)
        for number in range(sums.shape[1] // 128):
            tile = sums[:, number * 128 : (number + 1) * 128].reshape(pairs, 2, slab, 128)
            ours, theirs = tile[:, 0], tile[:, 1]
            ours, theirs = jnp.where(first, ours, theirs), jnp.where(first, theirs, ours)
            at = (start + number) * slab
            for target_ref, value in ((keep_ref, ours), (send_ref, theirs)):
                if start + number < tiles:
                    target_ref[:, at : at + slab, :] = value.astype(jnp.bfloat16)
                else:
                    lane = lax.broadcasted_iota(jnp.int32, (pairs, slab // 2, 128), 2)
                    lower = jnp.broadcast_to(value[:, slab // 2 :, :1], lane.shape)
                    value = jnp.where(lane == 0, value[:, : slab // 2], lower)
                    target_ref[:, at : at + slab // 2, :] = value.astype(jnp.bfloat16)


def project(core, part, noise, picks, filtered, square, rows, ori, pairs):
    many, wide = filtered.shape
    deep = picks.shape[1]
    slab = deep // (2 * pairs)
    lines = (wide + square.shape[1]) // 128 * slab - slab // 2
    half = jax.ShapeDtypeStruct((pairs, lines, 128), jnp.bfloat16)
    return pl.pallas_call(
        functools.partial(project_kernel, rows, ori),
        in_specs=[scalar()] + [whole()] * 5,
        out_specs=(whole(), whole(), whole()),
        out_shape=(jax.ShapeDtypeStruct((8, part.shape[1]), jnp.float32), half, half),
        compiler_params=params(LARGE),
        cost_estimate=cost(1 << 29, 4 << 20),
        name="project",
    )(core, part, noise, picks, filtered, square)


def middle_kernel(high_ref, keep_ref, got_ref, own_ref, *send_refs):
    pairs = keep_ref.shape[0]
    for ahead in range(pairs):
        at = (high_ref[0] + ahead) % pairs
        total = keep_ref[at].astype(jnp.float32) + got_ref[at].astype(jnp.float32)
        if ahead == 0:
            own_ref[...] = total
        else:
            send_refs[ahead - 1][...] = total.astype(jnp.bfloat16)


def middle(high, keep, got):
    pairs, slab, wide = keep.shape
    return pl.pallas_call(
        middle_kernel,
        in_specs=[scalar(), whole(), whole()],
        out_specs=(whole(),) * pairs,
        out_shape=(jax.ShapeDtypeStruct((slab, wide), jnp.float32),)
        + (jax.ShapeDtypeStruct((slab, wide), jnp.bfloat16),) * (pairs - 1),
        compiler_params=params(SMALL),
        cost_estimate=cost(1 << 20, 2 << 20),
        name="middle",
    )(high, keep, got)


def finish_kernel(own_ref, *refs):
    data_ref, weight_ref, data_out, weight_out = refs[-4:]
    slab, npix = weight_ref.shape
    half = npix // 2
    total = own_ref[...]
    for part_ref in refs[:-4]:
        total = total + part_ref[...].astype(jnp.float32)
    for start in range(0, 2 * npix, 128):
        at = start // 128 * slab
        data_out[:, start : start + 128] = data_ref[:, start : start + 128] + total[at : at + slab]
    lower = []
    for start in range(0, half, 128):
        at = (2 * npix + start) // 128 * slab
        lower.append(total[at : at + slab])
    lower = jnp.concatenate(lower, 1)
    weight_out[:, :half] = weight_ref[:, :half] + lower
    source = lax.broadcasted_iota(jnp.int32, (half, half), 0)
    target = lax.broadcasted_iota(jnp.int32, (half, half), 1)
    upper = jnp.dot(
        lower,
        jnp.where(source + target == half, 1.0, 0.0),
        preferred_element_type=jnp.float32,
        precision=lax.Precision.HIGHEST,
    )
    last = total[total.shape[0] - slab // 2 :]
    last = jnp.concatenate([last[:, :1], last[:, 1:2]], 0)
    lane = lax.broadcasted_iota(jnp.int32, (slab, half), 1)
    weight_out[:, half:] = weight_ref[:, half:] + jnp.where(lane == 0, last, upper)


def finish(own, parts, data_old, weight_old):
    return pl.pallas_call(
        finish_kernel,
        out_shape=(
            jax.ShapeDtypeStruct(data_old.shape, jnp.float32),
            jax.ShapeDtypeStruct(weight_old.shape, jnp.float32),
        ),
        compiler_params=params(SMALL),
        cost_estimate=cost(1 << 20, 2 << 20),
        name="finish",
    )(own, *parts, data_old, weight_old)


def on_device(images, defocus, noise, orient, planes, weights, volume, data_old, weight_old):
    npix = images.shape[1]
    ori = orient.shape[1]
    n_img = lax.axis_size("img")
    n_vol = lax.axis_size("vol")
    rows = npix // n_img
    slab = volume.shape[0]
    deep = n_vol * slab * rows
    many = n_img * rows
    pairs = n_vol // 2
    slot = lax.axis_index("img").astype(jnp.int32).reshape(1)
    place = lax.axis_index("vol").astype(jnp.int32)

    fourier = transform(orient, defocus, noise, images[0], *dft_tables(npix))
    fourier = lax.all_to_all(
        fourier.reshape(n_img, rows, 2 * npix + META), "img", split_axis=0, concat_axis=0, tiled=True
    ).reshape(many, 2 * npix + META)
    vol_rows = lax.all_gather(volume.reshape(slab * rows, 2 * npix), "vol", axis=0, tiled=True)
    lookup = prepare(jnp.swapaxes(planes, 1, 2), jnp.swapaxes(weights, 1, 2), deep)
    filtered, picks, part, about = compare(slot, fourier, lookup, vol_rows, ori, rows, n_img)
    square, noise_all = squares(slot, about, ori, rows, npix)
    part = lax.all_to_all(
        part.reshape(n_img, 2, 2 * n_img), "img", split_axis=0, concat_axis=0, tiled=True
    ).reshape(2 * n_img, 2 * n_img)
    probs, keep, send = project(
        (place % 2).reshape(1), part, noise_all, picks, filtered, square, rows, ori, pairs
    )
    mine = lax.dynamic_slice_in_dim(
        probs[:2].reshape(2 * 2, n_img), lax.axis_index("img"), 1, 1
    ).reshape(1, ori)
    got = lax.ppermute(send, "vol", [(v, v ^ 1) for v in range(n_vol)])
    own, *sends = middle((place // 2).reshape(1), keep, got)
    parts = [
        lax.ppermute(part, "vol", [(v, (v + 2 * ahead) % n_vol) for v in range(n_vol)])
        for ahead, part in enumerate(sends, 1)
    ]
    data, weight = finish(
        own,
        parts,
        data_old.reshape(slab * rows, 2 * npix),
        weight_old.reshape(slab * rows, npix),
    )
    return (mine, data.reshape(data_old.shape), weight.reshape(weight_old.shape))


def solution(mesh):
    placed = (
        P(("img", "vol"), None, None),
        P(("img", "vol")),
        P(("img", "vol")),
        P(("img", "vol"), None),
        P(None, None, "img"),
        P(None, None, "img"),
        P("vol", "img", None),
        P("vol", "img", None),
        P("vol", "img", None),
    )
    return jax.shard_map(
        on_device,
        mesh=mesh,
        in_specs=placed,
        out_specs=(P(("img", "vol"), None), P("vol", "img", None), P("vol", "img", None)),
        check_vma=False,
    )
```

```python
import functools
import math

import jax
import jax.numpy as jnp
import ml_dtypes
import numpy as np
from jax import lax
from jax.experimental import pallas as pl
from jax.experimental.pallas import tpu as pltpu
from jax.sharding import PartitionSpec as P

AMP = 0.1
TILT = math.asin(AMP)
TURN = 2.0 * math.pi
TURN_HIGH = math.floor(TURN * 4096) / 4096
TURN_LOW = TURN - TURN_HIGH
SINE = tuple(
    factor / TURN ** (2 * power + 1)
    for power, factor in enumerate(
        (
            6.283185272722434,
            -41.341697068956265,
            81.60502462257806,
            -76.70155117622761,
            42.01616582127327,
            -14.868610992503873,
            3.199693654235983,
        )
    )
)
HUGE = 56 * 1024 * 1024
LARGE = 32 * 1024 * 1024
SMALL = 16 * 1024 * 1024
META = 128


def dft_tables(npix):
    index = np.arange(npix)
    angle = (index[:, None] * index[None, :] % npix) * (2.0 * math.pi / npix)
    scale = 1.0 / math.sqrt(npix)
    parts = [np.cos(angle) * scale, np.sin(angle) * scale]
    halves = [part[: npix // 2, parity::2] for parity in range(2) for part in parts]
    return tuple(
        jnp.asarray(np.concatenate(table, 1).astype(np.float32).astype(ml_dtypes.bfloat16))
        for table in (parts, halves)
    )


def frequency(index, npix):
    return ((index + npix // 2) % npix - npix // 2).astype(jnp.float32) / npix


def params(size):
    return pltpu.CompilerParams(vmem_limit_bytes=size)


def cost(flops, size):
    return pl.CostEstimate(flops=flops, bytes_accessed=size, transcendentals=0)


def whole():
    return pl.BlockSpec(memory_space=pltpu.VMEM)


def scalar():
    return pl.BlockSpec(memory_space=pltpu.SMEM)


def same(a, b):
    return lax.dot_general(a, b, (((1,), (1,)), ((), ())), preferred_element_type=jnp.float32)


def three_parts(value):
    parts = []
    for _ in range(3):
        part = value.astype(jnp.bfloat16).astype(jnp.float32)
        parts.append(part)
        value = value - part
    return parts


def bits(rows):
    assert rows & (rows - 1) == 0
    return rows.bit_length() - 1


def spread_over(rows, shape, image_axis):
    image = lax.broadcasted_iota(jnp.int32, shape, image_axis)
    owner = lax.broadcasted_iota(jnp.int32, shape, 1 - image_axis) >> bits(rows)
    return jnp.where(owner == image, 1.0, 0.0).astype(jnp.bfloat16)


def own_row(values, rows):
    height, width = values.shape
    sublane = lax.broadcasted_iota(jnp.int32, (rows, width), 0)
    lane = lax.broadcasted_iota(jnp.int32, (rows, width), 1) & (rows - 1)
    return jnp.where((sublane == lane)[None], values.reshape(height // rows, rows, width), 0.0)


def transform_kernel(chunk, orient_hbm, defocus_hbm, noise_hbm, image_hbm, table_hbm, halves_hbm, out_hbm, orient_ref, defocus_ref, noise_ref, image_ref, wide_ref, table_ref, halves_ref, both_ref, out_ref, in_sems, out_sems):
    npix = image_ref.shape[0]
    half = npix // 2
    ori = orient_ref.shape[1]
    starts = list(range(0, 2 * npix, chunk))
    pairs = [(image_hbm, image_ref)]
    pairs += [(table_hbm.at[:, pl.ds(start, chunk)], table_ref.at[:, pl.ds(start, chunk)]) for start in starts]
    pairs += [(halves_hbm, halves_ref), (orient_hbm, orient_ref), (defocus_hbm, defocus_ref), (noise_hbm, noise_ref)]
    loads = []
    for number, (source, target) in enumerate(pairs):
        load = pltpu.make_async_copy(source, target, in_sems.at[number])
        load.start()
        loads.append(load)
    loads[0].wait()
    tiles = range(npix // 128)
    for tile in tiles:
        wide_ref[tile] = image_ref[:, tile * 128 : (tile + 1) * 128].astype(jnp.float32)
    image = jnp.concatenate(
        [
            jnp.concatenate([wide_ref[tile, pl.ds(parity, half, 2), :] for tile in tiles], 1)
            for parity in range(2)
        ],
        0,
    ).astype(jnp.bfloat16)
    for number, start in enumerate(starts):
        loads[1 + number].wait()
        first = jnp.dot(
            image, table_ref[:, start : start + chunk], preferred_element_type=jnp.float32
        ).astype(jnp.bfloat16)
        for parity in range(2):
            part = first[parity * half : (parity + 1) * half]
            upper = slice(parity * npix, parity * npix + half)
            lower = slice(parity * npix + half, (parity + 1) * npix)
            if start < npix:
                both_ref[upper, start : start + chunk] = part
                both_ref[lower, npix + start : npix + start + chunk] = -part
            else:
                both_ref[upper, start : start + chunk] = -part
                both_ref[lower, start - npix : start - npix + chunk] = -part
    for load in loads[1 + len(starts) :]:
        load.wait()
    saves = []

    def save(start, size):
        at = pl.ds(start, size)
        copy = pltpu.make_async_copy(out_ref.at[:, at], out_hbm.at[:, at], out_sems.at[len(saves)])
        copy.start()
        saves.append(copy)

    lane = lax.broadcasted_iota(jnp.int32, (8, META), 1)
    codes = jnp.zeros((8, META), jnp.int32)
    for o in range(ori):
        label = orient_ref[0, o]
        codes = jnp.where(lane == o, label & 255, codes)
        codes = jnp.where(lane == ori + o, label >> 8, codes)
    about = codes.astype(jnp.float32)
    place = 2 * ori
    for scalar_ref in (defocus_ref, noise_ref):
        for part in three_parts(jnp.full((8, META), scalar_ref[0], jnp.float32)):
            about = jnp.where(lane == place, part, about)
            place += 1
    out_ref[:, 2 * npix :] = jnp.broadcast_to(about[:1], (npix, META)).astype(jnp.bfloat16)
    save(2 * npix, META)
    chunk = chunk // 2
    for start in range(0, 2 * npix, chunk):
        even, odd = (
            jnp.dot(
                halves_ref[:, parity * npix : (parity + 1) * npix],
                both_ref[parity * npix : (parity + 1) * npix, start : start + chunk],
                preferred_element_type=jnp.float32,
            )
            for parity in range(2)
        )
        out_ref[:half, start : start + chunk] = (even + odd).astype(jnp.bfloat16)
        out_ref[half:, start : start + chunk] = (even - odd).astype(jnp.bfloat16)
        save(start, chunk)
    for copy in saves:
        copy.wait()


def transform(orient, defocus, noise, image, table, halves):
    npix = image.shape[0]
    chunk = npix
    pieces = 2 * npix // chunk
    return pl.pallas_call(
        functools.partial(transform_kernel, chunk),
        in_specs=[pl.BlockSpec(memory_space=pl.ANY)] * 6,
        out_specs=pl.BlockSpec(memory_space=pl.ANY),
        out_shape=jax.ShapeDtypeStruct((npix, 2 * npix + META), jnp.bfloat16),
        scratch_shapes=[
            pltpu.SMEM(orient.shape, jnp.int32),
            pltpu.SMEM(defocus.shape, jnp.float32),
            pltpu.SMEM(noise.shape, jnp.float32),
            pltpu.VMEM((npix, npix), jnp.bfloat16),
            pltpu.VMEM((npix // 128, npix, 128), jnp.float32),
            pltpu.VMEM((npix, 2 * npix), jnp.bfloat16),
            pltpu.VMEM((npix // 2, 2 * npix), jnp.bfloat16),
            pltpu.VMEM((2 * npix, 2 * npix), jnp.bfloat16),
            pltpu.VMEM((npix, 2 * npix + META), jnp.bfloat16),
            pltpu.SemaphoreType.DMA((pieces + 5,)),
            pltpu.SemaphoreType.DMA((2 * pieces + 1,)),
        ],
        compiler_params=params(HUGE),
        cost_estimate=cost(12 * npix**3, 10 * npix * npix),
        name="transform",
    )(orient, defocus, noise, image, table, halves)


def prepare_kernel(planes_ref, weights_ref, lookup_ref):
    deep, labels = lookup_ref.shape
    rows = planes_ref.shape[1]
    level = lax.broadcasted_iota(jnp.int32, (deep // rows, rows, labels), 0)
    total = jnp.zeros((deep // rows, rows, labels), jnp.float32)
    for k in range(2):
        weight = weights_ref[k].astype(jnp.float32)
        total = total + jnp.where(level == planes_ref[k][None], weight[None], 0.0)
    lookup_ref[...] = total.reshape(deep, labels).astype(jnp.bfloat16)


def prepare(planes, weights, deep):
    labels = planes.shape[2]
    return pl.pallas_call(
        prepare_kernel,
        in_specs=[whole(), whole()],
        out_specs=whole(),
        out_shape=jax.ShapeDtypeStruct((deep, labels), jnp.bfloat16),
        compiler_params=params(SMALL),
        cost_estimate=cost(1 << 22, 1 << 20),
        name="prepare",
    )(planes, weights)


def contrast(defocus, row_square, start, width, npix):
    column = start + lax.broadcasted_iota(jnp.int32, (1, width), 1)
    freq_x = frequency(column, npix)
    chi = defocus * (row_square + freq_x * freq_x)
    turns = jnp.floor(chi * (1.0 / TURN) + (TILT / TURN + 0.5))
    angle = ((chi - turns * TURN_HIGH) - turns * TURN_LOW) + TILT
    square = angle * angle
    series = -SINE[-1]
    for term in SINE[-2::-1]:
        series = series * square - term
    return series * angle


def line_geometry(meta, ori, rows, many, npix, slot):
    place = 2 * ori
    defocus = meta[:, place : place + 1] + meta[:, place + 1 : place + 2] + meta[:, place + 2 : place + 3]
    index = (lax.broadcasted_iota(jnp.int32, (many, 1), 0) & (rows - 1)) + slot * rows
    freq_y = jnp.where(index < npix // 2, index, index - npix).astype(jnp.float32) / npix
    return defocus, freq_y * freq_y


def compare_kernel(ori, rows, slot_ref, fourier_ref, lookup_ref, volume_ref, filtered_ref, picks_ref, part_ref, about_ref, mix_ref, power_ref):
    many, wide = filtered_ref.shape
    npix = wide // 2
    deep = volume_ref.shape[0]
    images = many // rows

    meta = fourier_ref[:, wide:]
    here = lax.broadcasted_iota(jnp.int32, (images, many), 0) << bits(rows)
    there = lax.broadcasted_iota(jnp.int32, (images, many), 1)
    pick = jnp.where(here == there, 1.0, 0.0).astype(jnp.bfloat16)
    about = jnp.dot(pick, meta, preferred_element_type=jnp.float32)
    about_ref[...] = about
    label = lax.broadcasted_iota(jnp.int32, (images, lookup_ref.shape[1]), 1).astype(jnp.float32)
    found = []
    for o in range(ori):
        mine = about[:, o : o + 1] + 256.0 * about[:, ori + o : ori + o + 1]
        found.append(jnp.where(label == mine, 1.0, 0.0).astype(jnp.bfloat16))
    found = same(jnp.concatenate(found, 0), lookup_ref[...]).astype(jnp.bfloat16)
    picks_ref[...] = found
    spread = spread_over(rows, (many, images), 1)
    for o in range(ori):
        every = jnp.dot(
            spread, found[o * images : (o + 1) * images], preferred_element_type=jnp.float32
        )
        mix_ref[o * many : (o + 1) * many, :] = (
            own_row(every, rows).reshape(many, deep).astype(jnp.bfloat16)
        )
    defocus, row_square = line_geometry(meta.astype(jnp.float32), ori, rows, many, npix, slot_ref[0])
    for number, start in enumerate(range(0, npix, 128)):
        real = slice(start, start + 128)
        imag = slice(npix + start, npix + start + 128)
        planes = jnp.concatenate([volume_ref[:, real], volume_ref[:, imag]], 1)
        ctf = contrast(defocus, row_square, start, 128, npix)
        for part in (real, imag):
            filtered_ref[:, part] = (ctf * fourier_ref[:, part].astype(jnp.float32)).astype(jnp.bfloat16)
        square = ctf * ctf
        for o in range(ori):
            section = jnp.dot(
                mix_ref[o * many : (o + 1) * many, :], planes, preferred_element_type=jnp.float32
            )
            section = section * section
            power = square * (section[:, :128] + section[:, 128:])
            if number:
                power = power + power_ref[o]
            power_ref[o] = power

    found = own_row(same(filtered_ref[...], volume_ref[...]), rows)
    found = jnp.sum(found, axis=1)
    halves = []
    for o in range(ori):
        cross = found * picks_ref[o * images : (o + 1) * images, :].astype(jnp.float32)
        lanes = cross[:, :128]
        for start in range(128, deep, 128):
            lanes = lanes + cross[:, start : start + 128]
        power = jnp.sum(power_ref[o].reshape(images, rows, 128), axis=1)
        halves.append(lanes - 0.5 * power)
    upper = jnp.concatenate(halves[: ori // 2], 0)
    lower = jnp.concatenate(halves[ori // 2 :], 0)
    upper = jnp.sum(jnp.transpose(upper), axis=0, keepdims=True)
    lower = jnp.sum(jnp.transpose(lower), axis=0, keepdims=True)
    even = (lax.broadcasted_iota(jnp.int32, part_ref.shape, 0) & 1) == 0
    part_ref[...] = jnp.where(even, upper, lower)


def compare(slot, fourier, lookup, volume, ori, rows, copies):
    many = fourier.shape[0]
    deep, wide = volume.shape
    images = many // rows
    return pl.pallas_call(
        functools.partial(compare_kernel, ori, rows),
        in_specs=[scalar()] + [whole()] * 3,
        out_specs=(whole(),) * 4,
        out_shape=(
            jax.ShapeDtypeStruct((many, wide), jnp.bfloat16),
            jax.ShapeDtypeStruct((ori * images, deep), jnp.bfloat16),
            jax.ShapeDtypeStruct((copies * 2, 2 * images), jnp.float32),
            jax.ShapeDtypeStruct((images, META), jnp.float32),
        ),
        scratch_shapes=[
            pltpu.VMEM((ori * many, deep), jnp.bfloat16),
            pltpu.VMEM((ori, many, 128), jnp.float32),
        ],
        compiler_params=params(LARGE),
        cost_estimate=cost(1 << 31, 5 << 20),
        name="compare",
    )(slot, fourier, lookup, volume)


def squares_kernel(ori, rows, npix, slot_ref, about_ref, square_ref, noise_ref):
    many = square_ref.shape[0]
    images = many // rows
    about = about_ref[...]
    meta = jnp.dot(
        spread_over(rows, (many, images), 1),
        about.astype(jnp.bfloat16),
        preferred_element_type=jnp.float32,
    )
    defocus, row_square = line_geometry(meta, ori, rows, many, npix, slot_ref[0])
    for start in range(0, square_ref.shape[1], 128):
        ctf = contrast(defocus, row_square, start, 128, npix)
        square_ref[:, start : start + 128] = (ctf * ctf).astype(jnp.bfloat16)
    place = 2 * ori + 3
    turned = jnp.transpose(jnp.concatenate([about, about], 0))
    noise_ref[...] = turned[place : place + 1] + turned[place + 1 : place + 2] + turned[place + 2 : place + 3]


def squares(slot, about, ori, rows, npix):
    images = about.shape[0]
    return pl.pallas_call(
        functools.partial(squares_kernel, ori, rows, npix),
        in_specs=[scalar(), whole()],
        out_specs=(whole(), whole()),
        out_shape=(
            jax.ShapeDtypeStruct((images * rows, npix // 2 + 128), jnp.bfloat16),
            jax.ShapeDtypeStruct((1, 2 * images), jnp.float32),
        ),
        compiler_params=params(SMALL),
        cost_estimate=cost(1 << 27, 1 << 20),
        name="squares",
    )(slot, about)


def pack(target_ref, share, source_ref, start, last):
    pairs = target_ref.shape[0]
    slab = share.shape[0] // pairs
    sums = jnp.dot(share, source_ref[...], preferred_element_type=jnp.float32)
    for number in range(sums.shape[1] // 128):
        value = sums[:, number * 128 : (number + 1) * 128].reshape(pairs, slab, 128)
        at = (start + number) * slab
        if start + number < last:
            target_ref[:, at : at + slab, :] = value.astype(jnp.bfloat16)
        else:
            lane = lax.broadcasted_iota(jnp.int32, (pairs, slab // 2, 128), 2)
            lower = jnp.broadcast_to(value[:, slab // 2 :, :1], lane.shape)
            value = jnp.where(lane == 0, value[:, : slab // 2], lower)
            target_ref[:, at : at + slab // 2, :] = value.astype(jnp.bfloat16)


def pack_both(target_ref, share, filtered_ref, square_ref):
    tiles = filtered_ref.shape[1] // 128
    last = tiles + square_ref.shape[1] // 128 - 1
    pack(target_ref, share, filtered_ref, 0, last)
    pack(target_ref, share, square_ref, tiles, last)


def project_kernel(rows, ori, core_ref, part_ref, noise_ref, picks_ref, filtered_ref, square_ref, probs_ref, share_ref, send_ref):
    many = filtered_ref.shape[0]
    deep = picks_ref.shape[1]
    lanes = part_ref.shape[1]
    images = lanes // 2
    sums = jnp.sum(part_ref[...].reshape(part_ref.shape[0] // 8, 8, lanes), axis=0)
    sums = sums + pltpu.roll(sums, 4, 0)
    sums = sums + pltpu.roll(sums, 2, 0)
    score = sums / noise_ref[...]
    top = jnp.maximum(score, pltpu.roll(score, 1, 0))
    top = jnp.maximum(top, pltpu.roll(top, images, 1))
    power = jnp.exp(score - top)
    total = power + pltpu.roll(power, 1, 0)
    total = total + pltpu.roll(total, images, 1)
    probs = power / total
    probs_ref[...] = probs
    column = jnp.transpose(jnp.concatenate([probs] * (lanes // 8), 0))
    share = jnp.zeros((images, deep), jnp.float32)
    for o in range(ori):
        half = o % 2
        chance = column[half * images : (half + 1) * images, o // 2 : o // 2 + 1]
        share = share + chance * picks_ref[o * images : (o + 1) * images, :].astype(jnp.float32)
    share = jnp.dot(
        jnp.transpose(share).astype(jnp.bfloat16),
        spread_over(rows, (images, many), 0),
        preferred_element_type=jnp.float32,
    )
    pairs = send_ref.shape[0]
    share = own_row(share, rows).reshape(pairs, 2, deep // (2 * pairs), many)
    first = core_ref[0] == 0
    ours = jnp.where(first, share[:, 0], share[:, 1]).reshape(deep // 2, many)
    theirs = jnp.where(first, share[:, 1], share[:, 0]).reshape(deep // 2, many)
    share_ref[...] = ours.astype(jnp.bfloat16)
    pack_both(send_ref, theirs.astype(jnp.bfloat16), filtered_ref, square_ref)


def packed(deep, filtered, square, pairs):
    slab = deep // (2 * pairs)
    lines = (filtered.shape[1] + square.shape[1]) // 128 * slab - slab // 2
    return jax.ShapeDtypeStruct((pairs, lines, 128), jnp.bfloat16)


def project(core, part, noise, picks, filtered, square, rows, ori, pairs):
    many = filtered.shape[0]
    deep = picks.shape[1]
    return pl.pallas_call(
        functools.partial(project_kernel, rows, ori),
        in_specs=[scalar()] + [whole()] * 5,
        out_specs=(whole(), whole(), whole()),
        out_shape=(
            jax.ShapeDtypeStruct((8, part.shape[1]), jnp.float32),
            jax.ShapeDtypeStruct((deep // 2, many), jnp.bfloat16),
            packed(deep, filtered, square, pairs),
        ),
        compiler_params=params(LARGE),
        cost_estimate=cost(1 << 28, 4 << 20),
        name="project",
    )(core, part, noise, picks, filtered, square)


def keep_kernel(share_ref, filtered_ref, square_ref, keep_ref):
    pack_both(keep_ref, share_ref[...], filtered_ref, square_ref)


def keep_own(share, filtered, square, pairs):
    return pl.pallas_call(
        keep_kernel,
        out_shape=packed(2 * share.shape[0], filtered, square, pairs),
        compiler_params=params(SMALL),
        cost_estimate=cost(1 << 28, 2 << 20),
        name="keep_own",
    )(share, filtered, square)


def middle_kernel(high_ref, keep_ref, got_ref, own_ref, *send_refs):
    pairs = keep_ref.shape[0]
    for ahead in range(pairs):
        at = (high_ref[0] + ahead) % pairs
        total = keep_ref[at].astype(jnp.float32) + got_ref[at].astype(jnp.float32)
        if ahead == 0:
            own_ref[...] = total
        else:
            send_refs[ahead - 1][...] = total.astype(jnp.bfloat16)


def middle(high, keep, got):
    pairs, slab, wide = keep.shape
    return pl.pallas_call(
        middle_kernel,
        in_specs=[scalar(), whole(), whole()],
        out_specs=(whole(),) * pairs,
        out_shape=(jax.ShapeDtypeStruct((slab, wide), jnp.float32),)
        + (jax.ShapeDtypeStruct((slab, wide), jnp.bfloat16),) * (pairs - 1),
        compiler_params=params(SMALL),
        cost_estimate=cost(1 << 20, 2 << 20),
        name="middle",
    )(high, keep, got)


def spread_lines(total, slab, npix, precision):
    half = npix // 2
    tiles = [total[at : at + slab] for at in range(0, total.shape[0] - slab // 2, slab)]
    data = jnp.concatenate(tiles[: 2 * npix // 128], 1)
    lower = jnp.concatenate(tiles[2 * npix // 128 :], 1)
    source = lax.broadcasted_iota(jnp.int32, (half, half), 0)
    target = lax.broadcasted_iota(jnp.int32, (half, half), 1)
    mirror = jnp.where(source + target == half, 1.0, 0.0).astype(total.dtype)
    upper = jnp.dot(lower, mirror, preferred_element_type=jnp.float32, precision=precision)
    last = total[total.shape[0] - slab // 2 :].astype(jnp.float32)
    last = jnp.concatenate([last[:, :1], last[:, 1:2]], 0)
    lane = lax.broadcasted_iota(jnp.int32, (slab, half), 1)
    upper = jnp.where(lane == 0, last, upper)
    return data.astype(jnp.float32), lower.astype(jnp.float32), upper


def finish_kernel(precision, first_ref, *refs):
    data_ref, weight_ref, data_out, weight_out = refs[-4:]
    slab, npix = weight_ref.shape
    total = first_ref[...]
    for part_ref in refs[:-4]:
        total = total + part_ref[...].astype(jnp.float32)
    data, lower, upper = spread_lines(total, slab, npix, precision)
    data_out[...] = data_ref[...] + data
    weight_out[:, : npix // 2] = weight_ref[:, : npix // 2] + lower
    weight_out[:, npix // 2 :] = weight_ref[:, npix // 2 :] + upper


def finish(first, parts, data_old, weight_old):
    exact = first.dtype == jnp.bfloat16
    return pl.pallas_call(
        functools.partial(finish_kernel, None if exact else lax.Precision.HIGHEST),
        out_shape=(
            jax.ShapeDtypeStruct(data_old.shape, jnp.float32),
            jax.ShapeDtypeStruct(weight_old.shape, jnp.float32),
        ),
        compiler_params=params(SMALL),
        cost_estimate=cost(1 << 20, 2 << 20),
        name="finish" if exact else "collect",
    )(first, *parts, data_old, weight_old)


def on_device(images, defocus, noise, orient, planes, weights, volume, data_old, weight_old):
    npix = images.shape[1]
    ori = orient.shape[1]
    n_img = lax.axis_size("img")
    n_vol = lax.axis_size("vol")
    rows = npix // n_img
    slab = volume.shape[0]
    deep = n_vol * slab * rows
    many = n_img * rows
    pairs = n_vol // 2
    slot = lax.axis_index("img").astype(jnp.int32).reshape(1)
    place = lax.axis_index("vol").astype(jnp.int32)

    fourier = transform(orient, defocus, noise, images[0], *dft_tables(npix))
    fourier = lax.all_to_all(
        fourier.reshape(n_img, rows, 2 * npix + META), "img", split_axis=0, concat_axis=0, tiled=True
    ).reshape(many, 2 * npix + META)
    vol_rows = lax.all_gather(volume.reshape(slab * rows, 2 * npix), "vol", axis=0, tiled=True)
    lookup = prepare(jnp.swapaxes(planes, 1, 2), jnp.swapaxes(weights, 1, 2), deep)
    filtered, picks, part, about = compare(slot, fourier, lookup, vol_rows, ori, rows, n_img)
    square, noise_all = squares(slot, about, ori, rows, npix)
    part = lax.all_to_all(
        part.reshape(n_img, 2, 2 * n_img), "img", split_axis=0, concat_axis=0, tiled=True
    ).reshape(2 * n_img, 2 * n_img)
    probs, share, send = project(
        (place % 2).reshape(1), part, noise_all, picks, filtered, square, rows, ori, pairs
    )
    mine = lax.dynamic_slice_in_dim(
        probs[:2].reshape(2 * 2, n_img), lax.axis_index("img"), 1, 1
    ).reshape(1, ori)
    got = lax.ppermute(send, "vol", [(v, v ^ 1) for v in range(n_vol)])
    keep = keep_own(share, filtered, square, pairs)
    own, *sends = middle((place // 2).reshape(1), keep, got)
    parts = [
        lax.ppermute(part, "vol", [(v, (v + 2 * ahead) % n_vol) for v in range(n_vol)])
        for ahead, part in enumerate(sends, 1)
    ]
    data, weight = finish(
        own,
        parts[:-1],
        data_old.reshape(slab * rows, 2 * npix),
        weight_old.reshape(slab * rows, npix),
    )
    data, weight = finish(parts[-1], [], data, weight)
    return (mine, data.reshape(data_old.shape), weight.reshape(weight_old.shape))


def solution(mesh):
    placed = (
        P(("img", "vol"), None, None),
        P(("img", "vol")),
        P(("img", "vol")),
        P(("img", "vol"), None),
        P(None, None, "img"),
        P(None, None, "img"),
        P("vol", "img", None),
        P("vol", "img", None),
        P("vol", "img", None),
    )
    return jax.shard_map(
        on_device,
        mesh=mesh,
        in_specs=placed,
        out_specs=(P(("img", "vol"), None), P("vol", "img", None), P("vol", "img", None)),
        check_vma=False,
    )
```

```python
import functools
import math

import jax
import jax.numpy as jnp
import ml_dtypes
import numpy as np
from jax import lax
from jax.experimental import pallas as pl
from jax.experimental.pallas import tpu as pltpu
from jax.sharding import PartitionSpec as P

AMP = 0.1
TILT = math.asin(AMP)
TURN = 2.0 * math.pi
TURN_HIGH = math.floor(TURN * 4096) / 4096
TURN_LOW = TURN - TURN_HIGH
SINE = tuple(
    factor / TURN ** (2 * power + 1)
    for power, factor in enumerate(
        (
            6.283185272722434,
            -41.341697068956265,
            81.60502462257806,
            -76.70155117622761,
            42.01616582127327,
            -14.868610992503873,
            3.199693654235983,
        )
    )
)
HUGE = 56 * 1024 * 1024
LARGE = 32 * 1024 * 1024
SMALL = 16 * 1024 * 1024
META = 128


def dft_tables(npix):
    index = np.arange(npix)
    angle = (index[:, None] * index[None, :] % npix) * (2.0 * math.pi / npix)
    scale = 1.0 / math.sqrt(npix)
    parts = [np.cos(angle) * scale, np.sin(angle) * scale]
    halves = [part[: npix // 2, parity::2] for parity in range(2) for part in parts]
    return tuple(
        jnp.asarray(np.concatenate(table, 1).astype(np.float32).astype(ml_dtypes.bfloat16))
        for table in (parts, halves)
    )


def frequency(index, npix):
    return ((index + npix // 2) % npix - npix // 2).astype(jnp.float32) / npix


def params(size):
    return pltpu.CompilerParams(vmem_limit_bytes=size)


def cost(flops, size):
    return pl.CostEstimate(flops=flops, bytes_accessed=size, transcendentals=0)


def whole():
    return pl.BlockSpec(memory_space=pltpu.VMEM)


def scalar():
    return pl.BlockSpec(memory_space=pltpu.SMEM)


def same(a, b):
    return lax.dot_general(a, b, (((1,), (1,)), ((), ())), preferred_element_type=jnp.float32)


def three_parts(value):
    parts = []
    for _ in range(3):
        part = value.astype(jnp.bfloat16).astype(jnp.float32)
        parts.append(part)
        value = value - part
    return parts


def bits(rows):
    assert rows & (rows - 1) == 0
    return rows.bit_length() - 1


def spread_over(rows, shape, image_axis):
    image = lax.broadcasted_iota(jnp.int32, shape, image_axis)
    owner = lax.broadcasted_iota(jnp.int32, shape, 1 - image_axis) >> bits(rows)
    return jnp.where(owner == image, 1.0, 0.0).astype(jnp.bfloat16)


def own_row(values, rows):
    height, width = values.shape
    sublane = lax.broadcasted_iota(jnp.int32, (rows, width), 0)
    lane = lax.broadcasted_iota(jnp.int32, (rows, width), 1) & (rows - 1)
    return jnp.where((sublane == lane)[None], values.reshape(height // rows, rows, width), 0.0)


def transform_kernel(chunk, orient_hbm, defocus_hbm, noise_hbm, image_hbm, table_hbm, halves_hbm, out_hbm, orient_ref, defocus_ref, noise_ref, image_ref, wide_ref, table_ref, halves_ref, both_ref, out_ref, in_sems, out_sems):
    npix = image_ref.shape[0]
    half = npix // 2
    ori = orient_ref.shape[1]
    starts = list(range(0, 2 * npix, chunk))
    pairs = [(image_hbm, image_ref)]
    pairs += [(table_hbm.at[:, pl.ds(start, chunk)], table_ref.at[:, pl.ds(start, chunk)]) for start in starts]
    pairs += [(halves_hbm, halves_ref), (orient_hbm, orient_ref), (defocus_hbm, defocus_ref), (noise_hbm, noise_ref)]
    loads = []
    for number, (source, target) in enumerate(pairs):
        load = pltpu.make_async_copy(source, target, in_sems.at[number])
        load.start()
        loads.append(load)
    loads[0].wait()
    tiles = range(npix // 128)
    for tile in tiles:
        wide_ref[tile] = image_ref[:, tile * 128 : (tile + 1) * 128].astype(jnp.float32)
    image = jnp.concatenate(
        [
            jnp.concatenate([wide_ref[tile, pl.ds(parity, half, 2), :] for tile in tiles], 1)
            for parity in range(2)
        ],
        0,
    ).astype(jnp.bfloat16)
    for number, start in enumerate(starts):
        loads[1 + number].wait()
        first = jnp.dot(
            image, table_ref[:, start : start + chunk], preferred_element_type=jnp.float32
        ).astype(jnp.bfloat16)
        for parity in range(2):
            part = first[parity * half : (parity + 1) * half]
            upper = slice(parity * npix, parity * npix + half)
            lower = slice(parity * npix + half, (parity + 1) * npix)
            if start < npix:
                both_ref[upper, start : start + chunk] = part
                both_ref[lower, npix + start : npix + start + chunk] = -part
            else:
                both_ref[upper, start : start + chunk] = -part
                both_ref[lower, start - npix : start - npix + chunk] = -part
    for load in loads[1 + len(starts) :]:
        load.wait()

    def save(at, number):
        return pltpu.make_async_copy(out_ref.at[:, at], out_hbm.at[:, at], out_sems.at[number])

    lane = lax.broadcasted_iota(jnp.int32, (8, META), 1)
    codes = jnp.zeros((8, META), jnp.int32)
    for o in range(ori):
        label = orient_ref[0, o]
        codes = jnp.where(lane == o, label & 255, codes)
        codes = jnp.where(lane == ori + o, label >> 8, codes)
    about = codes.astype(jnp.float32)
    place = 2 * ori
    for scalar_ref in (defocus_ref, noise_ref):
        for part in three_parts(jnp.full((8, META), scalar_ref[0], jnp.float32)):
            about = jnp.where(lane == place, part, about)
            place += 1
    out_ref[:, 2 * npix :] = jnp.broadcast_to(about[:1], (npix, META)).astype(jnp.bfloat16)
    chunk = chunk // 2
    steps = 2 * npix // chunk
    save(pl.ds(2 * npix, META), steps).start()

    @pl.loop(0, steps)
    def _(step):
        at = pl.ds(pl.multiple_of(step * chunk, chunk), chunk)
        even, odd = (
            jnp.dot(
                halves_ref[:, parity * npix : (parity + 1) * npix],
                both_ref[parity * npix : (parity + 1) * npix, at],
                preferred_element_type=jnp.float32,
            )
            for parity in range(2)
        )
        out_ref[:half, at] = (even + odd).astype(jnp.bfloat16)
        out_ref[half:, at] = (even - odd).astype(jnp.bfloat16)
        save(at, step).start()

    for step in range(steps):
        save(pl.ds(step * chunk, chunk), step).wait()
    save(pl.ds(2 * npix, META), steps).wait()


def transform(orient, defocus, noise, image, table, halves):
    npix = image.shape[0]
    chunk = npix
    pieces = 2 * npix // chunk
    return pl.pallas_call(
        functools.partial(transform_kernel, chunk),
        in_specs=[pl.BlockSpec(memory_space=pl.ANY)] * 6,
        out_specs=pl.BlockSpec(memory_space=pl.ANY),
        out_shape=jax.ShapeDtypeStruct((npix, 2 * npix + META), jnp.bfloat16),
        scratch_shapes=[
            pltpu.SMEM(orient.shape, jnp.int32),
            pltpu.SMEM(defocus.shape, jnp.float32),
            pltpu.SMEM(noise.shape, jnp.float32),
            pltpu.VMEM((npix, npix), jnp.bfloat16),
            pltpu.VMEM((npix // 128, npix, 128), jnp.float32),
            pltpu.VMEM((npix, 2 * npix), jnp.bfloat16),
            pltpu.VMEM((npix // 2, 2 * npix), jnp.bfloat16),
            pltpu.VMEM((2 * npix, 2 * npix), jnp.bfloat16),
            pltpu.VMEM((npix, 2 * npix + META), jnp.bfloat16),
            pltpu.SemaphoreType.DMA((pieces + 5,)),
            pltpu.SemaphoreType.DMA((2 * pieces + 1,)),
        ],
        compiler_params=params(HUGE),
        cost_estimate=cost(12 * npix**3, 10 * npix * npix),
        name="transform",
    )(orient, defocus, noise, image, table, halves)


def prepare_kernel(planes_ref, weights_ref, lookup_ref):
    deep, labels = lookup_ref.shape
    rows = planes_ref.shape[1]
    level = lax.broadcasted_iota(jnp.int32, (deep // rows, rows, labels), 0)
    total = jnp.zeros((deep // rows, rows, labels), jnp.float32)
    for k in range(2):
        weight = weights_ref[k].astype(jnp.float32)
        total = total + jnp.where(level == planes_ref[k][None], weight[None], 0.0)
    lookup_ref[...] = total.reshape(deep, labels).astype(jnp.bfloat16)


def prepare(planes, weights, deep):
    labels = planes.shape[2]
    return pl.pallas_call(
        prepare_kernel,
        in_specs=[whole(), whole()],
        out_specs=whole(),
        out_shape=jax.ShapeDtypeStruct((deep, labels), jnp.bfloat16),
        compiler_params=params(SMALL),
        cost_estimate=cost(1 << 22, 1 << 20),
        name="prepare",
    )(planes, weights)


def contrast(defocus, row_square, start, width, npix):
    column = start + lax.broadcasted_iota(jnp.int32, (1, width), 1)
    freq_x = frequency(column, npix)
    chi = defocus * (row_square + freq_x * freq_x)
    turns = jnp.floor(chi * (1.0 / TURN) + (TILT / TURN + 0.5))
    angle = ((chi - turns * TURN_HIGH) - turns * TURN_LOW) + TILT
    square = angle * angle
    series = -SINE[-1]
    for term in SINE[-2::-1]:
        series = series * square - term
    return series * angle


def line_geometry(meta, ori, rows, many, npix, slot):
    place = 2 * ori
    defocus = meta[:, place : place + 1] + meta[:, place + 1 : place + 2] + meta[:, place + 2 : place + 3]
    index = (lax.broadcasted_iota(jnp.int32, (many, 1), 0) & (rows - 1)) + slot * rows
    freq_y = jnp.where(index < npix // 2, index, index - npix).astype(jnp.float32) / npix
    return defocus, freq_y * freq_y


def compare_kernel(ori, rows, slot_ref, fourier_ref, lookup_ref, volume_ref, filtered_ref, picks_ref, part_ref, about_ref, mix_ref, power_ref):
    many, wide = filtered_ref.shape
    npix = wide // 2
    deep = volume_ref.shape[0]
    images = many // rows

    meta = fourier_ref[:, wide:]
    here = lax.broadcasted_iota(jnp.int32, (images, many), 0) << bits(rows)
    there = lax.broadcasted_iota(jnp.int32, (images, many), 1)
    pick = jnp.where(here == there, 1.0, 0.0).astype(jnp.bfloat16)
    about = jnp.dot(pick, meta, preferred_element_type=jnp.float32)
    about_ref[...] = about
    label = lax.broadcasted_iota(jnp.int32, (images, lookup_ref.shape[1]), 1).astype(jnp.float32)
    found = []
    for o in range(ori):
        mine = about[:, o : o + 1] + 256.0 * about[:, ori + o : ori + o + 1]
        found.append(jnp.where(label == mine, 1.0, 0.0).astype(jnp.bfloat16))
    found = same(jnp.concatenate(found, 0), lookup_ref[...]).astype(jnp.bfloat16)
    picks_ref[...] = found
    spread = spread_over(rows, (many, images), 1)
    for o in range(ori):
        every = jnp.dot(
            spread, found[o * images : (o + 1) * images], preferred_element_type=jnp.float32
        )
        mix_ref[o * many : (o + 1) * many, :] = (
            own_row(every, rows).reshape(many, deep).astype(jnp.bfloat16)
        )
    defocus, row_square = line_geometry(meta.astype(jnp.float32), ori, rows, many, npix, slot_ref[0])
    power_ref[...] = jnp.zeros(power_ref.shape, jnp.float32)

    @pl.loop(0, npix // 128)
    def _(number):
        start = pl.multiple_of(number * 128, 128)
        real = pl.ds(start, 128)
        imag = pl.ds(pl.multiple_of(npix + start, 128), 128)
        planes = jnp.concatenate([volume_ref[:, real], volume_ref[:, imag]], 1)
        ctf = contrast(defocus, row_square, start, 128, npix)
        for part in (real, imag):
            filtered_ref[:, part] = (ctf * fourier_ref[:, part].astype(jnp.float32)).astype(jnp.bfloat16)
        square = ctf * ctf
        for o in range(ori):
            section = jnp.dot(
                mix_ref[o * many : (o + 1) * many, :], planes, preferred_element_type=jnp.float32
            )
            section = section * section
            power_ref[o] += square * (section[:, :128] + section[:, 128:])

    found = own_row(same(filtered_ref[...], volume_ref[...]), rows)
    found = jnp.sum(found, axis=1)
    halves = []
    for o in range(ori):
        cross = found * picks_ref[o * images : (o + 1) * images, :].astype(jnp.float32)
        lanes = cross[:, :128]
        for start in range(128, deep, 128):
            lanes = lanes + cross[:, start : start + 128]
        power = jnp.sum(power_ref[o].reshape(images, rows, 128), axis=1)
        halves.append(lanes - 0.5 * power)
    upper = jnp.concatenate(halves[: ori // 2], 0)
    lower = jnp.concatenate(halves[ori // 2 :], 0)
    upper = jnp.sum(jnp.transpose(upper), axis=0, keepdims=True)
    lower = jnp.sum(jnp.transpose(lower), axis=0, keepdims=True)
    even = (lax.broadcasted_iota(jnp.int32, part_ref.shape, 0) & 1) == 0
    part_ref[...] = jnp.where(even, upper, lower)


def compare(slot, fourier, lookup, volume, ori, rows, copies):
    many = fourier.shape[0]
    deep, wide = volume.shape
    images = many // rows
    return pl.pallas_call(
        functools.partial(compare_kernel, ori, rows),
        in_specs=[scalar()] + [whole()] * 3,
        out_specs=(whole(),) * 4,
        out_shape=(
            jax.ShapeDtypeStruct((many, wide), jnp.bfloat16),
            jax.ShapeDtypeStruct((ori * images, deep), jnp.bfloat16),
            jax.ShapeDtypeStruct((copies * 2, 2 * images), jnp.float32),
            jax.ShapeDtypeStruct((images, META), jnp.float32),
        ),
        scratch_shapes=[
            pltpu.VMEM((ori * many, deep), jnp.bfloat16),
            pltpu.VMEM((ori, many, 128), jnp.float32),
        ],
        compiler_params=params(LARGE),
        cost_estimate=cost(1 << 31, 5 << 20),
        name="compare",
    )(slot, fourier, lookup, volume)


def squares_kernel(ori, rows, npix, slot_ref, about_ref, square_ref, noise_ref):
    many = square_ref.shape[0]
    images = many // rows
    about = about_ref[...]
    meta = jnp.dot(
        spread_over(rows, (many, images), 1),
        about.astype(jnp.bfloat16),
        preferred_element_type=jnp.float32,
    )
    defocus, row_square = line_geometry(meta, ori, rows, many, npix, slot_ref[0])
    for start in range(0, square_ref.shape[1], 128):
        ctf = contrast(defocus, row_square, start, 128, npix)
        square_ref[:, start : start + 128] = (ctf * ctf).astype(jnp.bfloat16)
    place = 2 * ori + 3
    turned = jnp.transpose(jnp.concatenate([about, about], 0))
    noise_ref[...] = turned[place : place + 1] + turned[place + 1 : place + 2] + turned[place + 2 : place + 3]


def squares(slot, about, ori, rows, npix):
    images = about.shape[0]
    return pl.pallas_call(
        functools.partial(squares_kernel, ori, rows, npix),
        in_specs=[scalar(), whole()],
        out_specs=(whole(), whole()),
        out_shape=(
            jax.ShapeDtypeStruct((images * rows, npix // 2 + 128), jnp.bfloat16),
            jax.ShapeDtypeStruct((1, 2 * images), jnp.float32),
        ),
        compiler_params=params(SMALL),
        cost_estimate=cost(1 << 27, 1 << 20),
        name="squares",
    )(slot, about)


def pack(target_ref, share, source_ref, start, last):
    pairs = target_ref.shape[0]
    slab = share.shape[0] // pairs
    sums = jnp.dot(share, source_ref[...], preferred_element_type=jnp.float32)
    for number in range(sums.shape[1] // 128):
        value = sums[:, number * 128 : (number + 1) * 128].reshape(pairs, slab, 128)
        at = (start + number) * slab
        if start + number < last:
            target_ref[:, at : at + slab, :] = value.astype(jnp.bfloat16)
        else:
            lane = lax.broadcasted_iota(jnp.int32, (pairs, slab // 2, 128), 2)
            lower = jnp.broadcast_to(value[:, slab // 2 :, :1], lane.shape)
            value = jnp.where(lane == 0, value[:, : slab // 2], lower)
            target_ref[:, at : at + slab // 2, :] = value.astype(jnp.bfloat16)


def pack_both(target_ref, share, filtered_ref, square_ref):
    tiles = filtered_ref.shape[1] // 128
    last = tiles + square_ref.shape[1] // 128 - 1
    pack(target_ref, share, filtered_ref, 0, last)
    pack(target_ref, share, square_ref, tiles, last)


def project_kernel(rows, ori, core_ref, part_ref, noise_ref, picks_ref, filtered_ref, square_ref, probs_ref, share_ref, send_ref):
    many = filtered_ref.shape[0]
    deep = picks_ref.shape[1]
    lanes = part_ref.shape[1]
    images = lanes // 2
    sums = jnp.sum(part_ref[...].reshape(part_ref.shape[0] // 8, 8, lanes), axis=0)
    sums = sums + pltpu.roll(sums, 4, 0)
    sums = sums + pltpu.roll(sums, 2, 0)
    score = sums / noise_ref[...]
    top = jnp.maximum(score, pltpu.roll(score, 1, 0))
    top = jnp.maximum(top, pltpu.roll(top, images, 1))
    power = jnp.exp(score - top)
    total = power + pltpu.roll(power, 1, 0)
    total = total + pltpu.roll(total, images, 1)
    probs = power / total
    probs_ref[...] = probs
    column = jnp.transpose(jnp.concatenate([probs] * (lanes // 8), 0))
    share = jnp.zeros((images, deep), jnp.float32)
    for o in range(ori):
        half = o % 2
        chance = column[half * images : (half + 1) * images, o // 2 : o // 2 + 1]
        share = share + chance * picks_ref[o * images : (o + 1) * images, :].astype(jnp.float32)
    share = jnp.dot(
        jnp.transpose(share).astype(jnp.bfloat16),
        spread_over(rows, (images, many), 0),
        preferred_element_type=jnp.float32,
    )
    pairs = send_ref.shape[0]
    share = own_row(share, rows).reshape(pairs, 2, deep // (2 * pairs), many)
    first = core_ref[0] == 0
    ours = jnp.where(first, share[:, 0], share[:, 1]).reshape(deep // 2, many)
    theirs = jnp.where(first, share[:, 1], share[:, 0]).reshape(deep // 2, many)
    share_ref[...] = ours.astype(jnp.bfloat16)
    pack_both(send_ref, theirs.astype(jnp.bfloat16), filtered_ref, square_ref)


def packed(deep, filtered, square, pairs):
    slab = deep // (2 * pairs)
    lines = (filtered.shape[1] + square.shape[1]) // 128 * slab - slab // 2
    return jax.ShapeDtypeStruct((pairs, lines, 128), jnp.bfloat16)


def project(core, part, noise, picks, filtered, square, rows, ori, pairs):
    many = filtered.shape[0]
    deep = picks.shape[1]
    return pl.pallas_call(
        functools.partial(project_kernel, rows, ori),
        in_specs=[scalar()] + [whole()] * 5,
        out_specs=(whole(), whole(), whole()),
        out_shape=(
            jax.ShapeDtypeStruct((8, part.shape[1]), jnp.float32),
            jax.ShapeDtypeStruct((deep // 2, many), jnp.bfloat16),
            packed(deep, filtered, square, pairs),
        ),
        compiler_params=params(LARGE),
        cost_estimate=cost(1 << 28, 4 << 20),
        name="project",
    )(core, part, noise, picks, filtered, square)


def keep_kernel(share_ref, filtered_ref, square_ref, keep_ref):
    pack_both(keep_ref, share_ref[...], filtered_ref, square_ref)


def keep_own(share, filtered, square, pairs):
    return pl.pallas_call(
        keep_kernel,
        out_shape=packed(2 * share.shape[0], filtered, square, pairs),
        compiler_params=params(SMALL),
        cost_estimate=cost(1 << 28, 2 << 20),
        name="keep_own",
    )(share, filtered, square)


def middle_kernel(high_ref, keep_ref, got_ref, own_ref, *send_refs):
    pairs = keep_ref.shape[0]
    for ahead in range(pairs):
        at = (high_ref[0] + ahead) % pairs
        total = keep_ref[at].astype(jnp.float32) + got_ref[at].astype(jnp.float32)
        if ahead == 0:
            own_ref[...] = total
        else:
            send_refs[ahead - 1][...] = total.astype(jnp.bfloat16)


def middle(high, keep, got):
    pairs, slab, wide = keep.shape
    return pl.pallas_call(
        middle_kernel,
        in_specs=[scalar(), whole(), whole()],
        out_specs=(whole(),) * pairs,
        out_shape=(jax.ShapeDtypeStruct((slab, wide), jnp.float32),)
        + (jax.ShapeDtypeStruct((slab, wide), jnp.bfloat16),) * (pairs - 1),
        compiler_params=params(SMALL),
        cost_estimate=cost(1 << 20, 2 << 20),
        name="middle",
    )(high, keep, got)


def spread_lines(total, slab, npix):
    half = npix // 2
    tiles = [total[at : at + slab] for at in range(0, total.shape[0] - slab // 2, slab)]
    data = jnp.concatenate(tiles[: 2 * npix // 128], 1)
    lower = jnp.concatenate(tiles[2 * npix // 128 :], 1)
    source = lax.broadcasted_iota(jnp.int32, (half, half), 0)
    target = lax.broadcasted_iota(jnp.int32, (half, half), 1)
    mirror = jnp.where(source + target == half, 1.0, 0.0)
    upper = jnp.dot(lower, mirror, preferred_element_type=jnp.float32, precision=lax.Precision.HIGHEST)
    last = total[total.shape[0] - slab // 2 :]
    last = jnp.concatenate([last[:, :1], last[:, 1:2]], 0)
    lane = lax.broadcasted_iota(jnp.int32, (slab, half), 1)
    upper = jnp.where(lane == 0, last, upper)
    return data, lower, upper


def finish_kernel(own_ref, *refs):
    data_ref, weight_ref, data_out, weight_out = refs[-4:]
    slab, npix = weight_ref.shape
    total = own_ref[...]
    for part_ref in refs[:-4]:
        total = total + part_ref[...].astype(jnp.float32)
    data, lower, upper = spread_lines(total, slab, npix)
    data_out[...] = data_ref[...] + data
    weight_out[:, : npix // 2] = weight_ref[:, : npix // 2] + lower
    weight_out[:, npix // 2 :] = weight_ref[:, npix // 2 :] + upper


def finish(own, parts, data_old, weight_old):
    return pl.pallas_call(
        finish_kernel,
        out_shape=(
            jax.ShapeDtypeStruct(data_old.shape, jnp.float32),
            jax.ShapeDtypeStruct(weight_old.shape, jnp.float32),
        ),
        compiler_params=params(SMALL),
        cost_estimate=cost(1 << 20, 2 << 20),
        name="finish",
    )(own, *parts, data_old, weight_old)


def on_device(images, defocus, noise, orient, planes, weights, volume, data_old, weight_old):
    npix = images.shape[1]
    ori = orient.shape[1]
    n_img = lax.axis_size("img")
    n_vol = lax.axis_size("vol")
    rows = npix // n_img
    slab = volume.shape[0]
    deep = n_vol * slab * rows
    many = n_img * rows
    pairs = n_vol // 2
    slot = lax.axis_index("img").astype(jnp.int32).reshape(1)
    place = lax.axis_index("vol").astype(jnp.int32)

    fourier = transform(orient, defocus, noise, images[0], *dft_tables(npix))
    fourier = lax.all_to_all(
        fourier.reshape(n_img, rows, 2 * npix + META), "img", split_axis=0, concat_axis=0, tiled=True
    ).reshape(many, 2 * npix + META)
    vol_rows = lax.all_gather(volume.reshape(slab * rows, 2 * npix), "vol", axis=0, tiled=True)
    lookup = prepare(jnp.swapaxes(planes, 1, 2), jnp.swapaxes(weights, 1, 2), deep)
    filtered, picks, part, about = compare(slot, fourier, lookup, vol_rows, ori, rows, n_img)
    square, noise_all = squares(slot, about, ori, rows, npix)
    part = lax.all_to_all(
        part.reshape(n_img, 2, 2 * n_img), "img", split_axis=0, concat_axis=0, tiled=True
    ).reshape(2 * n_img, 2 * n_img)
    probs, share, send = project(
        (place % 2).reshape(1), part, noise_all, picks, filtered, square, rows, ori, pairs
    )
    mine = lax.dynamic_slice_in_dim(
        probs[:2].reshape(2 * 2, n_img), lax.axis_index("img"), 1, 1
    ).reshape(1, ori)
    got = lax.ppermute(send, "vol", [(v, v ^ 1) for v in range(n_vol)])
    keep = keep_own(share, filtered, square, pairs)
    own, *sends = middle((place // 2).reshape(1), keep, got)
    parts = [
        lax.ppermute(part, "vol", [(v, (v + 2 * ahead) % n_vol) for v in range(n_vol)])
        for ahead, part in ((2, sends[1]), (1, sends[0]), (3, sends[2]))
    ]
    data, weight = finish(
        own,
        parts,
        data_old.reshape(slab * rows, 2 * npix),
        weight_old.reshape(slab * rows, npix),
    )
    return (mine, data.reshape(data_old.shape), weight.reshape(weight_old.shape))


def solution(mesh):
    placed = (
        P(("img", "vol"), None, None),
        P(("img", "vol")),
        P(("img", "vol")),
        P(("img", "vol"), None),
        P(None, None, "img"),
        P(None, None, "img"),
        P("vol", "img", None),
        P("vol", "img", None),
        P("vol", "img", None),
    )
    return jax.shard_map(
        on_device,
        mesh=mesh,
        in_specs=placed,
        out_specs=(P(("img", "vol"), None), P("vol", "img", None), P("vol", "img", None)),
        check_vma=False,
    )
```

```python
import functools
import math

import jax
import jax.numpy as jnp
import ml_dtypes
import numpy as np
from jax import lax
from jax.experimental import pallas as pl
from jax.experimental.pallas import tpu as pltpu
from jax.sharding import PartitionSpec as P

AMP = 0.1
TILT = math.asin(AMP)
TURN = 2.0 * math.pi
TURN_HIGH = math.floor(TURN * 4096) / 4096
TURN_LOW = TURN - TURN_HIGH
SINE = tuple(
    factor / TURN ** (2 * power + 1)
    for power, factor in enumerate(
        (
            6.283185272722434,
            -41.341697068956265,
            81.60502462257806,
            -76.70155117622761,
            42.01616582127327,
            -14.868610992503873,
            3.199693654235983,
        )
    )
)
HUGE = 56 * 1024 * 1024
LARGE = 32 * 1024 * 1024
SMALL = 16 * 1024 * 1024
META = 128


def dft_tables(npix):
    index = np.arange(npix)
    angle = (index[:, None] * index[None, :] % npix) * (2.0 * math.pi / npix)
    scale = 1.0 / math.sqrt(npix)
    parts = [np.cos(angle) * scale, np.sin(angle) * scale]
    halves = [part[: npix // 2, parity::2] for parity in range(2) for part in parts]
    return tuple(
        jnp.asarray(np.concatenate(table, 1).astype(np.float32).astype(ml_dtypes.bfloat16))
        for table in (parts, halves)
    )


def frequency(index, npix):
    return ((index + npix // 2) % npix - npix // 2).astype(jnp.float32) / npix


def params(size):
    return pltpu.CompilerParams(vmem_limit_bytes=size)


def cost(flops, size):
    return pl.CostEstimate(flops=flops, bytes_accessed=size, transcendentals=0)


def whole():
    return pl.BlockSpec(memory_space=pltpu.VMEM)


def scalar():
    return pl.BlockSpec(memory_space=pltpu.SMEM)


def same(a, b):
    return lax.dot_general(a, b, (((1,), (1,)), ((), ())), preferred_element_type=jnp.float32)


def three_parts(value):
    parts = []
    for _ in range(3):
        part = value.astype(jnp.bfloat16).astype(jnp.float32)
        parts.append(part)
        value = value - part
    return parts


def bits(rows):
    assert rows & (rows - 1) == 0
    return rows.bit_length() - 1


def spread_over(rows, shape, image_axis):
    image = lax.broadcasted_iota(jnp.int32, shape, image_axis)
    owner = lax.broadcasted_iota(jnp.int32, shape, 1 - image_axis) >> bits(rows)
    return jnp.where(owner == image, 1.0, 0.0).astype(jnp.bfloat16)


def own_row(values, rows):
    height, width = values.shape
    sublane = lax.broadcasted_iota(jnp.int32, (rows, width), 0)
    lane = lax.broadcasted_iota(jnp.int32, (rows, width), 1) & (rows - 1)
    return jnp.where((sublane == lane)[None], values.reshape(height // rows, rows, width), 0.0)


def transform_kernel(chunk, orient_hbm, defocus_hbm, noise_hbm, image_hbm, table_hbm, halves_hbm, out_hbm, orient_ref, defocus_ref, noise_ref, image_ref, wide_ref, table_ref, halves_ref, both_ref, out_ref, in_sems, out_sems):
    npix = image_ref.shape[0]
    half = npix // 2
    ori = orient_ref.shape[1]
    starts = list(range(0, 2 * npix, chunk))
    pairs = [(image_hbm, image_ref)]
    pairs += [(table_hbm.at[:, pl.ds(start, chunk)], table_ref.at[:, pl.ds(start, chunk)]) for start in starts]
    pairs += [(halves_hbm, halves_ref), (orient_hbm, orient_ref), (defocus_hbm, defocus_ref), (noise_hbm, noise_ref)]
    loads = []
    for number, (source, target) in enumerate(pairs):
        load = pltpu.make_async_copy(source, target, in_sems.at[number])
        load.start()
        loads.append(load)
    loads[0].wait()
    tiles = range(npix // 128)
    for tile in tiles:
        wide_ref[tile] = image_ref[:, tile * 128 : (tile + 1) * 128].astype(jnp.float32)
    image = jnp.concatenate(
        [
            jnp.concatenate([wide_ref[tile, pl.ds(parity, half, 2), :] for tile in tiles], 1)
            for parity in range(2)
        ],
        0,
    ).astype(jnp.bfloat16)
    for number, start in enumerate(starts):
        loads[1 + number].wait()
        first = jnp.dot(
            image, table_ref[:, start : start + chunk], preferred_element_type=jnp.float32
        ).astype(jnp.bfloat16)
        for parity in range(2):
            part = first[parity * half : (parity + 1) * half]
            upper = slice(parity * npix, parity * npix + half)
            lower = slice(parity * npix + half, (parity + 1) * npix)
            if start < npix:
                both_ref[upper, start : start + chunk] = part
                both_ref[lower, npix + start : npix + start + chunk] = -part
            else:
                both_ref[upper, start : start + chunk] = -part
                both_ref[lower, start - npix : start - npix + chunk] = -part
    for load in loads[1 + len(starts) :]:
        load.wait()
    lane = lax.broadcasted_iota(jnp.int32, (8, META), 1)
    codes = jnp.zeros((8, META), jnp.int32)
    for o in range(ori):
        label = orient_ref[0, o]
        codes = jnp.where(lane == o, label & 255, codes)
        codes = jnp.where(lane == ori + o, label >> 8, codes)
    about = codes.astype(jnp.float32)
    place = 2 * ori
    for scalar_ref in (defocus_ref, noise_ref):
        for part in three_parts(jnp.full((8, META), scalar_ref[0], jnp.float32)):
            about = jnp.where(lane == place, part, about)
            place += 1
    out_ref[:, 2 * npix :] = jnp.broadcast_to(about[:1], (npix, META)).astype(jnp.bfloat16)
    even, odd = (
        jnp.dot(
            halves_ref[:, parity * npix : (parity + 1) * npix],
            both_ref[parity * npix : (parity + 1) * npix, :],
            preferred_element_type=jnp.float32,
        )
        for parity in range(2)
    )
    saves = []
    for part, value in enumerate((even + odd, even - odd)):
        at = slice(part * half, (part + 1) * half)
        out_ref[at, : 2 * npix] = value.astype(jnp.bfloat16)
        copy = pltpu.make_async_copy(
            out_ref.at[pl.ds(part * half, half)], out_hbm.at[pl.ds(part * half, half)], out_sems.at[part]
        )
        copy.start()
        saves.append(copy)
    for copy in saves:
        copy.wait()


def transform(orient, defocus, noise, image, table, halves):
    npix = image.shape[0]
    chunk = npix
    pieces = 2 * npix // chunk
    return pl.pallas_call(
        functools.partial(transform_kernel, chunk),
        in_specs=[pl.BlockSpec(memory_space=pl.ANY)] * 6,
        out_specs=pl.BlockSpec(memory_space=pl.ANY),
        out_shape=jax.ShapeDtypeStruct((npix, 2 * npix + META), jnp.bfloat16),
        scratch_shapes=[
            pltpu.SMEM(orient.shape, jnp.int32),
            pltpu.SMEM(defocus.shape, jnp.float32),
            pltpu.SMEM(noise.shape, jnp.float32),
            pltpu.VMEM((npix, npix), jnp.bfloat16),
            pltpu.VMEM((npix // 128, npix, 128), jnp.float32),
            pltpu.VMEM((npix, 2 * npix), jnp.bfloat16),
            pltpu.VMEM((npix // 2, 2 * npix), jnp.bfloat16),
            pltpu.VMEM((2 * npix, 2 * npix), jnp.bfloat16),
            pltpu.VMEM((npix, 2 * npix + META), jnp.bfloat16),
            pltpu.SemaphoreType.DMA((pieces + 5,)),
            pltpu.SemaphoreType.DMA((2,)),
        ],
        compiler_params=params(HUGE),
        cost_estimate=cost(12 * npix**3, 10 * npix * npix),
        name="transform",
    )(orient, defocus, noise, image, table, halves)


def prepare_kernel(planes_ref, weights_ref, lookup_ref):
    deep, labels = lookup_ref.shape
    rows = planes_ref.shape[1]
    level = lax.broadcasted_iota(jnp.int32, (deep // rows, rows, labels), 0)
    total = jnp.zeros((deep // rows, rows, labels), jnp.float32)
    for k in range(2):
        weight = weights_ref[k].astype(jnp.float32)
        total = total + jnp.where(level == planes_ref[k][None], weight[None], 0.0)
    lookup_ref[...] = total.reshape(deep, labels).astype(jnp.bfloat16)


def prepare(planes, weights, deep):
    labels = planes.shape[2]
    return pl.pallas_call(
        prepare_kernel,
        in_specs=[whole(), whole()],
        out_specs=whole(),
        out_shape=jax.ShapeDtypeStruct((deep, labels), jnp.bfloat16),
        compiler_params=params(SMALL),
        cost_estimate=cost(1 << 22, 1 << 20),
        name="prepare",
    )(planes, weights)


def contrast(defocus, row_square, start, width, npix):
    column = start + lax.broadcasted_iota(jnp.int32, (1, width), 1)
    freq_x = frequency(column, npix)
    chi = defocus * (row_square + freq_x * freq_x)
    turns = jnp.floor(chi * (1.0 / TURN) + (TILT / TURN + 0.5))
    angle = ((chi - turns * TURN_HIGH) - turns * TURN_LOW) + TILT
    square = angle * angle
    series = -SINE[-1]
    for term in SINE[-2::-1]:
        series = series * square - term
    return series * angle


def line_geometry(meta, ori, rows, many, npix, slot):
    place = 2 * ori
    defocus = meta[:, place : place + 1] + meta[:, place + 1 : place + 2] + meta[:, place + 2 : place + 3]
    index = (lax.broadcasted_iota(jnp.int32, (many, 1), 0) & (rows - 1)) + slot * rows
    freq_y = jnp.where(index < npix // 2, index, index - npix).astype(jnp.float32) / npix
    return defocus, freq_y * freq_y


def compare_kernel(ori, rows, slot_ref, fourier_ref, lookup_ref, volume_ref, filtered_ref, picks_ref, part_ref, about_ref, mix_ref, square_ref):
    many, wide = filtered_ref.shape
    npix = wide // 2
    deep = volume_ref.shape[0]
    images = many // rows

    meta = fourier_ref[:, wide:]
    here = lax.broadcasted_iota(jnp.int32, (images, many), 0) << bits(rows)
    there = lax.broadcasted_iota(jnp.int32, (images, many), 1)
    pick = jnp.where(here == there, 1.0, 0.0).astype(jnp.bfloat16)
    about = jnp.dot(pick, meta, preferred_element_type=jnp.float32)
    about_ref[...] = about
    label = lax.broadcasted_iota(jnp.int32, (images, lookup_ref.shape[1]), 1).astype(jnp.float32)
    found = []
    for o in range(ori):
        mine = about[:, o : o + 1] + 256.0 * about[:, ori + o : ori + o + 1]
        found.append(jnp.where(label == mine, 1.0, 0.0).astype(jnp.bfloat16))
    found = same(jnp.concatenate(found, 0), lookup_ref[...]).astype(jnp.bfloat16)
    picks_ref[...] = found
    spread = spread_over(rows, (many, images), 1)
    for o in range(ori):
        every = jnp.dot(
            spread, found[o * images : (o + 1) * images], preferred_element_type=jnp.float32
        )
        mix_ref[o * many : (o + 1) * many, :] = (
            own_row(every, rows).reshape(many, deep).astype(jnp.bfloat16)
        )
    defocus, row_square = line_geometry(meta.astype(jnp.float32), ori, rows, many, npix, slot_ref[0])
    for start in range(0, npix, 128):
        ctf = contrast(defocus, row_square, start, 128, npix)
        for at in (start, npix + start):
            filtered_ref[:, at : at + 128] = (
                ctf * fourier_ref[:, at : at + 128].astype(jnp.float32)
            ).astype(jnp.bfloat16)
        square_ref[:, start : start + 128] = ctf * ctf
    powers = []
    for o in range(ori):
        section = jnp.dot(
            mix_ref[o * many : (o + 1) * many, :], volume_ref[...], preferred_element_type=jnp.float32
        )
        section = section * section
        power = jnp.zeros((many, 128), jnp.float32)
        for start in range(0, npix, 128):
            both = section[:, start : start + 128] + section[:, npix + start : npix + start + 128]
            power = power + square_ref[:, start : start + 128] * both
        powers.append(jnp.sum(power.reshape(images, rows, 128), axis=1))

    found = own_row(same(filtered_ref[...], volume_ref[...]), rows)
    found = jnp.sum(found, axis=1)
    halves = []
    for o in range(ori):
        cross = found * picks_ref[o * images : (o + 1) * images, :].astype(jnp.float32)
        lanes = cross[:, :128]
        for start in range(128, deep, 128):
            lanes = lanes + cross[:, start : start + 128]
        halves.append(lanes - 0.5 * powers[o])
    upper = jnp.concatenate(halves[: ori // 2], 0)
    lower = jnp.concatenate(halves[ori // 2 :], 0)
    upper = jnp.sum(jnp.transpose(upper), axis=0, keepdims=True)
    lower = jnp.sum(jnp.transpose(lower), axis=0, keepdims=True)
    even = (lax.broadcasted_iota(jnp.int32, part_ref.shape, 0) & 1) == 0
    part_ref[...] = jnp.where(even, upper, lower)


def compare(slot, fourier, lookup, volume, ori, rows, copies):
    many = fourier.shape[0]
    deep, wide = volume.shape
    images = many // rows
    return pl.pallas_call(
        functools.partial(compare_kernel, ori, rows),
        in_specs=[scalar()] + [whole()] * 3,
        out_specs=(whole(),) * 4,
        out_shape=(
            jax.ShapeDtypeStruct((many, wide), jnp.bfloat16),
            jax.ShapeDtypeStruct((ori * images, deep), jnp.bfloat16),
            jax.ShapeDtypeStruct((copies * 2, 2 * images), jnp.float32),
            jax.ShapeDtypeStruct((images, META), jnp.float32),
        ),
        scratch_shapes=[
            pltpu.VMEM((ori * many, deep), jnp.bfloat16),
            pltpu.VMEM((many, wide // 2), jnp.float32),
        ],
        compiler_params=params(LARGE),
        cost_estimate=cost(1 << 31, 5 << 20),
        name="compare",
    )(slot, fourier, lookup, volume)


def squares_kernel(ori, rows, npix, slot_ref, about_ref, square_ref, noise_ref):
    many = square_ref.shape[0]
    images = many // rows
    about = about_ref[...]
    meta = jnp.dot(
        spread_over(rows, (many, images), 1),
        about.astype(jnp.bfloat16),
        preferred_element_type=jnp.float32,
    )
    defocus, row_square = line_geometry(meta, ori, rows, many, npix, slot_ref[0])
    for start in range(0, square_ref.shape[1], 128):
        ctf = contrast(defocus, row_square, start, 128, npix)
        square_ref[:, start : start + 128] = (ctf * ctf).astype(jnp.bfloat16)
    place = 2 * ori + 3
    turned = jnp.transpose(jnp.concatenate([about, about], 0))
    noise_ref[...] = turned[place : place + 1] + turned[place + 1 : place + 2] + turned[place + 2 : place + 3]


def squares(slot, about, ori, rows, npix):
    images = about.shape[0]
    return pl.pallas_call(
        functools.partial(squares_kernel, ori, rows, npix),
        in_specs=[scalar(), whole()],
        out_specs=(whole(), whole()),
        out_shape=(
            jax.ShapeDtypeStruct((images * rows, npix // 2 + 128), jnp.bfloat16),
            jax.ShapeDtypeStruct((1, 2 * images), jnp.float32),
        ),
        compiler_params=params(SMALL),
        cost_estimate=cost(1 << 27, 1 << 20),
        name="squares",
    )(slot, about)


def pack(target_ref, share, source_ref, start, last):
    pairs = target_ref.shape[0]
    slab = share.shape[0] // pairs
    sums = jnp.dot(share, source_ref[...], preferred_element_type=jnp.float32)
    for number in range(sums.shape[1] // 128):
        value = sums[:, number * 128 : (number + 1) * 128].reshape(pairs, slab, 128)
        at = (start + number) * slab
        if start + number < last:
            target_ref[:, at : at + slab, :] = value.astype(jnp.bfloat16)
        else:
            lane = lax.broadcasted_iota(jnp.int32, (pairs, slab // 2, 128), 2)
            lower = jnp.broadcast_to(value[:, slab // 2 :, :1], lane.shape)
            value = jnp.where(lane == 0, value[:, : slab // 2], lower)
            target_ref[:, at : at + slab // 2, :] = value.astype(jnp.bfloat16)


def pack_both(target_ref, share, filtered_ref, square_ref):
    tiles = filtered_ref.shape[1] // 128
    last = tiles + square_ref.shape[1] // 128 - 1
    pack(target_ref, share, filtered_ref, 0, last)
    pack(target_ref, share, square_ref, tiles, last)


def project_kernel(rows, ori, core_ref, part_ref, noise_ref, picks_ref, filtered_ref, square_ref, probs_ref, share_ref, send_ref):
    many = filtered_ref.shape[0]
    deep = picks_ref.shape[1]
    lanes = part_ref.shape[1]
    images = lanes // 2
    sums = jnp.sum(part_ref[...].reshape(part_ref.shape[0] // 8, 8, lanes), axis=0)
    sums = sums + pltpu.roll(sums, 4, 0)
    sums = sums + pltpu.roll(sums, 2, 0)
    score = sums / noise_ref[...]
    top = jnp.maximum(score, pltpu.roll(score, 1, 0))
    top = jnp.maximum(top, pltpu.roll(top, images, 1))
    power = jnp.exp(score - top)
    total = power + pltpu.roll(power, 1, 0)
    total = total + pltpu.roll(total, images, 1)
    probs = power / total
    probs_ref[...] = probs
    column = jnp.transpose(jnp.concatenate([probs] * (lanes // 8), 0))
    share = jnp.zeros((images, deep), jnp.float32)
    for o in range(ori):
        half = o % 2
        chance = column[half * images : (half + 1) * images, o // 2 : o // 2 + 1]
        share = share + chance * picks_ref[o * images : (o + 1) * images, :].astype(jnp.float32)
    share = jnp.dot(
        jnp.transpose(share).astype(jnp.bfloat16),
        spread_over(rows, (images, many), 0),
        preferred_element_type=jnp.float32,
    )
    pairs = send_ref.shape[0]
    share = own_row(share, rows).reshape(pairs, 2, deep // (2 * pairs), many)
    first = core_ref[0] == 0
    ours = jnp.where(first, share[:, 0], share[:, 1]).reshape(deep // 2, many)
    theirs = jnp.where(first, share[:, 1], share[:, 0]).reshape(deep // 2, many)
    share_ref[...] = ours.astype(jnp.bfloat16)
    pack_both(send_ref, theirs.astype(jnp.bfloat16), filtered_ref, square_ref)


def packed(deep, filtered, square, pairs):
    slab = deep // (2 * pairs)
    lines = (filtered.shape[1] + square.shape[1]) // 128 * slab - slab // 2
    return jax.ShapeDtypeStruct((pairs, lines, 128), jnp.bfloat16)


def project(core, part, noise, picks, filtered, square, rows, ori, pairs):
    many = filtered.shape[0]
    deep = picks.shape[1]
    return pl.pallas_call(
        functools.partial(project_kernel, rows, ori),
        in_specs=[scalar()] + [whole()] * 5,
        out_specs=(whole(), whole(), whole()),
        out_shape=(
            jax.ShapeDtypeStruct((8, part.shape[1]), jnp.float32),
            jax.ShapeDtypeStruct((deep // 2, many), jnp.bfloat16),
            packed(deep, filtered, square, pairs),
        ),
        compiler_params=params(LARGE),
        cost_estimate=cost(1 << 28, 4 << 20),
        name="project",
    )(core, part, noise, picks, filtered, square)


def keep_kernel(share_ref, filtered_ref, square_ref, keep_ref):
    pack_both(keep_ref, share_ref[...], filtered_ref, square_ref)


def keep_own(share, filtered, square, pairs):
    return pl.pallas_call(
        keep_kernel,
        out_shape=packed(2 * share.shape[0], filtered, square, pairs),
        compiler_params=params(SMALL),
        cost_estimate=cost(1 << 28, 2 << 20),
        name="keep_own",
    )(share, filtered, square)


def middle_kernel(high_ref, keep_ref, got_ref, own_ref, *send_refs):
    pairs = keep_ref.shape[0]
    for ahead in range(pairs):
        at = (high_ref[0] + ahead) % pairs
        total = keep_ref[at].astype(jnp.float32) + got_ref[at].astype(jnp.float32)
        if ahead == 0:
            own_ref[...] = total
        else:
            send_refs[ahead - 1][...] = total.astype(jnp.bfloat16)


def middle(high, keep, got):
    pairs, slab, wide = keep.shape
    return pl.pallas_call(
        middle_kernel,
        in_specs=[scalar(), whole(), whole()],
        out_specs=(whole(),) * pairs,
        out_shape=(jax.ShapeDtypeStruct((slab, wide), jnp.float32),)
        + (jax.ShapeDtypeStruct((slab, wide), jnp.bfloat16),) * (pairs - 1),
        compiler_params=params(SMALL),
        cost_estimate=cost(1 << 20, 2 << 20),
        name="middle",
    )(high, keep, got)


def spread_lines(total, slab, npix):
    half = npix // 2
    tiles = [total[at : at + slab] for at in range(0, total.shape[0] - slab // 2, slab)]
    data = jnp.concatenate(tiles[: 2 * npix // 128], 1)
    lower = jnp.concatenate(tiles[2 * npix // 128 :], 1)
    source = lax.broadcasted_iota(jnp.int32, (half, half), 0)
    target = lax.broadcasted_iota(jnp.int32, (half, half), 1)
    mirror = jnp.where(source + target == half, 1.0, 0.0)
    upper = jnp.dot(lower, mirror, preferred_element_type=jnp.float32, precision=lax.Precision.HIGHEST)
    last = total[total.shape[0] - slab // 2 :]
    last = jnp.concatenate([last[:, :1], last[:, 1:2]], 0)
    lane = lax.broadcasted_iota(jnp.int32, (slab, half), 1)
    upper = jnp.where(lane == 0, last, upper)
    return data, lower, upper


def finish_kernel(own_ref, *refs):
    data_ref, weight_ref, data_out, weight_out = refs[-4:]
    slab, npix = weight_ref.shape
    total = own_ref[...]
    for part_ref in refs[:-4]:
        total = total + part_ref[...].astype(jnp.float32)
    data, lower, upper = spread_lines(total, slab, npix)
    data_out[...] = data_ref[...] + data
    weight_out[:, : npix // 2] = weight_ref[:, : npix // 2] + lower
    weight_out[:, npix // 2 :] = weight_ref[:, npix // 2 :] + upper


def finish(own, parts, data_old, weight_old):
    return pl.pallas_call(
        finish_kernel,
        out_shape=(
            jax.ShapeDtypeStruct(data_old.shape, jnp.float32),
            jax.ShapeDtypeStruct(weight_old.shape, jnp.float32),
        ),
        compiler_params=params(SMALL),
        cost_estimate=cost(1 << 20, 2 << 20),
        name="finish",
    )(own, *parts, data_old, weight_old)


def on_device(images, defocus, noise, orient, planes, weights, volume, data_old, weight_old):
    npix = images.shape[1]
    ori = orient.shape[1]
    n_img = lax.axis_size("img")
    n_vol = lax.axis_size("vol")
    rows = npix // n_img
    slab = volume.shape[0]
    deep = n_vol * slab * rows
    many = n_img * rows
    pairs = n_vol // 2
    slot = lax.axis_index("img").astype(jnp.int32).reshape(1)
    place = lax.axis_index("vol").astype(jnp.int32)

    fourier = transform(orient, defocus, noise, images[0], *dft_tables(npix))
    fourier = lax.all_to_all(
        fourier.reshape(n_img, rows, 2 * npix + META), "img", split_axis=0, concat_axis=0, tiled=True
    ).reshape(many, 2 * npix + META)
    vol_rows = lax.all_gather(volume.reshape(slab * rows, 2 * npix), "vol", axis=0, tiled=True)
    lookup = prepare(jnp.swapaxes(planes, 1, 2), jnp.swapaxes(weights, 1, 2), deep)
    filtered, picks, part, about = compare(slot, fourier, lookup, vol_rows, ori, rows, n_img)
    square, noise_all = squares(slot, about, ori, rows, npix)
    part = lax.all_to_all(
        part.reshape(n_img, 2, 2 * n_img), "img", split_axis=0, concat_axis=0, tiled=True
    ).reshape(2 * n_img, 2 * n_img)
    probs, share, send = project(
        (place % 2).reshape(1), part, noise_all, picks, filtered, square, rows, ori, pairs
    )
    mine = lax.dynamic_slice_in_dim(
        probs[:2].reshape(2 * 2, n_img), lax.axis_index("img"), 1, 1
    ).reshape(1, ori)
    got = lax.ppermute(send, "vol", [(v, v ^ 1) for v in range(n_vol)])
    keep = keep_own(share, filtered, square, pairs)
    own, *sends = middle((place // 2).reshape(1), keep, got)
    parts = [
        lax.ppermute(part, "vol", [(v, (v + 2 * ahead) % n_vol) for v in range(n_vol)])
        for ahead, part in ((2, sends[1]), (1, sends[0]), (3, sends[2]))
    ]
    data, weight = finish(
        own,
        parts,
        data_old.reshape(slab * rows, 2 * npix),
        weight_old.reshape(slab * rows, npix),
    )
    return (mine, data.reshape(data_old.shape), weight.reshape(weight_old.shape))


def solution(mesh):
    placed = (
        P(("img", "vol"), None, None),
        P(("img", "vol")),
        P(("img", "vol")),
        P(("img", "vol"), None),
        P(None, None, "img"),
        P(None, None, "img"),
        P("vol", "img", None),
        P("vol", "img", None),
        P("vol", "img", None),
    )
    return jax.shard_map(
        on_device,
        mesh=mesh,
        in_specs=placed,
        out_specs=(P(("img", "vol"), None), P("vol", "img", None), P("vol", "img", None)),
        check_vma=False,
    )
```

```python
import functools
import math

import jax
import jax.numpy as jnp
import ml_dtypes
import numpy as np
from jax import lax
from jax.experimental import pallas as pl
from jax.experimental.pallas import tpu as pltpu
from jax.sharding import PartitionSpec as P

AMP = 0.1
TILT = math.asin(AMP)
TURN = 2.0 * math.pi
TURN_HIGH = math.floor(TURN * 4096) / 4096
TURN_LOW = TURN - TURN_HIGH
SINE = tuple(
    factor / TURN ** (2 * power + 1)
    for power, factor in enumerate(
        (
            6.283185272722434,
            -41.341697068956265,
            81.60502462257806,
            -76.70155117622761,
            42.01616582127327,
            -14.868610992503873,
            3.199693654235983,
        )
    )
)
HUGE = 56 * 1024 * 1024
LARGE = 32 * 1024 * 1024
SMALL = 16 * 1024 * 1024
META = 128


def dft_tables(npix):
    index = np.arange(npix)
    angle = (index[:, None] * index[None, :] % npix) * (2.0 * math.pi / npix)
    scale = 1.0 / math.sqrt(npix)
    parts = [np.cos(angle) * scale, np.sin(angle) * scale]
    halves = [part[: npix // 2, parity::2] for parity in range(2) for part in parts]
    return tuple(
        jnp.asarray(np.concatenate(table, 1).astype(np.float32).astype(ml_dtypes.bfloat16))
        for table in (parts, halves)
    )


def frequency(index, npix):
    return ((index + npix // 2) % npix - npix // 2).astype(jnp.float32) / npix


def params(size):
    return pltpu.CompilerParams(vmem_limit_bytes=size)


def cost(flops, size):
    return pl.CostEstimate(flops=flops, bytes_accessed=size, transcendentals=0)


def whole():
    return pl.BlockSpec(memory_space=pltpu.VMEM)


def scalar():
    return pl.BlockSpec(memory_space=pltpu.SMEM)


def same(a, b):
    return lax.dot_general(a, b, (((1,), (1,)), ((), ())), preferred_element_type=jnp.float32)


def three_parts(value):
    parts = []
    for _ in range(3):
        part = value.astype(jnp.bfloat16).astype(jnp.float32)
        parts.append(part)
        value = value - part
    return parts


def bits(rows):
    assert rows & (rows - 1) == 0
    return rows.bit_length() - 1


def spread_over(rows, shape, image_axis):
    image = lax.broadcasted_iota(jnp.int32, shape, image_axis)
    owner = lax.broadcasted_iota(jnp.int32, shape, 1 - image_axis) >> bits(rows)
    return jnp.where(owner == image, 1.0, 0.0).astype(jnp.bfloat16)


def own_row(values, rows):
    height, width = values.shape
    sublane = lax.broadcasted_iota(jnp.int32, (rows, width), 0)
    lane = lax.broadcasted_iota(jnp.int32, (rows, width), 1) & (rows - 1)
    return jnp.where((sublane == lane)[None], values.reshape(height // rows, rows, width), 0.0)


def transform_kernel(chunk, orient_hbm, defocus_hbm, noise_hbm, image_hbm, table_hbm, halves_hbm, out_hbm, orient_ref, defocus_ref, noise_ref, image_ref, wide_ref, table_ref, halves_ref, both_ref, out_ref, in_sems, out_sems):
    npix = image_ref.shape[0]
    half = npix // 2
    ori = orient_ref.shape[1]
    starts = list(range(0, 2 * npix, chunk))
    pairs = [(image_hbm, image_ref)]
    pairs += [(table_hbm.at[:, pl.ds(start, chunk)], table_ref.at[:, pl.ds(start, chunk)]) for start in starts]
    pairs += [(halves_hbm, halves_ref), (orient_hbm, orient_ref), (defocus_hbm, defocus_ref), (noise_hbm, noise_ref)]
    loads = []
    for number, (source, target) in enumerate(pairs):
        load = pltpu.make_async_copy(source, target, in_sems.at[number])
        load.start()
        loads.append(load)
    loads[0].wait()
    tiles = range(npix // 128)
    for tile in tiles:
        wide_ref[tile] = image_ref[:, tile * 128 : (tile + 1) * 128].astype(jnp.float32)
    image = jnp.concatenate(
        [
            jnp.concatenate([wide_ref[tile, pl.ds(parity, half, 2), :] for tile in tiles], 1)
            for parity in range(2)
        ],
        0,
    ).astype(jnp.bfloat16)
    for number, start in enumerate(starts):
        loads[1 + number].wait()
        first = jnp.dot(
            image, table_ref[:, start : start + chunk], preferred_element_type=jnp.float32
        ).astype(jnp.bfloat16)
        for parity in range(2):
            part = first[parity * half : (parity + 1) * half]
            upper = slice(parity * npix, parity * npix + half)
            lower = slice(parity * npix + half, (parity + 1) * npix)
            if start < npix:
                both_ref[upper, start : start + chunk] = part
                both_ref[lower, npix + start : npix + start + chunk] = -part
            else:
                both_ref[upper, start : start + chunk] = -part
                both_ref[lower, start - npix : start - npix + chunk] = -part
    for load in loads[1 + len(starts) :]:
        load.wait()
    saves = []

    def save(start, size):
        at = pl.ds(start, size)
        copy = pltpu.make_async_copy(out_ref.at[:, at], out_hbm.at[:, at], out_sems.at[len(saves)])
        copy.start()
        saves.append(copy)

    lane = lax.broadcasted_iota(jnp.int32, (8, META), 1)
    codes = jnp.zeros((8, META), jnp.int32)
    for o in range(ori):
        label = orient_ref[0, o]
        codes = jnp.where(lane == o, label & 255, codes)
        codes = jnp.where(lane == ori + o, label >> 8, codes)
    about = codes.astype(jnp.float32)
    place = 2 * ori
    for scalar_ref in (defocus_ref, noise_ref):
        for part in three_parts(jnp.full((8, META), scalar_ref[0], jnp.float32)):
            about = jnp.where(lane == place, part, about)
            place += 1
    out_ref[:, 2 * npix :] = jnp.broadcast_to(about[:1], (npix, META)).astype(jnp.bfloat16)
    save(2 * npix, META)
    chunk = chunk // 2
    for start in range(0, 2 * npix, chunk):
        even, odd = (
            jnp.dot(
                halves_ref[:, parity * npix : (parity + 1) * npix],
                both_ref[parity * npix : (parity + 1) * npix, start : start + chunk],
                preferred_element_type=jnp.float32,
            )
            for parity in range(2)
        )
        out_ref[:half, start : start + chunk] = (even + odd).astype(jnp.bfloat16)
        out_ref[half:, start : start + chunk] = (even - odd).astype(jnp.bfloat16)
        save(start, chunk)
    for copy in saves:
        copy.wait()


def transform(orient, defocus, noise, image, table, halves):
    npix = image.shape[0]
    chunk = npix
    pieces = 2 * npix // chunk
    return pl.pallas_call(
        functools.partial(transform_kernel, chunk),
        in_specs=[pl.BlockSpec(memory_space=pl.ANY)] * 6,
        out_specs=pl.BlockSpec(memory_space=pl.ANY),
        out_shape=jax.ShapeDtypeStruct((npix, 2 * npix + META), jnp.bfloat16),
        scratch_shapes=[
            pltpu.SMEM(orient.shape, jnp.int32),
            pltpu.SMEM(defocus.shape, jnp.float32),
            pltpu.SMEM(noise.shape, jnp.float32),
            pltpu.VMEM((npix, npix), jnp.bfloat16),
            pltpu.VMEM((npix // 128, npix, 128), jnp.float32),
            pltpu.VMEM((npix, 2 * npix), jnp.bfloat16),
            pltpu.VMEM((npix // 2, 2 * npix), jnp.bfloat16),
            pltpu.VMEM((2 * npix, 2 * npix), jnp.bfloat16),
            pltpu.VMEM((npix, 2 * npix + META), jnp.bfloat16),
            pltpu.SemaphoreType.DMA((pieces + 5,)),
            pltpu.SemaphoreType.DMA((2 * pieces + 1,)),
        ],
        compiler_params=params(HUGE),
        cost_estimate=cost(12 * npix**3, 10 * npix * npix),
        name="transform",
    )(orient, defocus, noise, image, table, halves)


def prepare_kernel(planes_ref, weights_ref, lookup_ref):
    deep, labels = lookup_ref.shape
    rows = planes_ref.shape[1]
    level = lax.broadcasted_iota(jnp.int32, (deep // rows, rows, labels), 0)
    total = jnp.zeros((deep // rows, rows, labels), jnp.float32)
    for k in range(2):
        weight = weights_ref[k].astype(jnp.float32)
        total = total + jnp.where(level == planes_ref[k][None], weight[None], 0.0)
    lookup_ref[...] = total.reshape(deep, labels).astype(jnp.bfloat16)


def prepare(planes, weights, deep):
    labels = planes.shape[2]
    return pl.pallas_call(
        prepare_kernel,
        in_specs=[whole(), whole()],
        out_specs=whole(),
        out_shape=jax.ShapeDtypeStruct((deep, labels), jnp.bfloat16),
        compiler_params=params(SMALL),
        cost_estimate=cost(1 << 22, 1 << 20),
        name="prepare",
    )(planes, weights)


def contrast(defocus, row_square, start, width, npix):
    column = start + lax.broadcasted_iota(jnp.int32, (1, width), 1)
    freq_x = frequency(column, npix)
    chi = defocus * (row_square + freq_x * freq_x)
    turns = jnp.floor(chi * (1.0 / TURN) + (TILT / TURN + 0.5))
    angle = ((chi - turns * TURN_HIGH) - turns * TURN_LOW) + TILT
    square = angle * angle
    series = -SINE[-1]
    for term in SINE[-2::-1]:
        series = series * square - term
    return series * angle


def line_geometry(meta, ori, rows, many, npix, slot):
    place = 2 * ori
    defocus = meta[:, place : place + 1] + meta[:, place + 1 : place + 2] + meta[:, place + 2 : place + 3]
    index = (lax.broadcasted_iota(jnp.int32, (many, 1), 0) & (rows - 1)) + slot * rows
    freq_y = jnp.where(index < npix // 2, index, index - npix).astype(jnp.float32) / npix
    return defocus, freq_y * freq_y


def compare_kernel(ori, rows, slot_ref, fourier_ref, lookup_ref, volume_ref, filtered_ref, picks_ref, part_ref, about_ref, mix_ref, power_ref):
    many, wide = filtered_ref.shape
    npix = wide // 2
    deep = volume_ref.shape[0]
    images = many // rows

    meta = fourier_ref[:, wide:]
    here = lax.broadcasted_iota(jnp.int32, (images, many), 0) << bits(rows)
    there = lax.broadcasted_iota(jnp.int32, (images, many), 1)
    pick = jnp.where(here == there, 1.0, 0.0).astype(jnp.bfloat16)
    about = jnp.dot(pick, meta, preferred_element_type=jnp.float32)
    about_ref[...] = about
    label = lax.broadcasted_iota(jnp.int32, (images, lookup_ref.shape[1]), 1).astype(jnp.float32)
    found = []
    for o in range(ori):
        mine = about[:, o : o + 1] + 256.0 * about[:, ori + o : ori + o + 1]
        found.append(jnp.where(label == mine, 1.0, 0.0).astype(jnp.bfloat16))
    found = same(jnp.concatenate(found, 0), lookup_ref[...]).astype(jnp.bfloat16)
    picks_ref[...] = found
    spread = spread_over(rows, (many, images), 1)
    for o in range(ori):
        every = jnp.dot(
            spread, found[o * images : (o + 1) * images], preferred_element_type=jnp.float32
        )
        mix_ref[o * many : (o + 1) * many, :] = (
            own_row(every, rows).reshape(many, deep).astype(jnp.bfloat16)
        )
    defocus, row_square = line_geometry(meta.astype(jnp.float32), ori, rows, many, npix, slot_ref[0])
    for number, start in enumerate(range(0, npix, 128)):
        real = slice(start, start + 128)
        imag = slice(npix + start, npix + start + 128)
        planes = jnp.concatenate([volume_ref[:, real], volume_ref[:, imag]], 1)
        ctf = contrast(defocus, row_square, start, 128, npix)
        for part in (real, imag):
            filtered_ref[:, part] = (ctf * fourier_ref[:, part].astype(jnp.float32)).astype(jnp.bfloat16)
        square = ctf * ctf
        for o in range(ori):
            section = jnp.dot(
                mix_ref[o * many : (o + 1) * many, :], planes, preferred_element_type=jnp.float32
            )
            section = section * section
            power = square * (section[:, :128] + section[:, 128:])
            if number:
                power = power + power_ref[o]
            power_ref[o] = power

    found = own_row(same(filtered_ref[...], volume_ref[...]), rows)
    found = jnp.sum(found, axis=1)
    halves = []
    for o in range(ori):
        cross = found * picks_ref[o * images : (o + 1) * images, :].astype(jnp.float32)
        lanes = cross[:, :128]
        for start in range(128, deep, 128):
            lanes = lanes + cross[:, start : start + 128]
        power = jnp.sum(power_ref[o].reshape(images, rows, 128), axis=1)
        halves.append(lanes - 0.5 * power)
    upper = jnp.concatenate(halves[: ori // 2], 0)
    lower = jnp.concatenate(halves[ori // 2 :], 0)
    upper = jnp.sum(jnp.transpose(upper), axis=0, keepdims=True)
    lower = jnp.sum(jnp.transpose(lower), axis=0, keepdims=True)
    even = (lax.broadcasted_iota(jnp.int32, part_ref.shape, 0) & 1) == 0
    part_ref[...] = jnp.where(even, upper, lower)


def compare(slot, fourier, lookup, volume, ori, rows, copies):
    many = fourier.shape[0]
    deep, wide = volume.shape
    images = many // rows
    return pl.pallas_call(
        functools.partial(compare_kernel, ori, rows),
        in_specs=[scalar()] + [whole()] * 3,
        out_specs=(whole(),) * 4,
        out_shape=(
            jax.ShapeDtypeStruct((many, wide), jnp.bfloat16),
            jax.ShapeDtypeStruct((ori * images, deep), jnp.bfloat16),
            jax.ShapeDtypeStruct((copies * 2, 2 * images), jnp.float32),
            jax.ShapeDtypeStruct((images, META), jnp.float32),
        ),
        scratch_shapes=[
            pltpu.VMEM((ori * many, deep), jnp.bfloat16),
            pltpu.VMEM((ori, many, 128), jnp.float32),
        ],
        compiler_params=params(LARGE),
        cost_estimate=cost(1 << 31, 5 << 20),
        name="compare",
    )(slot, fourier, lookup, volume)


def squares_kernel(ori, rows, npix, slot_ref, about_ref, square_ref, noise_ref):
    many = square_ref.shape[0]
    images = many // rows
    about = about_ref[...]
    meta = jnp.dot(
        spread_over(rows, (many, images), 1),
        about.astype(jnp.bfloat16),
        preferred_element_type=jnp.float32,
    )
    defocus, row_square = line_geometry(meta, ori, rows, many, npix, slot_ref[0])
    for start in range(0, square_ref.shape[1], 128):
        ctf = contrast(defocus, row_square, start, 128, npix)
        square_ref[:, start : start + 128] = (ctf * ctf).astype(jnp.bfloat16)
    place = 2 * ori + 3
    turned = jnp.transpose(jnp.concatenate([about, about], 0))
    noise_ref[...] = turned[place : place + 1] + turned[place + 1 : place + 2] + turned[place + 2 : place + 3]


def squares(slot, about, ori, rows, npix):
    images = about.shape[0]
    return pl.pallas_call(
        functools.partial(squares_kernel, ori, rows, npix),
        in_specs=[scalar(), whole()],
        out_specs=(whole(), whole()),
        out_shape=(
            jax.ShapeDtypeStruct((images * rows, npix // 2 + 128), jnp.bfloat16),
            jax.ShapeDtypeStruct((1, 2 * images), jnp.float32),
        ),
        compiler_params=params(SMALL),
        cost_estimate=cost(1 << 27, 1 << 20),
        name="squares",
    )(slot, about)


def pack(target_ref, share, source_ref, start, last):
    pairs = target_ref.shape[0]
    slab = share.shape[0] // pairs
    sums = jnp.dot(share, source_ref[...], preferred_element_type=jnp.float32)
    for number in range(sums.shape[1] // 128):
        value = sums[:, number * 128 : (number + 1) * 128].reshape(pairs, slab, 128)
        at = (start + number) * slab
        if start + number < last:
            target_ref[:, at : at + slab, :] = value.astype(jnp.bfloat16)
        else:
            lane = lax.broadcasted_iota(jnp.int32, (pairs, slab // 2, 128), 2)
            lower = jnp.broadcast_to(value[:, slab // 2 :, :1], lane.shape)
            value = jnp.where(lane == 0, value[:, : slab // 2], lower)
            target_ref[:, at : at + slab // 2, :] = value.astype(jnp.bfloat16)


def pack_both(target_ref, share, filtered_ref, square_ref):
    tiles = filtered_ref.shape[1] // 128
    last = tiles + square_ref.shape[1] // 128 - 1
    pack(target_ref, share, filtered_ref, 0, last)
    pack(target_ref, share, square_ref, tiles, last)


def project_kernel(rows, ori, core_ref, part_ref, noise_ref, picks_ref, filtered_ref, square_ref, probs_ref, share_ref, send_ref):
    many = filtered_ref.shape[0]
    deep = picks_ref.shape[1]
    lanes = part_ref.shape[1]
    images = lanes // 2
    sums = jnp.sum(part_ref[...].reshape(part_ref.shape[0] // 8, 8, lanes), axis=0)
    sums = sums + pltpu.roll(sums, 4, 0)
    sums = sums + pltpu.roll(sums, 2, 0)
    score = sums / noise_ref[...]
    top = jnp.maximum(score, pltpu.roll(score, 1, 0))
    top = jnp.maximum(top, pltpu.roll(top, images, 1))
    power = jnp.exp(score - top)
    total = power + pltpu.roll(power, 1, 0)
    total = total + pltpu.roll(total, images, 1)
    probs = power / total
    probs_ref[...] = probs
    column = jnp.transpose(jnp.concatenate([probs] * (lanes // 8), 0))
    share = jnp.zeros((images, deep), jnp.float32)
    for o in range(ori):
        half = o % 2
        chance = column[half * images : (half + 1) * images, o // 2 : o // 2 + 1]
        share = share + chance * picks_ref[o * images : (o + 1) * images, :].astype(jnp.float32)
    share = jnp.dot(
        jnp.transpose(share).astype(jnp.bfloat16),
        spread_over(rows, (images, many), 0),
        preferred_element_type=jnp.float32,
    )
    pairs = send_ref.shape[0]
    share = own_row(share, rows).reshape(pairs, 2, deep // (2 * pairs), many)
    first = core_ref[0] == 0
    ours = jnp.where(first, share[:, 0], share[:, 1]).reshape(deep // 2, many)
    theirs = jnp.where(first, share[:, 1], share[:, 0]).reshape(deep // 2, many)
    share_ref[...] = ours.astype(jnp.bfloat16)
    pack_both(send_ref, theirs.astype(jnp.bfloat16), filtered_ref, square_ref)


def packed(deep, filtered, square, pairs):
    slab = deep // (2 * pairs)
    lines = (filtered.shape[1] + square.shape[1]) // 128 * slab - slab // 2
    return jax.ShapeDtypeStruct((pairs, lines, 128), jnp.bfloat16)


def project(core, part, noise, picks, filtered, square, rows, ori, pairs):
    many = filtered.shape[0]
    deep = picks.shape[1]
    return pl.pallas_call(
        functools.partial(project_kernel, rows, ori),
        in_specs=[scalar()] + [whole()] * 5,
        out_specs=(whole(), whole(), whole()),
        out_shape=(
            jax.ShapeDtypeStruct((8, part.shape[1]), jnp.float32),
            jax.ShapeDtypeStruct((deep // 2, many), jnp.bfloat16),
            packed(deep, filtered, square, pairs),
        ),
        compiler_params=params(LARGE),
        cost_estimate=cost(1 << 28, 4 << 20),
        name="project",
    )(core, part, noise, picks, filtered, square)


def keep_kernel(share_ref, filtered_ref, square_ref, keep_ref):
    pack_both(keep_ref, share_ref[...], filtered_ref, square_ref)


def keep_own(share, filtered, square, pairs):
    return pl.pallas_call(
        keep_kernel,
        out_shape=packed(2 * share.shape[0], filtered, square, pairs),
        compiler_params=params(SMALL),
        cost_estimate=cost(1 << 28, 2 << 20),
        name="keep_own",
    )(share, filtered, square)


def middle_kernel(high_ref, keep_ref, got_ref, own_ref, *send_refs):
    pairs = keep_ref.shape[0]
    for apart in range(pairs):
        at = high_ref[0] ^ apart
        total = keep_ref[at].astype(jnp.float32) + got_ref[at].astype(jnp.float32)
        if apart == 0:
            own_ref[...] = total
        else:
            send_refs[apart - 1][...] = total.astype(jnp.bfloat16)


def middle(high, keep, got):
    pairs, slab, wide = keep.shape
    return pl.pallas_call(
        middle_kernel,
        in_specs=[scalar(), whole(), whole()],
        out_specs=(whole(),) * pairs,
        out_shape=(jax.ShapeDtypeStruct((slab, wide), jnp.float32),)
        + (jax.ShapeDtypeStruct((slab, wide), jnp.bfloat16),) * (pairs - 1),
        compiler_params=params(SMALL),
        cost_estimate=cost(1 << 20, 2 << 20),
        name="middle",
    )(high, keep, got)


def spread_lines(total, slab, npix):
    half = npix // 2
    tiles = [total[at : at + slab] for at in range(0, total.shape[0] - slab // 2, slab)]
    data = jnp.concatenate(tiles[: 2 * npix // 128], 1)
    lower = jnp.concatenate(tiles[2 * npix // 128 :], 1)
    source = lax.broadcasted_iota(jnp.int32, (half, half), 0)
    target = lax.broadcasted_iota(jnp.int32, (half, half), 1)
    mirror = jnp.where(source + target == half, 1.0, 0.0)
    upper = jnp.dot(lower, mirror, preferred_element_type=jnp.float32, precision=lax.Precision.HIGHEST)
    last = total[total.shape[0] - slab // 2 :]
    last = jnp.concatenate([last[:, :1], last[:, 1:2]], 0)
    lane = lax.broadcasted_iota(jnp.int32, (slab, half), 1)
    upper = jnp.where(lane == 0, last, upper)
    return data, lower, upper


def finish_kernel(own_ref, *refs):
    data_ref, weight_ref, data_out, weight_out = refs[-4:]
    slab, npix = weight_ref.shape
    total = own_ref[...]
    for part_ref in refs[:-4]:
        total = total + part_ref[...].astype(jnp.float32)
    data, lower, upper = spread_lines(total, slab, npix)
    data_out[...] = data_ref[...] + data
    weight_out[:, : npix // 2] = weight_ref[:, : npix // 2] + lower
    weight_out[:, npix // 2 :] = weight_ref[:, npix // 2 :] + upper


def finish(own, parts, data_old, weight_old):
    return pl.pallas_call(
        finish_kernel,
        out_shape=(
            jax.ShapeDtypeStruct(data_old.shape, jnp.float32),
            jax.ShapeDtypeStruct(weight_old.shape, jnp.float32),
        ),
        compiler_params=params(SMALL),
        cost_estimate=cost(1 << 20, 2 << 20),
        name="finish",
    )(own, *parts, data_old, weight_old)


def on_device(images, defocus, noise, orient, planes, weights, volume, data_old, weight_old):
    npix = images.shape[1]
    ori = orient.shape[1]
    n_img = lax.axis_size("img")
    n_vol = lax.axis_size("vol")
    rows = npix // n_img
    slab = volume.shape[0]
    deep = n_vol * slab * rows
    many = n_img * rows
    pairs = n_vol // 2
    slot = lax.axis_index("img").astype(jnp.int32).reshape(1)
    place = lax.axis_index("vol").astype(jnp.int32)

    fourier = transform(orient, defocus, noise, images[0], *dft_tables(npix))
    fourier = lax.all_to_all(
        fourier.reshape(n_img, rows, 2 * npix + META), "img", split_axis=0, concat_axis=0, tiled=True
    ).reshape(many, 2 * npix + META)
    vol_rows = lax.all_gather(volume.reshape(slab * rows, 2 * npix), "vol", axis=0, tiled=True)
    lookup = prepare(jnp.swapaxes(planes, 1, 2), jnp.swapaxes(weights, 1, 2), deep)
    filtered, picks, part, about = compare(slot, fourier, lookup, vol_rows, ori, rows, n_img)
    square, noise_all = squares(slot, about, ori, rows, npix)
    part = lax.all_to_all(
        part.reshape(n_img, 2, 2 * n_img), "img", split_axis=0, concat_axis=0, tiled=True
    ).reshape(2 * n_img, 2 * n_img)
    probs, share, send = project(
        (place % 2).reshape(1), part, noise_all, picks, filtered, square, rows, ori, pairs
    )
    mine = lax.dynamic_slice_in_dim(
        probs[:2].reshape(2 * 2, n_img), lax.axis_index("img"), 1, 1
    ).reshape(1, ori)
    got = lax.ppermute(send, "vol", [(v, v ^ 1) for v in range(n_vol)])
    keep = keep_own(share, filtered, square, pairs)
    own, *sends = middle((place // 2).reshape(1), keep, got)
    parts = [
        lax.ppermute(sends[apart - 1], "vol", [(v, v ^ (2 * apart)) for v in range(n_vol)])
        for apart in (2, 3, 1)
    ]
    data, weight = finish(
        own,
        parts,
        data_old.reshape(slab * rows, 2 * npix),
        weight_old.reshape(slab * rows, npix),
    )
    return (mine, data.reshape(data_old.shape), weight.reshape(weight_old.shape))


def solution(mesh):
    placed = (
        P(("img", "vol"), None, None),
        P(("img", "vol")),
        P(("img", "vol")),
        P(("img", "vol"), None),
        P(None, None, "img"),
        P(None, None, "img"),
        P("vol", "img", None),
        P("vol", "img", None),
        P("vol", "img", None),
    )
    return jax.shard_map(
        on_device,
        mesh=mesh,
        in_specs=placed,
        out_specs=(P(("img", "vol"), None), P("vol", "img", None), P("vol", "img", None)),
        check_vma=False,
    )
```

```python
import functools
import math

import jax
import jax.numpy as jnp
import ml_dtypes
import numpy as np
from jax import lax
from jax.experimental import pallas as pl
from jax.experimental.pallas import tpu as pltpu
from jax.sharding import PartitionSpec as P

AMP = 0.1
TILT = math.asin(AMP)
TURN = 2.0 * math.pi
TURN_HIGH = math.floor(TURN * 4096) / 4096
TURN_LOW = TURN - TURN_HIGH
SINE = tuple(
    factor / TURN ** (2 * power + 1)
    for power, factor in enumerate(
        (
            6.283185272722434,
            -41.341697068956265,
            81.60502462257806,
            -76.70155117622761,
            42.01616582127327,
            -14.868610992503873,
            3.199693654235983,
        )
    )
)
HUGE = 56 * 1024 * 1024
LARGE = 32 * 1024 * 1024
SMALL = 16 * 1024 * 1024
META = 128


def dft_tables(npix):
    index = np.arange(npix)
    angle = (index[:, None] * index[None, :] % npix) * (2.0 * math.pi / npix)
    scale = 1.0 / math.sqrt(npix)
    parts = [np.cos(angle) * scale, np.sin(angle) * scale]
    halves = [part[: npix // 2, parity::2] for parity in range(2) for part in parts]
    return tuple(
        jnp.asarray(np.concatenate(table, 1).astype(np.float32).astype(ml_dtypes.bfloat16))
        for table in (parts, halves)
    )


def frequency(index, npix):
    return ((index + npix // 2) % npix - npix // 2).astype(jnp.float32) / npix


def params(size):
    return pltpu.CompilerParams(vmem_limit_bytes=size)


def cost(flops, size):
    return pl.CostEstimate(flops=flops, bytes_accessed=size, transcendentals=0)


def whole():
    return pl.BlockSpec(memory_space=pltpu.VMEM)


def scalar():
    return pl.BlockSpec(memory_space=pltpu.SMEM)


def same(a, b):
    return lax.dot_general(a, b, (((1,), (1,)), ((), ())), preferred_element_type=jnp.float32)


def three_parts(value):
    parts = []
    for _ in range(3):
        part = value.astype(jnp.bfloat16).astype(jnp.float32)
        parts.append(part)
        value = value - part
    return parts


def bits(rows):
    assert rows & (rows - 1) == 0
    return rows.bit_length() - 1


def spread_over(rows, shape, image_axis):
    image = lax.broadcasted_iota(jnp.int32, shape, image_axis)
    owner = lax.broadcasted_iota(jnp.int32, shape, 1 - image_axis) >> bits(rows)
    return jnp.where(owner == image, 1.0, 0.0).astype(jnp.bfloat16)


def own_row(values, rows):
    height, width = values.shape
    sublane = lax.broadcasted_iota(jnp.int32, (rows, width), 0)
    lane = lax.broadcasted_iota(jnp.int32, (rows, width), 1) & (rows - 1)
    return jnp.where((sublane == lane)[None], values.reshape(height // rows, rows, width), 0.0)


def transform_kernel(chunk, orient_hbm, defocus_hbm, noise_hbm, image_hbm, table_hbm, halves_hbm, out_hbm, orient_ref, defocus_ref, noise_ref, image_ref, wide_ref, table_ref, halves_ref, both_ref, out_ref, in_sems, out_sems):
    npix = image_ref.shape[0]
    half = npix // 2
    ori = orient_ref.shape[1]
    starts = list(range(0, 2 * npix, chunk))
    pairs = [(image_hbm, image_ref)]
    pairs += [(table_hbm.at[:, pl.ds(start, chunk)], table_ref.at[:, pl.ds(start, chunk)]) for start in starts]
    pairs += [(halves_hbm, halves_ref), (orient_hbm, orient_ref), (defocus_hbm, defocus_ref), (noise_hbm, noise_ref)]
    loads = []
    for number, (source, target) in enumerate(pairs):
        load = pltpu.make_async_copy(source, target, in_sems.at[number])
        load.start()
        loads.append(load)
    loads[0].wait()
    tiles = range(npix // 128)
    for tile in tiles:
        wide_ref[tile] = image_ref[:, tile * 128 : (tile + 1) * 128].astype(jnp.float32)
    image = jnp.concatenate(
        [
            jnp.concatenate([wide_ref[tile, pl.ds(parity, half, 2), :] for tile in tiles], 1)
            for parity in range(2)
        ],
        0,
    ).astype(jnp.bfloat16)
    for number, start in enumerate(starts):
        loads[1 + number].wait()
        first = jnp.dot(
            image, table_ref[:, start : start + chunk], preferred_element_type=jnp.float32
        ).astype(jnp.bfloat16)
        for parity in range(2):
            part = first[parity * half : (parity + 1) * half]
            upper = slice(parity * npix, parity * npix + half)
            lower = slice(parity * npix + half, (parity + 1) * npix)
            if start < npix:
                both_ref[upper, start : start + chunk] = part
                both_ref[lower, npix + start : npix + start + chunk] = -part
            else:
                both_ref[upper, start : start + chunk] = -part
                both_ref[lower, start - npix : start - npix + chunk] = -part
    for load in loads[1 + len(starts) :]:
        load.wait()
    saves = []

    def save(start, size):
        at = pl.ds(start, size)
        copy = pltpu.make_async_copy(out_ref.at[:, at], out_hbm.at[:, at], out_sems.at[len(saves)])
        copy.start()
        saves.append(copy)

    lane = lax.broadcasted_iota(jnp.int32, (8, META), 1)
    codes = jnp.zeros((8, META), jnp.int32)
    for o in range(ori):
        label = orient_ref[0, o]
        codes = jnp.where(lane == o, label & 255, codes)
        codes = jnp.where(lane == ori + o, label >> 8, codes)
    about = codes.astype(jnp.float32)
    place = 2 * ori
    for scalar_ref in (defocus_ref, noise_ref):
        for part in three_parts(jnp.full((8, META), scalar_ref[0], jnp.float32)):
            about = jnp.where(lane == place, part, about)
            place += 1
    out_ref[:, 2 * npix :] = jnp.broadcast_to(about[:1], (npix, META)).astype(jnp.bfloat16)
    save(2 * npix, META)
    chunk = chunk // 2
    for start in range(0, 2 * npix, chunk):
        even, odd = (
            jnp.dot(
                halves_ref[:, parity * npix : (parity + 1) * npix],
                both_ref[parity * npix : (parity + 1) * npix, start : start + chunk],
                preferred_element_type=jnp.float32,
            )
            for parity in range(2)
        )
        out_ref[:half, start : start + chunk] = (even + odd).astype(jnp.bfloat16)
        out_ref[half:, start : start + chunk] = (even - odd).astype(jnp.bfloat16)
        save(start, chunk)
    for copy in saves:
        copy.wait()


def transform(orient, defocus, noise, image, table, halves):
    npix = image.shape[0]
    chunk = npix
    pieces = 2 * npix // chunk
    return pl.pallas_call(
        functools.partial(transform_kernel, chunk),
        in_specs=[pl.BlockSpec(memory_space=pl.ANY)] * 6,
        out_specs=pl.BlockSpec(memory_space=pl.ANY),
        out_shape=jax.ShapeDtypeStruct((npix, 2 * npix + META), jnp.bfloat16),
        scratch_shapes=[
            pltpu.SMEM(orient.shape, jnp.int32),
            pltpu.SMEM(defocus.shape, jnp.float32),
            pltpu.SMEM(noise.shape, jnp.float32),
            pltpu.VMEM((npix, npix), jnp.bfloat16),
            pltpu.VMEM((npix // 128, npix, 128), jnp.float32),
            pltpu.VMEM((npix, 2 * npix), jnp.bfloat16),
            pltpu.VMEM((npix // 2, 2 * npix), jnp.bfloat16),
            pltpu.VMEM((2 * npix, 2 * npix), jnp.bfloat16),
            pltpu.VMEM((npix, 2 * npix + META), jnp.bfloat16),
            pltpu.SemaphoreType.DMA((pieces + 5,)),
            pltpu.SemaphoreType.DMA((2 * pieces + 1,)),
        ],
        compiler_params=params(HUGE),
        cost_estimate=cost(12 * npix**3, 10 * npix * npix),
        name="transform",
    )(orient, defocus, noise, image, table, halves)


def prepare_kernel(planes_ref, weights_ref, lookup_ref):
    deep, labels = lookup_ref.shape
    rows = planes_ref.shape[1]
    level = lax.broadcasted_iota(jnp.int32, (deep // rows, rows, labels), 0)
    total = jnp.zeros((deep // rows, rows, labels), jnp.float32)
    for k in range(2):
        weight = weights_ref[k].astype(jnp.float32)
        total = total + jnp.where(level == planes_ref[k][None], weight[None], 0.0)
    lookup_ref[...] = total.reshape(deep, labels).astype(jnp.bfloat16)


def prepare(planes, weights, deep):
    labels = planes.shape[2]
    return pl.pallas_call(
        prepare_kernel,
        in_specs=[whole(), whole()],
        out_specs=whole(),
        out_shape=jax.ShapeDtypeStruct((deep, labels), jnp.bfloat16),
        compiler_params=params(SMALL),
        cost_estimate=cost(1 << 22, 1 << 20),
        name="prepare",
    )(planes, weights)


def contrast(defocus, row_square, start, width, npix):
    column = start + lax.broadcasted_iota(jnp.int32, (1, width), 1)
    freq_x = frequency(column, npix)
    chi = defocus * (row_square + freq_x * freq_x)
    turns = jnp.floor(chi * (1.0 / TURN) + (TILT / TURN + 0.5))
    angle = ((chi - turns * TURN_HIGH) - turns * TURN_LOW) + TILT
    square = angle * angle
    series = -SINE[-1]
    for term in SINE[-2::-1]:
        series = series * square - term
    return series * angle


def line_geometry(meta, ori, rows, many, npix, slot):
    place = 2 * ori
    defocus = meta[:, place : place + 1] + meta[:, place + 1 : place + 2] + meta[:, place + 2 : place + 3]
    index = (lax.broadcasted_iota(jnp.int32, (many, 1), 0) & (rows - 1)) + slot * rows
    freq_y = jnp.where(index < npix // 2, index, index - npix).astype(jnp.float32) / npix
    return defocus, freq_y * freq_y


def compare_kernel(ori, rows, slot_ref, fourier_ref, lookup_ref, volume_ref, filtered_ref, picks_ref, part_ref, about_ref, mix_ref, power_ref):
    many, wide = filtered_ref.shape
    npix = wide // 2
    deep = volume_ref.shape[0]
    images = many // rows

    meta = fourier_ref[:, wide:]
    here = lax.broadcasted_iota(jnp.int32, (images, many), 0) << bits(rows)
    there = lax.broadcasted_iota(jnp.int32, (images, many), 1)
    pick = jnp.where(here == there, 1.0, 0.0).astype(jnp.bfloat16)
    about = jnp.dot(pick, meta, preferred_element_type=jnp.float32)
    about_ref[...] = about
    label = lax.broadcasted_iota(jnp.int32, (images, lookup_ref.shape[1]), 1).astype(jnp.float32)
    found = []
    for o in range(ori):
        mine = about[:, o : o + 1] + 256.0 * about[:, ori + o : ori + o + 1]
        found.append(jnp.where(label == mine, 1.0, 0.0).astype(jnp.bfloat16))
    found = same(jnp.concatenate(found, 0), lookup_ref[...]).astype(jnp.bfloat16)
    picks_ref[...] = found
    spread = spread_over(rows, (many, images), 1)
    for o in range(ori):
        every = jnp.dot(
            spread, found[o * images : (o + 1) * images], preferred_element_type=jnp.float32
        )
        mix_ref[o * many : (o + 1) * many, :] = (
            own_row(every, rows).reshape(many, deep).astype(jnp.bfloat16)
        )
    defocus, row_square = line_geometry(meta.astype(jnp.float32), ori, rows, many, npix, slot_ref[0])
    def sections(start):
        planes = jnp.concatenate(
            [volume_ref[:, at : at + 128] for at in (start, npix + start)], 1
        )
        return [
            jnp.dot(
                mix_ref[o * many : (o + 1) * many, :], planes, preferred_element_type=jnp.float32
            )
            for o in range(ori)
        ]

    current = sections(0)
    for start in range(0, npix, 128):
        ctf = contrast(defocus, row_square, start, 128, npix)
        for at in (start, npix + start):
            filtered_ref[:, at : at + 128] = (
                ctf * fourier_ref[:, at : at + 128].astype(jnp.float32)
            ).astype(jnp.bfloat16)
        square = ctf * ctf
        following = sections(start + 128) if start + 128 < npix else None
        for o in range(ori):
            section = current[o] * current[o]
            power = square * (section[:, :128] + section[:, 128:])
            if start:
                power = power + power_ref[o]
            power_ref[o] = power
        current = following

    found = own_row(same(filtered_ref[...], volume_ref[...]), rows)
    found = jnp.sum(found, axis=1)
    halves = []
    for o in range(ori):
        cross = found * picks_ref[o * images : (o + 1) * images, :].astype(jnp.float32)
        lanes = cross[:, :128]
        for start in range(128, deep, 128):
            lanes = lanes + cross[:, start : start + 128]
        power = jnp.sum(power_ref[o].reshape(images, rows, 128), axis=1)
        halves.append(lanes - 0.5 * power)
    upper = jnp.concatenate(halves[: ori // 2], 0)
    lower = jnp.concatenate(halves[ori // 2 :], 0)
    upper = jnp.sum(jnp.transpose(upper), axis=0, keepdims=True)
    lower = jnp.sum(jnp.transpose(lower), axis=0, keepdims=True)
    even = (lax.broadcasted_iota(jnp.int32, part_ref.shape, 0) & 1) == 0
    part_ref[...] = jnp.where(even, upper, lower)


def compare(slot, fourier, lookup, volume, ori, rows, copies):
    many = fourier.shape[0]
    deep, wide = volume.shape
    images = many // rows
    return pl.pallas_call(
        functools.partial(compare_kernel, ori, rows),
        in_specs=[scalar()] + [whole()] * 3,
        out_specs=(whole(),) * 4,
        out_shape=(
            jax.ShapeDtypeStruct((many, wide), jnp.bfloat16),
            jax.ShapeDtypeStruct((ori * images, deep), jnp.bfloat16),
            jax.ShapeDtypeStruct((copies * 2, 2 * images), jnp.float32),
            jax.ShapeDtypeStruct((images, META), jnp.float32),
        ),
        scratch_shapes=[
            pltpu.VMEM((ori * many, deep), jnp.bfloat16),
            pltpu.VMEM((ori, many, 128), jnp.float32),
        ],
        compiler_params=params(LARGE),
        cost_estimate=cost(1 << 31, 5 << 20),
        name="compare",
    )(slot, fourier, lookup, volume)


def squares_kernel(ori, rows, npix, slot_ref, about_ref, square_ref, noise_ref):
    many = square_ref.shape[0]
    images = many // rows
    about = about_ref[...]
    meta = jnp.dot(
        spread_over(rows, (many, images), 1),
        about.astype(jnp.bfloat16),
        preferred_element_type=jnp.float32,
    )
    defocus, row_square = line_geometry(meta, ori, rows, many, npix, slot_ref[0])
    for start in range(0, square_ref.shape[1], 128):
        ctf = contrast(defocus, row_square, start, 128, npix)
        square_ref[:, start : start + 128] = (ctf * ctf).astype(jnp.bfloat16)
    place = 2 * ori + 3
    turned = jnp.transpose(jnp.concatenate([about, about], 0))
    noise_ref[...] = turned[place : place + 1] + turned[place + 1 : place + 2] + turned[place + 2 : place + 3]


def squares(slot, about, ori, rows, npix):
    images = about.shape[0]
    return pl.pallas_call(
        functools.partial(squares_kernel, ori, rows, npix),
        in_specs=[scalar(), whole()],
        out_specs=(whole(), whole()),
        out_shape=(
            jax.ShapeDtypeStruct((images * rows, npix // 2 + 128), jnp.bfloat16),
            jax.ShapeDtypeStruct((1, 2 * images), jnp.float32),
        ),
        compiler_params=params(SMALL),
        cost_estimate=cost(1 << 27, 1 << 20),
        name="squares",
    )(slot, about)


def pack(target_ref, share, source_ref, start, last):
    pairs = target_ref.shape[0]
    slab = share.shape[0] // pairs
    sums = jnp.dot(share, source_ref[...], preferred_element_type=jnp.float32)
    for number in range(sums.shape[1] // 128):
        value = sums[:, number * 128 : (number + 1) * 128].reshape(pairs, slab, 128)
        at = (start + number) * slab
        if start + number < last:
            target_ref[:, at : at + slab, :] = value.astype(jnp.bfloat16)
        else:
            lane = lax.broadcasted_iota(jnp.int32, (pairs, slab // 2, 128), 2)
            lower = jnp.broadcast_to(value[:, slab // 2 :, :1], lane.shape)
            value = jnp.where(lane == 0, value[:, : slab // 2], lower)
            target_ref[:, at : at + slab // 2, :] = value.astype(jnp.bfloat16)


def pack_both(target_ref, share, filtered_ref, square_ref):
    tiles = filtered_ref.shape[1] // 128
    last = tiles + square_ref.shape[1] // 128 - 1
    pack(target_ref, share, filtered_ref, 0, last)
    pack(target_ref, share, square_ref, tiles, last)


def project_kernel(rows, ori, core_ref, part_ref, noise_ref, picks_ref, filtered_ref, square_ref, probs_ref, share_ref, send_ref):
    many = filtered_ref.shape[0]
    deep = picks_ref.shape[1]
    lanes = part_ref.shape[1]
    images = lanes // 2
    sums = jnp.sum(part_ref[...].reshape(part_ref.shape[0] // 8, 8, lanes), axis=0)
    sums = sums + pltpu.roll(sums, 4, 0)
    sums = sums + pltpu.roll(sums, 2, 0)
    score = sums / noise_ref[...]
    top = jnp.maximum(score, pltpu.roll(score, 1, 0))
    top = jnp.maximum(top, pltpu.roll(top, images, 1))
    power = jnp.exp(score - top)
    total = power + pltpu.roll(power, 1, 0)
    total = total + pltpu.roll(total, images, 1)
    probs = power / total
    probs_ref[...] = probs
    column = jnp.transpose(jnp.concatenate([probs] * (lanes // 8), 0))
    share = jnp.zeros((images, deep), jnp.float32)
    for o in range(ori):
        half = o % 2
        chance = column[half * images : (half + 1) * images, o // 2 : o // 2 + 1]
        share = share + chance * picks_ref[o * images : (o + 1) * images, :].astype(jnp.float32)
    share = jnp.dot(
        jnp.transpose(share).astype(jnp.bfloat16),
        spread_over(rows, (images, many), 0),
        preferred_element_type=jnp.float32,
    )
    pairs = send_ref.shape[0]
    share = own_row(share, rows).reshape(pairs, 2, deep // (2 * pairs), many)
    first = core_ref[0] == 0
    ours = jnp.where(first, share[:, 0], share[:, 1]).reshape(deep // 2, many)
    theirs = jnp.where(first, share[:, 1], share[:, 0]).reshape(deep // 2, many)
    share_ref[...] = ours.astype(jnp.bfloat16)
    pack_both(send_ref, theirs.astype(jnp.bfloat16), filtered_ref, square_ref)


def packed(deep, filtered, square, pairs):
    slab = deep // (2 * pairs)
    lines = (filtered.shape[1] + square.shape[1]) // 128 * slab - slab // 2
    return jax.ShapeDtypeStruct((pairs, lines, 128), jnp.bfloat16)


def project(core, part, noise, picks, filtered, square, rows, ori, pairs):
    many = filtered.shape[0]
    deep = picks.shape[1]
    return pl.pallas_call(
        functools.partial(project_kernel, rows, ori),
        in_specs=[scalar()] + [whole()] * 5,
        out_specs=(whole(), whole(), whole()),
        out_shape=(
            jax.ShapeDtypeStruct((8, part.shape[1]), jnp.float32),
            jax.ShapeDtypeStruct((deep // 2, many), jnp.bfloat16),
            packed(deep, filtered, square, pairs),
        ),
        compiler_params=params(LARGE),
        cost_estimate=cost(1 << 28, 4 << 20),
        name="project",
    )(core, part, noise, picks, filtered, square)


def keep_kernel(share_ref, filtered_ref, square_ref, keep_ref):
    pack_both(keep_ref, share_ref[...], filtered_ref, square_ref)


def keep_own(share, filtered, square, pairs):
    return pl.pallas_call(
        keep_kernel,
        out_shape=packed(2 * share.shape[0], filtered, square, pairs),
        compiler_params=params(SMALL),
        cost_estimate=cost(1 << 28, 2 << 20),
        name="keep_own",
    )(share, filtered, square)


def middle_kernel(high_ref, keep_ref, got_ref, own_ref, *send_refs):
    pairs = keep_ref.shape[0]
    for apart in range(pairs):
        at = high_ref[0] ^ apart
        total = keep_ref[at].astype(jnp.float32) + got_ref[at].astype(jnp.float32)
        if apart == 0:
            own_ref[...] = total
        else:
            send_refs[apart - 1][...] = total.astype(jnp.bfloat16)


def middle(high, keep, got):
    pairs, slab, wide = keep.shape
    return pl.pallas_call(
        middle_kernel,
        in_specs=[scalar(), whole(), whole()],
        out_specs=(whole(),) * pairs,
        out_shape=(jax.ShapeDtypeStruct((slab, wide), jnp.float32),)
        + (jax.ShapeDtypeStruct((slab, wide), jnp.bfloat16),) * (pairs - 1),
        compiler_params=params(SMALL),
        cost_estimate=cost(1 << 20, 2 << 20),
        name="middle",
    )(high, keep, got)


def mirror_columns(lower, last, precision=None):
    slab, half = lower.shape
    source = lax.broadcasted_iota(jnp.int32, (half, half), 0)
    target = lax.broadcasted_iota(jnp.int32, (half, half), 1)
    mirror = jnp.where(source + target == half, 1.0, 0.0).astype(lower.dtype)
    upper = jnp.dot(lower, mirror, preferred_element_type=jnp.float32, precision=precision)
    lane = lax.broadcasted_iota(jnp.int32, (slab, half), 1)
    return jnp.where(lane == 0, last, upper)


def spread_lines(lines, slab, npix):
    tiles = [lines[at : at + slab] for at in range(0, lines.shape[0] - slab // 2, slab)]
    last = lines[lines.shape[0] - slab // 2 :].astype(jnp.float32)
    last = jnp.concatenate([last[:, :1], last[:, 1:2]], 0)
    count = 2 * npix // 128
    return jnp.concatenate(tiles[:count], 1), jnp.concatenate(tiles[count:], 1), last


def collect_kernel(own_ref, data_ref, weight_ref, data_out, weight_out):
    slab, npix = weight_ref.shape
    half = npix // 2
    data, lower, last = spread_lines(own_ref[...], slab, npix)
    data_out[...] = data_ref[...] + data
    weight_out[:, :half] = weight_ref[:, :half] + lower
    weight_out[:, half:] = weight_ref[:, half:] + mirror_columns(
        lower, last, lax.Precision.HIGHEST
    )


def finish_kernel(*refs):
    *part_refs, data_ref, weight_ref, data_out, weight_out = refs
    slab, npix = weight_ref.shape
    half = npix // 2
    data = data_ref[...]
    weight = weight_ref[:, :half]
    lowers, lasts = [], []
    for part_ref in part_refs:
        part, lower, last = spread_lines(part_ref[...], slab, npix)
        data = data + part.astype(jnp.float32)
        weight = weight + lower.astype(jnp.float32)
        lowers.append(lower)
        lasts.append(last)
    uppers = mirror_columns(jnp.concatenate(lowers, 0), jnp.concatenate(lasts, 0))
    upper = weight_ref[:, half:]
    for number in range(len(part_refs)):
        upper = upper + uppers[number * slab : (number + 1) * slab]
    data_out[...] = data
    weight_out[:, :half] = weight
    weight_out[:, half:] = upper


def add_lines(kernel, name, lines, data, weight):
    return pl.pallas_call(
        kernel,
        out_shape=(
            jax.ShapeDtypeStruct(data.shape, jnp.float32),
            jax.ShapeDtypeStruct(weight.shape, jnp.float32),
        ),
        compiler_params=params(SMALL),
        cost_estimate=cost(1 << 20, 2 << 20),
        name=name,
    )(*lines, data, weight)


def on_device(images, defocus, noise, orient, planes, weights, volume, data_old, weight_old):
    npix = images.shape[1]
    ori = orient.shape[1]
    n_img = lax.axis_size("img")
    n_vol = lax.axis_size("vol")
    rows = npix // n_img
    slab = volume.shape[0]
    deep = n_vol * slab * rows
    many = n_img * rows
    pairs = n_vol // 2
    slot = lax.axis_index("img").astype(jnp.int32).reshape(1)
    place = lax.axis_index("vol").astype(jnp.int32)

    fourier = transform(orient, defocus, noise, images[0], *dft_tables(npix))
    fourier = lax.all_to_all(
        fourier.reshape(n_img, rows, 2 * npix + META), "img", split_axis=0, concat_axis=0, tiled=True
    ).reshape(many, 2 * npix + META)
    vol_rows = lax.all_gather(volume.reshape(slab * rows, 2 * npix), "vol", axis=0, tiled=True)
    lookup = prepare(jnp.swapaxes(planes, 1, 2), jnp.swapaxes(weights, 1, 2), deep)
    filtered, picks, part, about = compare(slot, fourier, lookup, vol_rows, ori, rows, n_img)
    square, noise_all = squares(slot, about, ori, rows, npix)
    part = lax.all_to_all(
        part.reshape(n_img, 2, 2 * n_img), "img", split_axis=0, concat_axis=0, tiled=True
    ).reshape(2 * n_img, 2 * n_img)
    probs, share, send = project(
        (place % 2).reshape(1), part, noise_all, picks, filtered, square, rows, ori, pairs
    )
    mine = lax.dynamic_slice_in_dim(
        probs[:2].reshape(2 * 2, n_img), lax.axis_index("img"), 1, 1
    ).reshape(1, ori)
    got = lax.ppermute(send, "vol", [(v, v ^ 1) for v in range(n_vol)])
    keep = keep_own(share, filtered, square, pairs)
    own, *sends = middle((place // 2).reshape(1), keep, got)
    parts = [
        lax.ppermute(sends[apart - 1], "vol", [(v, v ^ (2 * apart)) for v in range(n_vol)])
        for apart in (2, 1, 3)
    ]
    data, weight = add_lines(
        collect_kernel,
        "collect",
        [own],
        data_old.reshape(slab * rows, 2 * npix),
        weight_old.reshape(slab * rows, npix),
    )
    data, weight = add_lines(finish_kernel, "finish", parts, data, weight)
    return (mine, data.reshape(data_old.shape), weight.reshape(weight_old.shape))


def solution(mesh):
    placed = (
        P(("img", "vol"), None, None),
        P(("img", "vol")),
        P(("img", "vol")),
        P(("img", "vol"), None),
        P(None, None, "img"),
        P(None, None, "img"),
        P("vol", "img", None),
        P("vol", "img", None),
        P("vol", "img", None),
    )
    return jax.shard_map(
        on_device,
        mesh=mesh,
        in_specs=placed,
        out_specs=(P(("img", "vol"), None), P("vol", "img", None), P("vol", "img", None)),
        check_vma=False,
    )
```

```python
import functools
import math

import jax
import jax.numpy as jnp
import ml_dtypes
import numpy as np
from jax import lax
from jax.experimental import pallas as pl
from jax.experimental.pallas import tpu as pltpu
from jax.sharding import PartitionSpec as P

AMP = 0.1
TILT = math.asin(AMP)
TURN = 2.0 * math.pi
TURN_HIGH = math.floor(TURN * 4096) / 4096
TURN_LOW = TURN - TURN_HIGH
SINE = tuple(
    factor / TURN ** (2 * power + 1)
    for power, factor in enumerate(
        (
            6.283185272722434,
            -41.341697068956265,
            81.60502462257806,
            -76.70155117622761,
            42.01616582127327,
            -14.868610992503873,
            3.199693654235983,
        )
    )
)
HUGE = 56 * 1024 * 1024
LARGE = 32 * 1024 * 1024
SMALL = 16 * 1024 * 1024
META = 128


def dft_tables(npix):
    index = np.arange(npix)
    angle = (index[:, None] * index[None, :] % npix) * (2.0 * math.pi / npix)
    scale = 1.0 / math.sqrt(npix)
    parts = [np.cos(angle) * scale, np.sin(angle) * scale]
    halves = [part[: npix // 2, parity::2] for parity in range(2) for part in parts]
    return tuple(
        jnp.asarray(np.concatenate(table, 1).astype(np.float32).astype(ml_dtypes.bfloat16))
        for table in (parts, halves)
    )


def frequency(index, npix):
    return ((index + npix // 2) % npix - npix // 2).astype(jnp.float32) / npix


def params(size):
    return pltpu.CompilerParams(vmem_limit_bytes=size)


def cost(flops, size):
    return pl.CostEstimate(flops=flops, bytes_accessed=size, transcendentals=0)


def whole():
    return pl.BlockSpec(memory_space=pltpu.VMEM)


def scalar():
    return pl.BlockSpec(memory_space=pltpu.SMEM)


def same(a, b):
    return lax.dot_general(a, b, (((1,), (1,)), ((), ())), preferred_element_type=jnp.float32)


def three_parts(value):
    parts = []
    for _ in range(3):
        part = value.astype(jnp.bfloat16).astype(jnp.float32)
        parts.append(part)
        value = value - part
    return parts


def bits(rows):
    assert rows & (rows - 1) == 0
    return rows.bit_length() - 1


def spread_over(rows, shape, image_axis):
    image = lax.broadcasted_iota(jnp.int32, shape, image_axis)
    owner = lax.broadcasted_iota(jnp.int32, shape, 1 - image_axis) >> bits(rows)
    return jnp.where(owner == image, 1.0, 0.0).astype(jnp.bfloat16)


def own_row(values, rows):
    height, width = values.shape
    sublane = lax.broadcasted_iota(jnp.int32, (rows, width), 0)
    lane = lax.broadcasted_iota(jnp.int32, (rows, width), 1) & (rows - 1)
    return jnp.where((sublane == lane)[None], values.reshape(height // rows, rows, width), 0.0)


def transform_kernel(chunk, orient_hbm, defocus_hbm, noise_hbm, image_hbm, table_hbm, halves_hbm, out_hbm, orient_ref, defocus_ref, noise_ref, image_ref, wide_ref, table_ref, halves_ref, both_ref, out_ref, in_sems, out_sems):
    npix = image_ref.shape[0]
    half = npix // 2
    ori = orient_ref.shape[1]
    starts = list(range(0, 2 * npix, chunk))
    pairs = [(image_hbm, image_ref)]
    pairs += [(table_hbm.at[:, pl.ds(start, chunk)], table_ref.at[:, pl.ds(start, chunk)]) for start in starts]
    pairs += [(halves_hbm, halves_ref), (orient_hbm, orient_ref), (defocus_hbm, defocus_ref), (noise_hbm, noise_ref)]
    loads = []
    for number, (source, target) in enumerate(pairs):
        load = pltpu.make_async_copy(source, target, in_sems.at[number])
        load.start()
        loads.append(load)
    loads[0].wait()
    tiles = range(npix // 128)
    for tile in tiles:
        wide_ref[tile] = image_ref[:, tile * 128 : (tile + 1) * 128].astype(jnp.float32)
    image = jnp.concatenate(
        [
            jnp.concatenate([wide_ref[tile, pl.ds(parity, half, 2), :] for tile in tiles], 1)
            for parity in range(2)
        ],
        0,
    ).astype(jnp.bfloat16)
    for number, start in enumerate(starts):
        loads[1 + number].wait()
        first = jnp.dot(
            image, table_ref[:, start : start + chunk], preferred_element_type=jnp.float32
        ).astype(jnp.bfloat16)
        for parity in range(2):
            part = first[parity * half : (parity + 1) * half]
            upper = slice(parity * npix, parity * npix + half)
            lower = slice(parity * npix + half, (parity + 1) * npix)
            if start < npix:
                both_ref[upper, start : start + chunk] = part
                both_ref[lower, npix + start : npix + start + chunk] = -part
            else:
                both_ref[upper, start : start + chunk] = -part
                both_ref[lower, start - npix : start - npix + chunk] = -part
    for load in loads[1 + len(starts) :]:
        load.wait()
    saves = []

    def save(start, size):
        at = pl.ds(start, size)
        copy = pltpu.make_async_copy(out_ref.at[:, at], out_hbm.at[:, at], out_sems.at[len(saves)])
        copy.start()
        saves.append(copy)

    lane = lax.broadcasted_iota(jnp.int32, (8, META), 1)
    codes = jnp.zeros((8, META), jnp.int32)
    for o in range(ori):
        label = orient_ref[0, o]
        codes = jnp.where(lane == o, label & 255, codes)
        codes = jnp.where(lane == ori + o, label >> 8, codes)
    about = codes.astype(jnp.float32)
    place = 2 * ori
    for scalar_ref in (defocus_ref, noise_ref):
        for part in three_parts(jnp.full((8, META), scalar_ref[0], jnp.float32)):
            about = jnp.where(lane == place, part, about)
            place += 1
    out_ref[:, 2 * npix :] = jnp.broadcast_to(about[:1], (npix, META)).astype(jnp.bfloat16)
    save(2 * npix, META)
    chunk = chunk // 2
    for start in range(0, 2 * npix, chunk):
        even, odd = (
            jnp.dot(
                halves_ref[:, parity * npix : (parity + 1) * npix],
                both_ref[parity * npix : (parity + 1) * npix, start : start + chunk],
                preferred_element_type=jnp.float32,
            )
            for parity in range(2)
        )
        out_ref[:half, start : start + chunk] = (even + odd).astype(jnp.bfloat16)
        out_ref[half:, start : start + chunk] = (even - odd).astype(jnp.bfloat16)
        save(start, chunk)
    for copy in saves:
        copy.wait()


def transform(orient, defocus, noise, image, table, halves):
    npix = image.shape[0]
    chunk = npix
    pieces = 2 * npix // chunk
    return pl.pallas_call(
        functools.partial(transform_kernel, chunk),
        in_specs=[pl.BlockSpec(memory_space=pl.ANY)] * 6,
        out_specs=pl.BlockSpec(memory_space=pl.ANY),
        out_shape=jax.ShapeDtypeStruct((npix, 2 * npix + META), jnp.bfloat16),
        scratch_shapes=[
            pltpu.SMEM(orient.shape, jnp.int32),
            pltpu.SMEM(defocus.shape, jnp.float32),
            pltpu.SMEM(noise.shape, jnp.float32),
            pltpu.VMEM((npix, npix), jnp.bfloat16),
            pltpu.VMEM((npix // 128, npix, 128), jnp.float32),
            pltpu.VMEM((npix, 2 * npix), jnp.bfloat16),
            pltpu.VMEM((npix // 2, 2 * npix), jnp.bfloat16),
            pltpu.VMEM((2 * npix, 2 * npix), jnp.bfloat16),
            pltpu.VMEM((npix, 2 * npix + META), jnp.bfloat16),
            pltpu.SemaphoreType.DMA((pieces + 5,)),
            pltpu.SemaphoreType.DMA((2 * pieces + 1,)),
        ],
        compiler_params=params(HUGE),
        cost_estimate=cost(12 * npix**3, 10 * npix * npix),
        name="transform",
    )(orient, defocus, noise, image, table, halves)


def prepare_kernel(planes_ref, weights_ref, lookup_ref):
    deep, labels = lookup_ref.shape
    rows = planes_ref.shape[1]
    level = lax.broadcasted_iota(jnp.int32, (deep // rows, rows, labels), 0)
    total = jnp.zeros((deep // rows, rows, labels), jnp.float32)
    for k in range(2):
        weight = weights_ref[k].astype(jnp.float32)
        total = total + jnp.where(level == planes_ref[k][None], weight[None], 0.0)
    lookup_ref[...] = total.reshape(deep, labels).astype(jnp.bfloat16)


def prepare(planes, weights, deep):
    labels = planes.shape[2]
    return pl.pallas_call(
        prepare_kernel,
        in_specs=[whole(), whole()],
        out_specs=whole(),
        out_shape=jax.ShapeDtypeStruct((deep, labels), jnp.bfloat16),
        compiler_params=params(SMALL),
        cost_estimate=cost(1 << 22, 1 << 20),
        name="prepare",
    )(planes, weights)


def contrast(defocus, row_square, start, width, npix):
    column = start + lax.broadcasted_iota(jnp.int32, (1, width), 1)
    freq_x = frequency(column, npix)
    chi = defocus * (row_square + freq_x * freq_x)
    turns = jnp.floor(chi * (1.0 / TURN) + (TILT / TURN + 0.5))
    angle = ((chi - turns * TURN_HIGH) - turns * TURN_LOW) + TILT
    square = angle * angle
    series = -SINE[-1]
    for term in SINE[-2::-1]:
        series = series * square - term
    return series * angle


def line_geometry(meta, ori, rows, many, npix, slot):
    place = 2 * ori
    defocus = meta[:, place : place + 1] + meta[:, place + 1 : place + 2] + meta[:, place + 2 : place + 3]
    index = (lax.broadcasted_iota(jnp.int32, (many, 1), 0) & (rows - 1)) + slot * rows
    freq_y = jnp.where(index < npix // 2, index, index - npix).astype(jnp.float32) / npix
    return defocus, freq_y * freq_y


def compare_kernel(ori, rows, slot_ref, fourier_ref, lookup_ref, volume_ref, filtered_ref, picks_ref, part_ref, about_ref, mix_ref, power_ref):
    many, wide = filtered_ref.shape
    npix = wide // 2
    deep = volume_ref.shape[0]
    images = many // rows

    meta = fourier_ref[:, wide:]
    here = lax.broadcasted_iota(jnp.int32, (images, many), 0) << bits(rows)
    there = lax.broadcasted_iota(jnp.int32, (images, many), 1)
    pick = jnp.where(here == there, 1.0, 0.0).astype(jnp.bfloat16)
    about = jnp.dot(pick, meta, preferred_element_type=jnp.float32)
    about_ref[...] = about
    label = lax.broadcasted_iota(jnp.int32, (images, lookup_ref.shape[1]), 1).astype(jnp.float32)
    found = []
    for o in range(ori):
        mine = about[:, o : o + 1] + 256.0 * about[:, ori + o : ori + o + 1]
        found.append(jnp.where(label == mine, 1.0, 0.0).astype(jnp.bfloat16))
    found = same(jnp.concatenate(found, 0), lookup_ref[...]).astype(jnp.bfloat16)
    picks_ref[...] = found
    spread = spread_over(rows, (many, images), 1)
    for o in range(ori):
        every = jnp.dot(
            spread, found[o * images : (o + 1) * images], preferred_element_type=jnp.float32
        )
        mix_ref[o * many : (o + 1) * many, :] = (
            own_row(every, rows).reshape(many, deep).astype(jnp.bfloat16)
        )
    defocus, row_square = line_geometry(meta.astype(jnp.float32), ori, rows, many, npix, slot_ref[0])
    def sections(start):
        planes = jnp.concatenate(
            [volume_ref[:, at : at + 128] for at in (start, npix + start)], 1
        )
        return [
            jnp.dot(
                mix_ref[o * many : (o + 1) * many, :], planes, preferred_element_type=jnp.float32
            )
            for o in range(ori)
        ]

    current = sections(0)
    for start in range(0, npix, 128):
        ctf = contrast(defocus, row_square, start, 128, npix)
        for at in (start, npix + start):
            filtered_ref[:, at : at + 128] = (
                ctf * fourier_ref[:, at : at + 128].astype(jnp.float32)
            ).astype(jnp.bfloat16)
        square = ctf * ctf
        following = sections(start + 128) if start + 128 < npix else None
        for o in range(ori):
            section = current[o] * current[o]
            power = square * (section[:, :128] + section[:, 128:])
            if start:
                power = power + power_ref[o]
            power_ref[o] = power
        current = following

    found = own_row(same(filtered_ref[...], volume_ref[...]), rows)
    found = jnp.sum(found, axis=1)
    halves = []
    for o in range(ori):
        cross = found * picks_ref[o * images : (o + 1) * images, :].astype(jnp.float32)
        lanes = cross[:, :128]
        for start in range(128, deep, 128):
            lanes = lanes + cross[:, start : start + 128]
        power = jnp.sum(power_ref[o].reshape(images, rows, 128), axis=1)
        halves.append(lanes - 0.5 * power)
    upper = jnp.concatenate(halves[: ori // 2], 0)
    lower = jnp.concatenate(halves[ori // 2 :], 0)
    upper = jnp.sum(jnp.transpose(upper), axis=0, keepdims=True)
    lower = jnp.sum(jnp.transpose(lower), axis=0, keepdims=True)
    even = (lax.broadcasted_iota(jnp.int32, part_ref.shape, 0) & 1) == 0
    part_ref[...] = jnp.where(even, upper, lower)


def compare(slot, fourier, lookup, volume, ori, rows, copies):
    many = fourier.shape[0]
    deep, wide = volume.shape
    images = many // rows
    return pl.pallas_call(
        functools.partial(compare_kernel, ori, rows),
        in_specs=[scalar()] + [whole()] * 3,
        out_specs=(whole(),) * 4,
        out_shape=(
            jax.ShapeDtypeStruct((many, wide), jnp.bfloat16),
            jax.ShapeDtypeStruct((ori * images, deep), jnp.bfloat16),
            jax.ShapeDtypeStruct((copies * 2, 2 * images), jnp.float32),
            jax.ShapeDtypeStruct((images, META), jnp.float32),
        ),
        scratch_shapes=[
            pltpu.VMEM((ori * many, deep), jnp.bfloat16),
            pltpu.VMEM((ori, many, 128), jnp.float32),
        ],
        compiler_params=params(LARGE),
        cost_estimate=cost(1 << 31, 5 << 20),
        name="compare",
    )(slot, fourier, lookup, volume)


def squares_kernel(ori, rows, npix, slot_ref, about_ref, square_ref, noise_ref):
    many = square_ref.shape[0]
    images = many // rows
    about = about_ref[...]
    meta = jnp.dot(
        spread_over(rows, (many, images), 1),
        about.astype(jnp.bfloat16),
        preferred_element_type=jnp.float32,
    )
    defocus, row_square = line_geometry(meta, ori, rows, many, npix, slot_ref[0])
    for start in range(0, square_ref.shape[1], 128):
        ctf = contrast(defocus, row_square, start, 128, npix)
        square_ref[:, start : start + 128] = (ctf * ctf).astype(jnp.bfloat16)
    place = 2 * ori + 3
    turned = jnp.transpose(jnp.concatenate([about, about], 0))
    noise_ref[...] = turned[place : place + 1] + turned[place + 1 : place + 2] + turned[place + 2 : place + 3]


def squares(slot, about, ori, rows, npix):
    images = about.shape[0]
    return pl.pallas_call(
        functools.partial(squares_kernel, ori, rows, npix),
        in_specs=[scalar(), whole()],
        out_specs=(whole(), whole()),
        out_shape=(
            jax.ShapeDtypeStruct((images * rows, npix // 2 + 128), jnp.bfloat16),
            jax.ShapeDtypeStruct((1, 2 * images), jnp.float32),
        ),
        compiler_params=params(SMALL),
        cost_estimate=cost(1 << 27, 1 << 20),
        name="squares",
    )(slot, about)


def pack(target_ref, share, source_ref, start, last):
    pairs = target_ref.shape[0]
    slab = share.shape[0] // pairs
    sums = jnp.dot(share, source_ref[...], preferred_element_type=jnp.float32)
    for number in range(sums.shape[1] // 128):
        value = sums[:, number * 128 : (number + 1) * 128].reshape(pairs, slab, 128)
        at = (start + number) * slab
        if start + number < last:
            target_ref[:, at : at + slab, :] = value.astype(jnp.bfloat16)
        else:
            lane = lax.broadcasted_iota(jnp.int32, (pairs, slab // 2, 128), 2)
            lower = jnp.broadcast_to(value[:, slab // 2 :, :1], lane.shape)
            value = jnp.where(lane == 0, value[:, : slab // 2], lower)
            target_ref[:, at : at + slab // 2, :] = value.astype(jnp.bfloat16)


def pack_both(target_ref, share, filtered_ref, square_ref):
    tiles = filtered_ref.shape[1] // 128
    last = tiles + square_ref.shape[1] // 128 - 1
    pack(target_ref, share, filtered_ref, 0, last)
    pack(target_ref, share, square_ref, tiles, last)


def project_kernel(rows, ori, core_ref, part_ref, noise_ref, picks_ref, filtered_ref, square_ref, probs_ref, share_ref, send_ref):
    many = filtered_ref.shape[0]
    deep = picks_ref.shape[1]
    lanes = part_ref.shape[1]
    images = lanes // 2
    sums = jnp.sum(part_ref[...].reshape(part_ref.shape[0] // 8, 8, lanes), axis=0)
    sums = sums + pltpu.roll(sums, 4, 0)
    sums = sums + pltpu.roll(sums, 2, 0)
    score = sums / noise_ref[...]
    top = jnp.maximum(score, pltpu.roll(score, 1, 0))
    top = jnp.maximum(top, pltpu.roll(top, images, 1))
    power = jnp.exp(score - top)
    total = power + pltpu.roll(power, 1, 0)
    total = total + pltpu.roll(total, images, 1)
    probs = power / total
    probs_ref[...] = probs
    column = jnp.transpose(jnp.concatenate([probs] * (lanes // 8), 0))
    share = jnp.zeros((images, deep), jnp.float32)
    for o in range(ori):
        half = o % 2
        chance = column[half * images : (half + 1) * images, o // 2 : o // 2 + 1]
        share = share + chance * picks_ref[o * images : (o + 1) * images, :].astype(jnp.float32)
    share = jnp.dot(
        jnp.transpose(share).astype(jnp.bfloat16),
        spread_over(rows, (images, many), 0),
        preferred_element_type=jnp.float32,
    )
    pairs = send_ref.shape[0]
    share = own_row(share, rows).reshape(pairs, 2, deep // (2 * pairs), many)
    first = core_ref[0] == 0
    ours = jnp.where(first, share[:, 0], share[:, 1]).reshape(deep // 2, many)
    theirs = jnp.where(first, share[:, 1], share[:, 0]).reshape(deep // 2, many)
    share_ref[...] = ours.astype(jnp.bfloat16)
    pack_both(send_ref, theirs.astype(jnp.bfloat16), filtered_ref, square_ref)


def packed(deep, filtered, square, pairs):
    slab = deep // (2 * pairs)
    lines = (filtered.shape[1] + square.shape[1]) // 128 * slab - slab // 2
    return jax.ShapeDtypeStruct((pairs, lines, 128), jnp.bfloat16)


def project(core, part, noise, picks, filtered, square, rows, ori, pairs):
    many = filtered.shape[0]
    deep = picks.shape[1]
    return pl.pallas_call(
        functools.partial(project_kernel, rows, ori),
        in_specs=[scalar()] + [whole()] * 5,
        out_specs=(whole(), whole(), whole()),
        out_shape=(
            jax.ShapeDtypeStruct((8, part.shape[1]), jnp.float32),
            jax.ShapeDtypeStruct((deep // 2, many), jnp.bfloat16),
            packed(deep, filtered, square, pairs),
        ),
        compiler_params=params(LARGE),
        cost_estimate=cost(1 << 28, 4 << 20),
        name="project",
    )(core, part, noise, picks, filtered, square)


def keep_kernel(share_ref, filtered_ref, square_ref, keep_ref):
    pack_both(keep_ref, share_ref[...], filtered_ref, square_ref)


def keep_own(share, filtered, square, pairs):
    return pl.pallas_call(
        keep_kernel,
        out_shape=packed(2 * share.shape[0], filtered, square, pairs),
        compiler_params=params(SMALL),
        cost_estimate=cost(1 << 28, 2 << 20),
        name="keep_own",
    )(share, filtered, square)


def middle_kernel(high_ref, keep_ref, got_ref, own_ref, *send_refs):
    pairs = keep_ref.shape[0]
    for apart in range(pairs):
        at = high_ref[0] ^ apart
        total = keep_ref[at].astype(jnp.float32) + got_ref[at].astype(jnp.float32)
        if apart == 0:
            own_ref[...] = total
        else:
            send_refs[apart - 1][...] = total.astype(jnp.bfloat16)


def middle(high, keep, got):
    pairs, slab, wide = keep.shape
    return pl.pallas_call(
        middle_kernel,
        in_specs=[scalar(), whole(), whole()],
        out_specs=(whole(),) * pairs,
        out_shape=(jax.ShapeDtypeStruct((slab, wide), jnp.float32),)
        + (jax.ShapeDtypeStruct((slab, wide), jnp.bfloat16),) * (pairs - 1),
        compiler_params=params(SMALL),
        cost_estimate=cost(1 << 20, 2 << 20),
        name="middle",
    )(high, keep, got)


def mirror_columns(lower, last, precision=None):
    slab, half = lower.shape
    source = lax.broadcasted_iota(jnp.int32, (half, half), 0)
    target = lax.broadcasted_iota(jnp.int32, (half, half), 1)
    mirror = jnp.where(source + target == half, 1.0, 0.0).astype(lower.dtype)
    upper = jnp.dot(lower, mirror, preferred_element_type=jnp.float32, precision=precision)
    lane = lax.broadcasted_iota(jnp.int32, (slab, half), 1)
    return jnp.where(lane == 0, last, upper)


def spread_lines(lines, slab, npix):
    tiles = [lines[at : at + slab] for at in range(0, lines.shape[0] - slab // 2, slab)]
    last = lines[lines.shape[0] - slab // 2 :].astype(jnp.float32)
    last = jnp.concatenate([last[:, :1], last[:, 1:2]], 0)
    count = 2 * npix // 128
    return jnp.concatenate(tiles[:count], 1), jnp.concatenate(tiles[count:], 1), last


def collect_kernel(own_ref, data_ref, weight_ref, data_out, weight_out):
    slab, npix = weight_ref.shape
    half = npix // 2
    data, lower, last = spread_lines(own_ref[...], slab, npix)
    data_out[...] = data_ref[...] + data
    weight_out[:, :half] = weight_ref[:, :half] + lower
    weight_out[:, half:] = weight_ref[:, half:] + mirror_columns(
        lower, last, lax.Precision.HIGHEST
    )


def finish_kernel(*refs):
    *part_refs, data_ref, weight_ref, data_out, weight_out = refs
    slab, npix = weight_ref.shape
    half = npix // 2
    data = data_ref[...]
    weight = weight_ref[:, :half]
    lowers, lasts = [], []
    for part_ref in part_refs:
        part, lower, last = spread_lines(part_ref[...], slab, npix)
        data = data + part.astype(jnp.float32)
        weight = weight + lower.astype(jnp.float32)
        lowers.append(lower)
        lasts.append(last)
    uppers = mirror_columns(jnp.concatenate(lowers, 0), jnp.concatenate(lasts, 0))
    upper = weight_ref[:, half:]
    for number in range(len(part_refs)):
        upper = upper + uppers[number * slab : (number + 1) * slab]
    data_out[...] = data
    weight_out[:, :half] = weight
    weight_out[:, half:] = upper


def add_lines(kernel, name, lines, data, weight):
    return pl.pallas_call(
        kernel,
        out_shape=(
            jax.ShapeDtypeStruct(data.shape, jnp.float32),
            jax.ShapeDtypeStruct(weight.shape, jnp.float32),
        ),
        compiler_params=params(SMALL),
        cost_estimate=cost(1 << 20, 2 << 20),
        name=name,
    )(*lines, data, weight)


def on_device(images, defocus, noise, orient, planes, weights, volume, data_old, weight_old):
    npix = images.shape[1]
    ori = orient.shape[1]
    n_img = lax.axis_size("img")
    n_vol = lax.axis_size("vol")
    rows = npix // n_img
    slab = volume.shape[0]
    deep = n_vol * slab * rows
    many = n_img * rows
    pairs = n_vol // 2
    slot = lax.axis_index("img").astype(jnp.int32).reshape(1)
    place = lax.axis_index("vol").astype(jnp.int32)

    fourier = transform(orient, defocus, noise, images[0], *dft_tables(npix))
    fourier = lax.all_to_all(
        fourier.reshape(n_img, rows, 2 * npix + META), "img", split_axis=0, concat_axis=0, tiled=True
    ).reshape(many, 2 * npix + META)
    vol_rows = lax.all_gather(volume.reshape(slab * rows, 2 * npix), "vol", axis=0, tiled=True)
    lookup = prepare(jnp.swapaxes(planes, 1, 2), jnp.swapaxes(weights, 1, 2), deep)
    filtered, picks, part, about = compare(slot, fourier, lookup, vol_rows, ori, rows, n_img)
    square, noise_all = squares(slot, about, ori, rows, npix)
    part = lax.all_to_all(
        part.reshape(n_img, 2, 2 * n_img), "img", split_axis=0, concat_axis=0, tiled=True
    ).reshape(2 * n_img, 2 * n_img)
    probs, share, send = project(
        (place % 2).reshape(1), part, noise_all, picks, filtered, square, rows, ori, pairs
    )
    mine = lax.dynamic_slice_in_dim(
        probs[:2].reshape(2 * 2, n_img), lax.axis_index("img"), 1, 1
    ).reshape(1, ori)
    got = lax.ppermute(send, "vol", [(v, v ^ 1) for v in range(n_vol)])
    keep = keep_own(share, filtered, square, pairs)
    own, *sends = middle((place // 2).reshape(1), keep, got)
    parts = [
        lax.ppermute(sends[apart - 1], "vol", [(v, v ^ (2 * apart)) for v in range(n_vol)])
        for apart in (2, 3, 1)
    ]
    data, weight = add_lines(
        collect_kernel,
        "collect",
        [own],
        data_old.reshape(slab * rows, 2 * npix),
        weight_old.reshape(slab * rows, npix),
    )
    data, weight = add_lines(finish_kernel, "finish", parts, data, weight)
    return (mine, data.reshape(data_old.shape), weight.reshape(weight_old.shape))


def solution(mesh):
    placed = (
        P(("img", "vol"), None, None),
        P(("img", "vol")),
        P(("img", "vol")),
        P(("img", "vol"), None),
        P(None, None, "img"),
        P(None, None, "img"),
        P("vol", "img", None),
        P("vol", "img", None),
        P("vol", "img", None),
    )
    return jax.shard_map(
        on_device,
        mesh=mesh,
        in_specs=placed,
        out_specs=(P(("img", "vol"), None), P("vol", "img", None), P("vol", "img", None)),
        check_vma=False,
    )
```

```python
import functools
import math

import jax
import jax.numpy as jnp
import ml_dtypes
import numpy as np
from jax import lax
from jax.experimental import pallas as pl
from jax.experimental.pallas import tpu as pltpu
from jax.sharding import PartitionSpec as P

AMP = 0.1
TILT = math.asin(AMP)
TURN = 2.0 * math.pi
TURN_HIGH = math.floor(TURN * 4096) / 4096
TURN_LOW = TURN - TURN_HIGH
SINE = tuple(
    factor / TURN ** (2 * power + 1)
    for power, factor in enumerate(
        (
            6.283185272722434,
            -41.341697068956265,
            81.60502462257806,
            -76.70155117622761,
            42.01616582127327,
            -14.868610992503873,
            3.199693654235983,
        )
    )
)
HUGE = 56 * 1024 * 1024
LARGE = 32 * 1024 * 1024
SMALL = 16 * 1024 * 1024
META = 128


def dft_tables(npix):
    index = np.arange(npix)
    angle = (index[:, None] * index[None, :] % npix) * (2.0 * math.pi / npix)
    scale = 1.0 / math.sqrt(npix)
    parts = [np.cos(angle) * scale, np.sin(angle) * scale]
    halves = [part[: npix // 2, parity::2] for parity in range(2) for part in parts]
    return tuple(
        jnp.asarray(np.concatenate(table, 1).astype(np.float32).astype(ml_dtypes.bfloat16))
        for table in (parts, halves)
    )


def frequency(index, npix):
    return ((index + npix // 2) % npix - npix // 2).astype(jnp.float32) / npix


def params(size):
    return pltpu.CompilerParams(vmem_limit_bytes=size)


def cost(flops, size):
    return pl.CostEstimate(flops=flops, bytes_accessed=size, transcendentals=0)


def whole():
    return pl.BlockSpec(memory_space=pltpu.VMEM)


def scalar():
    return pl.BlockSpec(memory_space=pltpu.SMEM)


def same(a, b):
    return lax.dot_general(a, b, (((1,), (1,)), ((), ())), preferred_element_type=jnp.float32)


def three_parts(value):
    parts = []
    for _ in range(3):
        part = value.astype(jnp.bfloat16).astype(jnp.float32)
        parts.append(part)
        value = value - part
    return parts


def bits(rows):
    assert rows & (rows - 1) == 0
    return rows.bit_length() - 1


def spread_over(rows, shape, image_axis):
    image = lax.broadcasted_iota(jnp.int32, shape, image_axis)
    owner = lax.broadcasted_iota(jnp.int32, shape, 1 - image_axis) >> bits(rows)
    return jnp.where(owner == image, 1.0, 0.0).astype(jnp.bfloat16)


def own_row(values, rows):
    height, width = values.shape
    sublane = lax.broadcasted_iota(jnp.int32, (rows, width), 0)
    lane = lax.broadcasted_iota(jnp.int32, (rows, width), 1) & (rows - 1)
    return jnp.where((sublane == lane)[None], values.reshape(height // rows, rows, width), 0.0)


def transform_kernel(chunk, orient_hbm, defocus_hbm, image_hbm, table_hbm, halves_hbm, out_hbm, orient_ref, defocus_ref, image_ref, wide_ref, table_ref, halves_ref, both_ref, out_ref, in_sems, out_sems):
    npix = image_ref.shape[0]
    half = npix // 2
    ori = orient_ref.shape[1]
    starts = list(range(0, 2 * npix, chunk))
    pairs = [(image_hbm, image_ref)]
    pairs += [(table_hbm.at[:, pl.ds(start, chunk)], table_ref.at[:, pl.ds(start, chunk)]) for start in starts]
    pairs += [(halves_hbm, halves_ref), (orient_hbm, orient_ref), (defocus_hbm, defocus_ref)]
    loads = []
    for number, (source, target) in enumerate(pairs):
        load = pltpu.make_async_copy(source, target, in_sems.at[number])
        load.start()
        loads.append(load)
    loads[0].wait()
    tiles = range(npix // 128)
    for tile in tiles:
        wide_ref[tile] = image_ref[:, tile * 128 : (tile + 1) * 128].astype(jnp.float32)
    image = jnp.concatenate(
        [
            jnp.concatenate([wide_ref[tile, pl.ds(parity, half, 2), :] for tile in tiles], 1)
            for parity in range(2)
        ],
        0,
    ).astype(jnp.bfloat16)
    for number, start in enumerate(starts):
        loads[1 + number].wait()
        first = jnp.dot(
            image, table_ref[:, start : start + chunk], preferred_element_type=jnp.float32
        ).astype(jnp.bfloat16)
        for parity in range(2):
            part = first[parity * half : (parity + 1) * half]
            upper = slice(parity * npix, parity * npix + half)
            lower = slice(parity * npix + half, (parity + 1) * npix)
            if start < npix:
                both_ref[upper, start : start + chunk] = part
                both_ref[lower, npix + start : npix + start + chunk] = -part
            else:
                both_ref[upper, start : start + chunk] = -part
                both_ref[lower, start - npix : start - npix + chunk] = -part
    for load in loads[1 + len(starts) :]:
        load.wait()
    saves = []

    def save(start, size):
        at = pl.ds(start, size)
        copy = pltpu.make_async_copy(out_ref.at[:, at], out_hbm.at[:, at], out_sems.at[len(saves)])
        copy.start()
        saves.append(copy)

    lane = lax.broadcasted_iota(jnp.int32, (8, META), 1)
    codes = jnp.zeros((8, META), jnp.int32)
    for o in range(ori):
        label = orient_ref[0, o]
        codes = jnp.where(lane == o, label & 255, codes)
        codes = jnp.where(lane == ori + o, label >> 8, codes)
    about = codes.astype(jnp.float32)
    parts = three_parts(jnp.full((8, META), defocus_ref[0], jnp.float32))
    for place, part in enumerate(parts, 2 * ori):
        about = jnp.where(lane == place, part, about)
    out_ref[:, 2 * npix :] = jnp.broadcast_to(about[:1], (npix, META)).astype(jnp.bfloat16)
    save(2 * npix, META)
    chunk = chunk // 2
    for start in range(0, 2 * npix, chunk):
        even, odd = (
            jnp.dot(
                halves_ref[:, parity * npix : (parity + 1) * npix],
                both_ref[parity * npix : (parity + 1) * npix, start : start + chunk],
                preferred_element_type=jnp.float32,
            )
            for parity in range(2)
        )
        out_ref[:half, start : start + chunk] = (even + odd).astype(jnp.bfloat16)
        out_ref[half:, start : start + chunk] = (even - odd).astype(jnp.bfloat16)
        save(start, chunk)
    for copy in saves:
        copy.wait()


def transform(orient, defocus, image, table, halves):
    npix = image.shape[0]
    chunk = npix
    pieces = 2 * npix // chunk
    return pl.pallas_call(
        functools.partial(transform_kernel, chunk),
        in_specs=[pl.BlockSpec(memory_space=pl.ANY)] * 5,
        out_specs=pl.BlockSpec(memory_space=pl.ANY),
        out_shape=jax.ShapeDtypeStruct((npix, 2 * npix + META), jnp.bfloat16),
        scratch_shapes=[
            pltpu.SMEM(orient.shape, jnp.int32),
            pltpu.SMEM(defocus.shape, jnp.float32),
            pltpu.VMEM((npix, npix), jnp.bfloat16),
            pltpu.VMEM((npix // 128, npix, 128), jnp.float32),
            pltpu.VMEM((npix, 2 * npix), jnp.bfloat16),
            pltpu.VMEM((npix // 2, 2 * npix), jnp.bfloat16),
            pltpu.VMEM((2 * npix, 2 * npix), jnp.bfloat16),
            pltpu.VMEM((npix, 2 * npix + META), jnp.bfloat16),
            pltpu.SemaphoreType.DMA((pieces + 4,)),
            pltpu.SemaphoreType.DMA((2 * pieces + 1,)),
        ],
        compiler_params=params(HUGE),
        cost_estimate=cost(12 * npix**3, 10 * npix * npix),
        name="transform",
    )(orient, defocus, image, table, halves)


def prepare_kernel(planes_ref, weights_ref, lookup_ref):
    deep, labels = lookup_ref.shape
    rows = planes_ref.shape[1]
    level = lax.broadcasted_iota(jnp.int32, (deep // rows, rows, labels), 0)
    total = jnp.zeros((deep // rows, rows, labels), jnp.float32)
    for k in range(2):
        weight = weights_ref[k].astype(jnp.float32)
        total = total + jnp.where(level == planes_ref[k][None], weight[None], 0.0)
    lookup_ref[...] = total.reshape(deep, labels).astype(jnp.bfloat16)


def prepare(planes, weights, deep):
    labels = planes.shape[2]
    return pl.pallas_call(
        prepare_kernel,
        in_specs=[whole(), whole()],
        out_specs=whole(),
        out_shape=jax.ShapeDtypeStruct((deep, labels), jnp.bfloat16),
        compiler_params=params(SMALL),
        cost_estimate=cost(1 << 22, 1 << 20),
        name="prepare",
    )(planes, weights)


def contrast(defocus, row_square, start, width, npix):
    column = start + lax.broadcasted_iota(jnp.int32, (1, width), 1)
    freq_x = frequency(column, npix)
    chi = defocus * (row_square + freq_x * freq_x)
    turns = jnp.floor(chi * (1.0 / TURN) + (TILT / TURN + 0.5))
    angle = ((chi - turns * TURN_HIGH) - turns * TURN_LOW) + TILT
    square = angle * angle
    series = -SINE[-1]
    for term in SINE[-2::-1]:
        series = series * square - term
    return series * angle


def line_geometry(meta, ori, rows, many, npix, slot):
    place = 2 * ori
    defocus = meta[:, place : place + 1] + meta[:, place + 1 : place + 2] + meta[:, place + 2 : place + 3]
    index = (lax.broadcasted_iota(jnp.int32, (many, 1), 0) & (rows - 1)) + slot * rows
    freq_y = jnp.where(index < npix // 2, index, index - npix).astype(jnp.float32) / npix
    return defocus, freq_y * freq_y


def compare_kernel(ori, rows, slot_ref, noise_ref, fourier_ref, lookup_ref, volume_ref, filtered_ref, picks_ref, part_ref, about_ref, mix_ref, power_ref):
    many, wide = filtered_ref.shape
    npix = wide // 2
    deep = volume_ref.shape[0]
    images = many // rows

    meta = fourier_ref[:, wide:]
    here = lax.broadcasted_iota(jnp.int32, (images, many), 0) << bits(rows)
    there = lax.broadcasted_iota(jnp.int32, (images, many), 1)
    pick = jnp.where(here == there, 1.0, 0.0).astype(jnp.bfloat16)
    about = jnp.dot(pick, meta, preferred_element_type=jnp.float32)
    about_ref[...] = about
    label = lax.broadcasted_iota(jnp.int32, (images, lookup_ref.shape[1]), 1).astype(jnp.float32)
    found = []
    for o in range(ori):
        mine = about[:, o : o + 1] + 256.0 * about[:, ori + o : ori + o + 1]
        found.append(jnp.where(label == mine, 1.0, 0.0).astype(jnp.bfloat16))
    found = same(jnp.concatenate(found, 0), lookup_ref[...]).astype(jnp.bfloat16)
    picks_ref[...] = found
    spread = spread_over(rows, (many, images), 1)
    for o in range(ori):
        every = jnp.dot(
            spread, found[o * images : (o + 1) * images], preferred_element_type=jnp.float32
        )
        mix_ref[o * many : (o + 1) * many, :] = (
            own_row(every, rows).reshape(many, deep).astype(jnp.bfloat16)
        )
    defocus, row_square = line_geometry(meta.astype(jnp.float32), ori, rows, many, npix, slot_ref[0])
    def sections(start):
        planes = jnp.concatenate(
            [volume_ref[:, at : at + 128] for at in (start, npix + start)], 1
        )
        return [
            jnp.dot(
                mix_ref[o * many : (o + 1) * many, :], planes, preferred_element_type=jnp.float32
            )
            for o in range(ori)
        ]

    current = sections(0)
    for start in range(0, npix, 128):
        ctf = contrast(defocus, row_square, start, 128, npix)
        for at in (start, npix + start):
            filtered_ref[:, at : at + 128] = (
                ctf * fourier_ref[:, at : at + 128].astype(jnp.float32)
            ).astype(jnp.bfloat16)
        square = ctf * ctf
        following = sections(start + 128) if start + 128 < npix else None
        for o in range(ori):
            section = current[o] * current[o]
            power = square * (section[:, :128] + section[:, 128:])
            if start:
                power = power + power_ref[o]
            power_ref[o] = power
        current = following

    found = own_row(same(filtered_ref[...], volume_ref[...]), rows)
    found = jnp.sum(found, axis=1)
    halves = []
    for o in range(ori):
        cross = found * picks_ref[o * images : (o + 1) * images, :].astype(jnp.float32)
        lanes = cross[:, :128]
        for start in range(128, deep, 128):
            lanes = lanes + cross[:, start : start + 128]
        power = jnp.sum(power_ref[o].reshape(images, rows, 128), axis=1)
        halves.append(lanes - 0.5 * power)
    lane = lax.broadcasted_iota(jnp.int32, (images, 128), 1)
    image = lax.broadcasted_iota(jnp.int32, (images, 128), 0)
    noise = jnp.where((image == slot_ref[0]) & (lane == 0), noise_ref[0], 0.0)
    halves = [part - halves[0] for part in halves[1:]] + [noise]
    upper = jnp.concatenate(halves[: ori // 2], 0)
    lower = jnp.concatenate(halves[ori // 2 :], 0)
    upper = jnp.sum(jnp.transpose(upper), axis=0, keepdims=True)
    lower = jnp.sum(jnp.transpose(lower), axis=0, keepdims=True)
    even = (lax.broadcasted_iota(jnp.int32, part_ref.shape, 0) & 1) == 0
    part_ref[...] = jnp.where(even, upper, lower)


def compare(slot, noise, fourier, lookup, volume, ori, rows, copies):
    many = fourier.shape[0]
    deep, wide = volume.shape
    images = many // rows
    return pl.pallas_call(
        functools.partial(compare_kernel, ori, rows),
        in_specs=[scalar()] * 2 + [whole()] * 3,
        out_specs=(whole(),) * 4,
        out_shape=(
            jax.ShapeDtypeStruct((many, wide), jnp.bfloat16),
            jax.ShapeDtypeStruct((ori * images, deep), jnp.bfloat16),
            jax.ShapeDtypeStruct((copies * 2, 2 * images), jnp.float32),
            jax.ShapeDtypeStruct((images, META), jnp.float32),
        ),
        scratch_shapes=[
            pltpu.VMEM((ori * many, deep), jnp.bfloat16),
            pltpu.VMEM((ori, many, 128), jnp.float32),
        ],
        compiler_params=params(LARGE),
        cost_estimate=cost(1 << 31, 5 << 20),
        name="compare",
    )(slot, noise, fourier, lookup, volume)


def squares_kernel(ori, rows, npix, slot_ref, about_ref, square_ref):
    many = square_ref.shape[0]
    images = many // rows
    about = about_ref[...]
    meta = jnp.dot(
        spread_over(rows, (many, images), 1),
        about.astype(jnp.bfloat16),
        preferred_element_type=jnp.float32,
    )
    defocus, row_square = line_geometry(meta, ori, rows, many, npix, slot_ref[0])
    for start in range(0, square_ref.shape[1], 128):
        ctf = contrast(defocus, row_square, start, 128, npix)
        square_ref[:, start : start + 128] = (ctf * ctf).astype(jnp.bfloat16)


def squares(slot, about, ori, rows, npix):
    images = about.shape[0]
    return pl.pallas_call(
        functools.partial(squares_kernel, ori, rows, npix),
        in_specs=[scalar(), whole()],
        out_specs=whole(),
        out_shape=jax.ShapeDtypeStruct((images * rows, npix // 2 + 128), jnp.bfloat16),
        compiler_params=params(SMALL),
        cost_estimate=cost(1 << 27, 1 << 20),
        name="squares",
    )(slot, about)


def pack(target_ref, share, source_ref, start, last):
    pairs = target_ref.shape[0]
    slab = share.shape[0] // pairs
    sums = jnp.dot(share, source_ref[...], preferred_element_type=jnp.float32)
    for number in range(sums.shape[1] // 128):
        value = sums[:, number * 128 : (number + 1) * 128].reshape(pairs, slab, 128)
        at = (start + number) * slab
        if start + number < last:
            target_ref[:, at : at + slab, :] = value.astype(jnp.bfloat16)
        else:
            lane = lax.broadcasted_iota(jnp.int32, (pairs, slab // 2, 128), 2)
            lower = jnp.broadcast_to(value[:, slab // 2 :, :1], lane.shape)
            value = jnp.where(lane == 0, value[:, : slab // 2], lower)
            target_ref[:, at : at + slab // 2, :] = value.astype(jnp.bfloat16)


def pack_both(target_ref, share, filtered_ref, square_ref):
    tiles = filtered_ref.shape[1] // 128
    last = tiles + square_ref.shape[1] // 128 - 1
    pack(target_ref, share, filtered_ref, 0, last)
    pack(target_ref, share, square_ref, tiles, last)


def project_kernel(rows, ori, core_ref, part_ref, picks_ref, filtered_ref, square_ref, probs_ref, share_ref, send_ref):
    many = filtered_ref.shape[0]
    deep = picks_ref.shape[1]
    lanes = part_ref.shape[1]
    images = lanes // 2
    sums = jnp.sum(part_ref[...].reshape(part_ref.shape[0] // 8, 8, lanes), axis=0)
    sums = sums + pltpu.roll(sums, 4, 0)
    sums = sums + pltpu.roll(sums, 2, 0)
    line = lax.broadcasted_iota(jnp.int32, sums.shape, 0) & 1
    lane = lax.broadcasted_iota(jnp.int32, sums.shape, 1)
    noise = jnp.where(line == 1, sums, pltpu.roll(sums, 1, 0))
    noise = jnp.where(lane >= images, noise, pltpu.roll(noise, images, 1))
    score = jnp.where((line == 1) & (lane >= images), 0.0, sums / noise)
    top = jnp.maximum(score, pltpu.roll(score, 1, 0))
    top = jnp.maximum(top, pltpu.roll(top, images, 1))
    power = jnp.exp(score - top)
    total = power + pltpu.roll(power, 1, 0)
    total = total + pltpu.roll(total, images, 1)
    probs = power / total
    probs_ref[...] = probs
    column = jnp.transpose(jnp.concatenate([probs] * (lanes // 8), 0))
    share = jnp.zeros((images, deep), jnp.float32)
    for o in range(ori):
        place = (o - 1) % ori
        half, line = place % 2, place // 2
        chance = column[half * images : (half + 1) * images, line : line + 1]
        share = share + chance * picks_ref[o * images : (o + 1) * images, :].astype(jnp.float32)
    share = jnp.dot(
        jnp.transpose(share).astype(jnp.bfloat16),
        spread_over(rows, (images, many), 0),
        preferred_element_type=jnp.float32,
    )
    pairs = send_ref.shape[0]
    share = own_row(share, rows).reshape(pairs, 2, deep // (2 * pairs), many)
    first = core_ref[0] == 0
    ours = jnp.where(first, share[:, 0], share[:, 1]).reshape(deep // 2, many)
    theirs = jnp.where(first, share[:, 1], share[:, 0]).reshape(deep // 2, many)
    share_ref[...] = ours.astype(jnp.bfloat16)
    pack_both(send_ref, theirs.astype(jnp.bfloat16), filtered_ref, square_ref)


def packed(deep, filtered, square, pairs):
    slab = deep // (2 * pairs)
    lines = (filtered.shape[1] + square.shape[1]) // 128 * slab - slab // 2
    return jax.ShapeDtypeStruct((pairs, lines, 128), jnp.bfloat16)


def project(core, part, picks, filtered, square, rows, ori, pairs):
    many = filtered.shape[0]
    deep = picks.shape[1]
    return pl.pallas_call(
        functools.partial(project_kernel, rows, ori),
        in_specs=[scalar()] + [whole()] * 4,
        out_specs=(whole(), whole(), whole()),
        out_shape=(
            jax.ShapeDtypeStruct((8, part.shape[1]), jnp.float32),
            jax.ShapeDtypeStruct((deep // 2, many), jnp.bfloat16),
            packed(deep, filtered, square, pairs),
        ),
        compiler_params=params(LARGE),
        cost_estimate=cost(1 << 28, 4 << 20),
        name="project",
    )(core, part, picks, filtered, square)


def keep_kernel(share_ref, filtered_ref, square_ref, keep_ref):
    pack_both(keep_ref, share_ref[...], filtered_ref, square_ref)


def keep_own(share, filtered, square, pairs):
    return pl.pallas_call(
        keep_kernel,
        out_shape=packed(2 * share.shape[0], filtered, square, pairs),
        compiler_params=params(SMALL),
        cost_estimate=cost(1 << 28, 2 << 20),
        name="keep_own",
    )(share, filtered, square)


def middle_kernel(high_ref, keep_ref, got_ref, own_ref, *send_refs):
    pairs = keep_ref.shape[0]
    for apart in range(pairs):
        at = high_ref[0] ^ apart
        total = keep_ref[at].astype(jnp.float32) + got_ref[at].astype(jnp.float32)
        if apart == 0:
            own_ref[...] = total
        else:
            send_refs[apart - 1][...] = total.astype(jnp.bfloat16)


def middle(high, keep, got):
    pairs, slab, wide = keep.shape
    return pl.pallas_call(
        middle_kernel,
        in_specs=[scalar(), whole(), whole()],
        out_specs=(whole(),) * pairs,
        out_shape=(jax.ShapeDtypeStruct((slab, wide), jnp.float32),)
        + (jax.ShapeDtypeStruct((slab, wide), jnp.bfloat16),) * (pairs - 1),
        compiler_params=params(SMALL),
        cost_estimate=cost(1 << 20, 2 << 20),
        name="middle",
    )(high, keep, got)


def mirror_columns(lower, last, precision=None):
    slab, half = lower.shape
    source = lax.broadcasted_iota(jnp.int32, (half, half), 0)
    target = lax.broadcasted_iota(jnp.int32, (half, half), 1)
    mirror = jnp.where(source + target == half, 1.0, 0.0).astype(lower.dtype)
    upper = jnp.dot(lower, mirror, preferred_element_type=jnp.float32, precision=precision)
    lane = lax.broadcasted_iota(jnp.int32, (slab, half), 1)
    return jnp.where(lane == 0, last, upper)


def spread_lines(lines, slab, npix):
    tiles = [lines[at : at + slab] for at in range(0, lines.shape[0] - slab // 2, slab)]
    last = lines[lines.shape[0] - slab // 2 :].astype(jnp.float32)
    last = jnp.concatenate([last[:, :1], last[:, 1:2]], 0)
    count = 2 * npix // 128
    return jnp.concatenate(tiles[:count], 1), jnp.concatenate(tiles[count:], 1), last


def collect_kernel(own_ref, data_ref, weight_ref, data_out, weight_out):
    slab, npix = weight_ref.shape
    half = npix // 2
    data, lower, last = spread_lines(own_ref[...], slab, npix)
    data_out[...] = data_ref[...] + data
    weight_out[:, :half] = weight_ref[:, :half] + lower
    weight_out[:, half:] = weight_ref[:, half:] + mirror_columns(
        lower, last, lax.Precision.HIGHEST
    )


def finish_kernel(*refs):
    *part_refs, data_ref, weight_ref, data_out, weight_out = refs
    slab, npix = weight_ref.shape
    half = npix // 2
    data = data_ref[...]
    weight = weight_ref[:, :half]
    lowers, lasts = [], []
    for part_ref in part_refs:
        part, lower, last = spread_lines(part_ref[...], slab, npix)
        data = data + part.astype(jnp.float32)
        weight = weight + lower.astype(jnp.float32)
        lowers.append(lower)
        lasts.append(last)
    uppers = mirror_columns(jnp.concatenate(lowers, 0), jnp.concatenate(lasts, 0))
    upper = weight_ref[:, half:]
    for number in range(len(part_refs)):
        upper = upper + uppers[number * slab : (number + 1) * slab]
    data_out[...] = data
    weight_out[:, :half] = weight
    weight_out[:, half:] = upper


def add_lines(kernel, name, lines, data, weight):
    return pl.pallas_call(
        kernel,
        out_shape=(
            jax.ShapeDtypeStruct(data.shape, jnp.float32),
            jax.ShapeDtypeStruct(weight.shape, jnp.float32),
        ),
        compiler_params=params(SMALL),
        cost_estimate=cost(1 << 20, 2 << 20),
        name=name,
    )(*lines, data, weight)


def on_device(images, defocus, noise, orient, planes, weights, volume, data_old, weight_old):
    npix = images.shape[1]
    ori = orient.shape[1]
    n_img = lax.axis_size("img")
    n_vol = lax.axis_size("vol")
    rows = npix // n_img
    slab = volume.shape[0]
    deep = n_vol * slab * rows
    many = n_img * rows
    pairs = n_vol // 2
    slot = lax.axis_index("img").astype(jnp.int32).reshape(1)
    place = lax.axis_index("vol").astype(jnp.int32)

    fourier = transform(orient, defocus, images[0], *dft_tables(npix))
    fourier = lax.all_to_all(
        fourier.reshape(n_img, rows, 2 * npix + META), "img", split_axis=0, concat_axis=0, tiled=True
    ).reshape(many, 2 * npix + META)
    vol_rows = lax.all_gather(volume.reshape(slab * rows, 2 * npix), "vol", axis=0, tiled=True)
    lookup = prepare(jnp.swapaxes(planes, 1, 2), jnp.swapaxes(weights, 1, 2), deep)
    filtered, picks, part, about = compare(
        slot, noise, fourier, lookup, vol_rows, ori, rows, n_img
    )
    square = squares(slot, about, ori, rows, npix)
    part = lax.all_to_all(
        part.reshape(n_img, 2, 2 * n_img), "img", split_axis=0, concat_axis=0, tiled=True
    ).reshape(2 * n_img, 2 * n_img)
    probs, share, send = project(
        (place % 2).reshape(1), part, picks, filtered, square, rows, ori, pairs
    )
    mine = lax.dynamic_slice_in_dim(
        probs[:2].reshape(2 * 2, n_img), lax.axis_index("img"), 1, 1
    ).reshape(1, ori)
    mine = jnp.concatenate([mine[:, ori - 1 :], mine[:, : ori - 1]], 1)
    got = lax.ppermute(send, "vol", [(v, v ^ 1) for v in range(n_vol)])
    keep = keep_own(share, filtered, square, pairs)
    own, *sends = middle((place // 2).reshape(1), keep, got)
    parts = [
        lax.ppermute(sends[apart - 1], "vol", [(v, v ^ (2 * apart)) for v in range(n_vol)])
        for apart in (2, 3, 1)
    ]
    data, weight = add_lines(
        collect_kernel,
        "collect",
        [own],
        data_old.reshape(slab * rows, 2 * npix),
        weight_old.reshape(slab * rows, npix),
    )
    data, weight = add_lines(finish_kernel, "finish", parts, data, weight)
    return (mine, data.reshape(data_old.shape), weight.reshape(weight_old.shape))


def solution(mesh):
    placed = (
        P(("img", "vol"), None, None),
        P(("img", "vol")),
        P(("img", "vol")),
        P(("img", "vol"), None),
        P(None, None, "img"),
        P(None, None, "img"),
        P("vol", "img", None),
        P("vol", "img", None),
        P("vol", "img", None),
    )
    return jax.shard_map(
        on_device,
        mesh=mesh,
        in_specs=placed,
        out_specs=(P(("img", "vol"), None), P("vol", "img", None), P("vol", "img", None)),
        check_vma=False,
    )
```

```python
import functools
import math

import jax
import jax.numpy as jnp
import ml_dtypes
import numpy as np
from jax import lax
from jax.experimental import pallas as pl
from jax.experimental.pallas import tpu as pltpu
from jax.sharding import PartitionSpec as P

AMP = 0.1
TILT = math.asin(AMP)
TURN = 2.0 * math.pi
TURN_HIGH = math.floor(TURN * 4096) / 4096
TURN_LOW = TURN - TURN_HIGH
SINE = tuple(
    factor / TURN ** (2 * power + 1)
    for power, factor in enumerate(
        (
            6.283185272722434,
            -41.341697068956265,
            81.60502462257806,
            -76.70155117622761,
            42.01616582127327,
            -14.868610992503873,
            3.199693654235983,
        )
    )
)
HUGE = 56 * 1024 * 1024
LARGE = 32 * 1024 * 1024
SMALL = 16 * 1024 * 1024
META = 128


def dft_tables(npix):
    index = np.arange(npix)
    angle = (index[:, None] * index[None, :] % npix) * (2.0 * math.pi / npix)
    scale = 1.0 / math.sqrt(npix)
    parts = [np.cos(angle) * scale, np.sin(angle) * scale]
    halves = [part[: npix // 2, parity::2] for parity in range(2) for part in parts]
    return tuple(
        jnp.asarray(np.concatenate(table, 1).astype(np.float32).astype(ml_dtypes.bfloat16))
        for table in (parts, halves)
    )


def frequency(index, npix):
    return ((index + npix // 2) % npix - npix // 2).astype(jnp.float32) / npix


def params(size):
    return pltpu.CompilerParams(vmem_limit_bytes=size)


def cost(flops, size):
    return pl.CostEstimate(flops=flops, bytes_accessed=size, transcendentals=0)


def whole():
    return pl.BlockSpec(memory_space=pltpu.VMEM)


def scalar():
    return pl.BlockSpec(memory_space=pltpu.SMEM)


def same(a, b):
    return lax.dot_general(a, b, (((1,), (1,)), ((), ())), preferred_element_type=jnp.float32)


def three_parts(value):
    parts = []
    for _ in range(3):
        part = value.astype(jnp.bfloat16).astype(jnp.float32)
        parts.append(part)
        value = value - part
    return parts


def bits(rows):
    assert rows & (rows - 1) == 0
    return rows.bit_length() - 1


def spread_over(rows, shape, image_axis):
    image = lax.broadcasted_iota(jnp.int32, shape, image_axis)
    owner = lax.broadcasted_iota(jnp.int32, shape, 1 - image_axis) >> bits(rows)
    return jnp.where(owner == image, 1.0, 0.0).astype(jnp.bfloat16)


def own_row(values, rows):
    height, width = values.shape
    sublane = lax.broadcasted_iota(jnp.int32, (rows, width), 0)
    lane = lax.broadcasted_iota(jnp.int32, (rows, width), 1) & (rows - 1)
    return jnp.where((sublane == lane)[None], values.reshape(height // rows, rows, width), 0.0)


def transform_kernel(chunk, orient_hbm, defocus_hbm, image_hbm, table_hbm, halves_hbm, out_hbm, orient_ref, defocus_ref, image_ref, wide_ref, table_ref, halves_ref, both_ref, out_ref, in_sems, out_sems):
    npix = image_ref.shape[0]
    half = npix // 2
    ori = orient_ref.shape[1]
    starts = list(range(0, 2 * npix, chunk))
    pairs = [(image_hbm, image_ref)]
    pairs += [(table_hbm.at[:, pl.ds(start, chunk)], table_ref.at[:, pl.ds(start, chunk)]) for start in starts]
    pairs += [(halves_hbm, halves_ref), (orient_hbm, orient_ref), (defocus_hbm, defocus_ref)]
    loads = []
    for number, (source, target) in enumerate(pairs):
        load = pltpu.make_async_copy(source, target, in_sems.at[number])
        load.start()
        loads.append(load)
    loads[0].wait()
    tiles = range(npix // 128)
    for tile in tiles:
        wide_ref[tile] = image_ref[:, tile * 128 : (tile + 1) * 128].astype(jnp.float32)
    image = jnp.concatenate(
        [
            jnp.concatenate([wide_ref[tile, pl.ds(parity, half, 2), :] for tile in tiles], 1)
            for parity in range(2)
        ],
        0,
    ).astype(jnp.bfloat16)
    for number, start in enumerate(starts):
        loads[1 + number].wait()
        first = jnp.dot(
            image, table_ref[:, start : start + chunk], preferred_element_type=jnp.float32
        ).astype(jnp.bfloat16)
        for parity in range(2):
            part = first[parity * half : (parity + 1) * half]
            upper = slice(parity * npix, parity * npix + half)
            lower = slice(parity * npix + half, (parity + 1) * npix)
            if start < npix:
                both_ref[upper, start : start + chunk] = part
                both_ref[lower, npix + start : npix + start + chunk] = -part
            else:
                both_ref[upper, start : start + chunk] = -part
                both_ref[lower, start - npix : start - npix + chunk] = -part
    for load in loads[1 + len(starts) :]:
        load.wait()
    saves = []

    def save(start, size):
        at = pl.ds(start, size)
        copy = pltpu.make_async_copy(out_ref.at[:, at], out_hbm.at[:, at], out_sems.at[len(saves)])
        copy.start()
        saves.append(copy)

    lane = lax.broadcasted_iota(jnp.int32, (8, META), 1)
    codes = jnp.zeros((8, META), jnp.int32)
    for o in range(ori):
        label = orient_ref[0, o]
        codes = jnp.where(lane == o, label & 255, codes)
        codes = jnp.where(lane == ori + o, label >> 8, codes)
    about = codes.astype(jnp.float32)
    parts = three_parts(jnp.full((8, META), defocus_ref[0], jnp.float32))
    for place, part in enumerate(parts, 2 * ori):
        about = jnp.where(lane == place, part, about)
    out_ref[:, 2 * npix :] = jnp.broadcast_to(about[:1], (npix, META)).astype(jnp.bfloat16)
    save(2 * npix, META)
    chunk = chunk // 2
    for start in range(0, 2 * npix, chunk):
        even, odd = (
            jnp.dot(
                halves_ref[:, parity * npix : (parity + 1) * npix],
                both_ref[parity * npix : (parity + 1) * npix, start : start + chunk],
                preferred_element_type=jnp.float32,
            )
            for parity in range(2)
        )
        out_ref[:half, start : start + chunk] = (even + odd).astype(jnp.bfloat16)
        out_ref[half:, start : start + chunk] = (even - odd).astype(jnp.bfloat16)
        save(start, chunk)
    for copy in saves:
        copy.wait()


def transform(orient, defocus, image, table, halves):
    npix = image.shape[0]
    chunk = npix
    pieces = 2 * npix // chunk
    return pl.pallas_call(
        functools.partial(transform_kernel, chunk),
        in_specs=[pl.BlockSpec(memory_space=pl.ANY)] * 5,
        out_specs=pl.BlockSpec(memory_space=pl.ANY),
        out_shape=jax.ShapeDtypeStruct((npix, 2 * npix + META), jnp.bfloat16),
        scratch_shapes=[
            pltpu.SMEM(orient.shape, jnp.int32),
            pltpu.SMEM(defocus.shape, jnp.float32),
            pltpu.VMEM((npix, npix), jnp.bfloat16),
            pltpu.VMEM((npix // 128, npix, 128), jnp.float32),
            pltpu.VMEM((npix, 2 * npix), jnp.bfloat16),
            pltpu.VMEM((npix // 2, 2 * npix), jnp.bfloat16),
            pltpu.VMEM((2 * npix, 2 * npix), jnp.bfloat16),
            pltpu.VMEM((npix, 2 * npix + META), jnp.bfloat16),
            pltpu.SemaphoreType.DMA((pieces + 4,)),
            pltpu.SemaphoreType.DMA((2 * pieces + 1,)),
        ],
        compiler_params=params(HUGE),
        cost_estimate=cost(12 * npix**3, 10 * npix * npix),
        name="transform",
    )(orient, defocus, image, table, halves)


def prepare_kernel(planes_ref, weights_ref, lookup_ref):
    deep, labels = lookup_ref.shape
    rows = planes_ref.shape[1]
    level = lax.broadcasted_iota(jnp.int32, (deep // rows, rows, labels), 0)
    total = jnp.zeros((deep // rows, rows, labels), jnp.float32)
    for k in range(2):
        weight = weights_ref[k].astype(jnp.float32)
        total = total + jnp.where(level == planes_ref[k][None], weight[None], 0.0)
    lookup_ref[...] = total.reshape(deep, labels).astype(jnp.bfloat16)


def prepare(planes, weights, deep):
    labels = planes.shape[2]
    return pl.pallas_call(
        prepare_kernel,
        in_specs=[whole(), whole()],
        out_specs=whole(),
        out_shape=jax.ShapeDtypeStruct((deep, labels), jnp.bfloat16),
        compiler_params=params(SMALL),
        cost_estimate=cost(1 << 22, 1 << 20),
        name="prepare",
    )(planes, weights)


def contrast(defocus, row_square, start, width, npix):
    column = start + lax.broadcasted_iota(jnp.int32, (1, width), 1)
    freq_x = frequency(column, npix)
    chi = defocus * (row_square + freq_x * freq_x)
    turns = jnp.floor(chi * (1.0 / TURN) + (TILT / TURN + 0.5))
    angle = ((chi - turns * TURN_HIGH) - turns * TURN_LOW) + TILT
    square = angle * angle
    series = -SINE[-1]
    for term in SINE[-2::-1]:
        series = series * square - term
    return series * angle


def line_geometry(meta, ori, rows, many, npix, slot):
    place = 2 * ori
    defocus = meta[:, place : place + 1] + meta[:, place + 1 : place + 2] + meta[:, place + 2 : place + 3]
    index = (lax.broadcasted_iota(jnp.int32, (many, 1), 0) & (rows - 1)) + slot * rows
    freq_y = jnp.where(index < npix // 2, index, index - npix).astype(jnp.float32) / npix
    return defocus, freq_y * freq_y


def compare_kernel(ori, rows, slot_ref, noise_ref, fourier_ref, lookup_ref, volume_ref, filtered_ref, picks_ref, part_ref, about_ref, mix_ref, power_ref):
    many, wide = filtered_ref.shape
    npix = wide // 2
    deep = volume_ref.shape[0]
    images = many // rows

    meta = fourier_ref[:, wide:]
    here = lax.broadcasted_iota(jnp.int32, (images, many), 0) << bits(rows)
    there = lax.broadcasted_iota(jnp.int32, (images, many), 1)
    pick = jnp.where(here == there, 1.0, 0.0).astype(jnp.bfloat16)
    about = jnp.dot(pick, meta, preferred_element_type=jnp.float32)
    about_ref[...] = about
    label = lax.broadcasted_iota(jnp.int32, (images, lookup_ref.shape[1]), 1).astype(jnp.float32)
    found = []
    for o in range(ori):
        mine = about[:, o : o + 1] + 256.0 * about[:, ori + o : ori + o + 1]
        found.append(jnp.where(label == mine, 1.0, 0.0).astype(jnp.bfloat16))
    found = same(jnp.concatenate(found, 0), lookup_ref[...]).astype(jnp.bfloat16)
    picks_ref[...] = found
    spread = spread_over(rows, (many, images), 1)
    for o in range(ori):
        every = jnp.dot(
            spread, found[o * images : (o + 1) * images], preferred_element_type=jnp.float32
        )
        mix_ref[o * many : (o + 1) * many, :] = (
            own_row(every, rows).reshape(many, deep).astype(jnp.bfloat16)
        )
    defocus, row_square = line_geometry(meta.astype(jnp.float32), ori, rows, many, npix, slot_ref[0])
    def sections(start):
        planes = jnp.concatenate(
            [volume_ref[:, at : at + 128] for at in (start, npix + start)], 1
        )
        return [
            jnp.dot(
                mix_ref[o * many : (o + 1) * many, :], planes, preferred_element_type=jnp.float32
            )
            for o in range(ori)
        ]

    current = sections(0)
    for start in range(0, npix, 128):
        ctf = contrast(defocus, row_square, start, 128, npix)
        for at in (start, npix + start):
            filtered_ref[:, at : at + 128] = (
                ctf * fourier_ref[:, at : at + 128].astype(jnp.float32)
            ).astype(jnp.bfloat16)
        square = ctf * ctf
        following = sections(start + 128) if start + 128 < npix else None
        for o in range(ori):
            section = current[o] * current[o]
            power = square * (section[:, :128] + section[:, 128:])
            if start:
                power = power + power_ref[o]
            power_ref[o] = power
        current = following

    found = own_row(same(filtered_ref[...], volume_ref[...]), rows)
    found = jnp.sum(found, axis=1)
    halves = []
    for o in range(ori):
        cross = found * picks_ref[o * images : (o + 1) * images, :].astype(jnp.float32)
        lanes = cross[:, :128]
        for start in range(128, deep, 128):
            lanes = lanes + cross[:, start : start + 128]
        power = jnp.sum(power_ref[o].reshape(images, rows, 128), axis=1)
        halves.append(lanes - 0.5 * power)
    lane = lax.broadcasted_iota(jnp.int32, (images, 128), 1)
    image = lax.broadcasted_iota(jnp.int32, (images, 128), 0)
    noise = jnp.where((image == slot_ref[0]) & (lane == 0), noise_ref[0], 0.0)
    halves = [noise] + [part - halves[0] for part in halves[1:]]
    upper = jnp.concatenate(halves[: ori // 2], 0)
    lower = jnp.concatenate(halves[ori // 2 :], 0)
    upper = jnp.sum(jnp.transpose(upper), axis=0, keepdims=True)
    lower = jnp.sum(jnp.transpose(lower), axis=0, keepdims=True)
    even = (lax.broadcasted_iota(jnp.int32, part_ref.shape, 0) & 1) == 0
    part_ref[...] = jnp.where(even, upper, lower)


def compare(slot, noise, fourier, lookup, volume, ori, rows, copies):
    many = fourier.shape[0]
    deep, wide = volume.shape
    images = many // rows
    return pl.pallas_call(
        functools.partial(compare_kernel, ori, rows),
        in_specs=[scalar()] * 2 + [whole()] * 3,
        out_specs=(whole(),) * 4,
        out_shape=(
            jax.ShapeDtypeStruct((many, wide), jnp.bfloat16),
            jax.ShapeDtypeStruct((ori * images, deep), jnp.bfloat16),
            jax.ShapeDtypeStruct((copies * 2, 2 * images), jnp.float32),
            jax.ShapeDtypeStruct((images, META), jnp.float32),
        ),
        scratch_shapes=[
            pltpu.VMEM((ori * many, deep), jnp.bfloat16),
            pltpu.VMEM((ori, many, 128), jnp.float32),
        ],
        compiler_params=params(LARGE),
        cost_estimate=cost(1 << 31, 5 << 20),
        name="compare",
    )(slot, noise, fourier, lookup, volume)


def squares_kernel(ori, rows, npix, slot_ref, about_ref, square_ref):
    many = square_ref.shape[0]
    images = many // rows
    about = about_ref[...]
    meta = jnp.dot(
        spread_over(rows, (many, images), 1),
        about.astype(jnp.bfloat16),
        preferred_element_type=jnp.float32,
    )
    defocus, row_square = line_geometry(meta, ori, rows, many, npix, slot_ref[0])
    for start in range(0, square_ref.shape[1], 128):
        ctf = contrast(defocus, row_square, start, 128, npix)
        square_ref[:, start : start + 128] = (ctf * ctf).astype(jnp.bfloat16)


def squares(slot, about, ori, rows, npix):
    images = about.shape[0]
    return pl.pallas_call(
        functools.partial(squares_kernel, ori, rows, npix),
        in_specs=[scalar(), whole()],
        out_specs=whole(),
        out_shape=jax.ShapeDtypeStruct((images * rows, npix // 2 + 128), jnp.bfloat16),
        compiler_params=params(SMALL),
        cost_estimate=cost(1 << 27, 1 << 20),
        name="squares",
    )(slot, about)


def pack(target_ref, share, source_ref, start, last):
    pairs = target_ref.shape[0]
    slab = share.shape[0] // pairs
    sums = jnp.dot(share, source_ref[...], preferred_element_type=jnp.float32)
    for number in range(sums.shape[1] // 128):
        value = sums[:, number * 128 : (number + 1) * 128].reshape(pairs, slab, 128)
        at = (start + number) * slab
        if start + number < last:
            target_ref[:, at : at + slab, :] = value.astype(jnp.bfloat16)
        else:
            lane = lax.broadcasted_iota(jnp.int32, (pairs, slab // 2, 128), 2)
            lower = jnp.broadcast_to(value[:, slab // 2 :, :1], lane.shape)
            value = jnp.where(lane == 0, value[:, : slab // 2], lower)
            target_ref[:, at : at + slab // 2, :] = value.astype(jnp.bfloat16)


def pack_both(target_ref, share, filtered_ref, square_ref):
    tiles = filtered_ref.shape[1] // 128
    last = tiles + square_ref.shape[1] // 128 - 1
    pack(target_ref, share, filtered_ref, 0, last)
    pack(target_ref, share, square_ref, tiles, last)


def project_kernel(rows, ori, core_ref, part_ref, picks_ref, filtered_ref, square_ref, probs_ref, share_ref, send_ref):
    many = filtered_ref.shape[0]
    deep = picks_ref.shape[1]
    lanes = part_ref.shape[1]
    images = lanes // 2
    sums = jnp.sum(part_ref[...].reshape(part_ref.shape[0] // 8, 8, lanes), axis=0)
    sums = sums + pltpu.roll(sums, 4, 0)
    sums = sums + pltpu.roll(sums, 2, 0)
    line = lax.broadcasted_iota(jnp.int32, sums.shape, 0) & 1
    lane = lax.broadcasted_iota(jnp.int32, sums.shape, 1)
    noise = jnp.where(line == 0, sums, pltpu.roll(sums, 1, 0))
    noise = jnp.where(lane < images, noise, pltpu.roll(noise, images, 1))
    score = jnp.where((line == 0) & (lane < images), 0.0, sums / noise)
    top = jnp.maximum(score, pltpu.roll(score, 1, 0))
    top = jnp.maximum(top, pltpu.roll(top, images, 1))
    power = jnp.exp(score - top)
    total = power + pltpu.roll(power, 1, 0)
    total = total + pltpu.roll(total, images, 1)
    probs = power / total
    probs_ref[...] = probs
    column = jnp.transpose(jnp.concatenate([probs] * (lanes // 8), 0))
    share = jnp.zeros((images, deep), jnp.float32)
    for o in range(ori):
        half = o % 2
        chance = column[half * images : (half + 1) * images, o // 2 : o // 2 + 1]
        share = share + chance * picks_ref[o * images : (o + 1) * images, :].astype(jnp.float32)
    share = jnp.dot(
        jnp.transpose(share).astype(jnp.bfloat16),
        spread_over(rows, (images, many), 0),
        preferred_element_type=jnp.float32,
    )
    pairs = send_ref.shape[0]
    share = own_row(share, rows).reshape(pairs, 2, deep // (2 * pairs), many)
    first = core_ref[0] == 0
    ours = jnp.where(first, share[:, 0], share[:, 1]).reshape(deep // 2, many)
    theirs = jnp.where(first, share[:, 1], share[:, 0]).reshape(deep // 2, many)
    share_ref[...] = ours.astype(jnp.bfloat16)
    pack_both(send_ref, theirs.astype(jnp.bfloat16), filtered_ref, square_ref)


def packed(deep, filtered, square, pairs):
    slab = deep // (2 * pairs)
    lines = (filtered.shape[1] + square.shape[1]) // 128 * slab - slab // 2
    return jax.ShapeDtypeStruct((pairs, lines, 128), jnp.bfloat16)


def project(core, part, picks, filtered, square, rows, ori, pairs):
    many = filtered.shape[0]
    deep = picks.shape[1]
    return pl.pallas_call(
        functools.partial(project_kernel, rows, ori),
        in_specs=[scalar()] + [whole()] * 4,
        out_specs=(whole(), whole(), whole()),
        out_shape=(
            jax.ShapeDtypeStruct((8, part.shape[1]), jnp.float32),
            jax.ShapeDtypeStruct((deep // 2, many), jnp.bfloat16),
            packed(deep, filtered, square, pairs),
        ),
        compiler_params=params(LARGE),
        cost_estimate=cost(1 << 28, 4 << 20),
        name="project",
    )(core, part, picks, filtered, square)


def keep_kernel(share_ref, filtered_ref, square_ref, keep_ref):
    pack_both(keep_ref, share_ref[...], filtered_ref, square_ref)


def keep_own(share, filtered, square, pairs):
    return pl.pallas_call(
        keep_kernel,
        out_shape=packed(2 * share.shape[0], filtered, square, pairs),
        compiler_params=params(SMALL),
        cost_estimate=cost(1 << 28, 2 << 20),
        name="keep_own",
    )(share, filtered, square)


def middle_kernel(high_ref, keep_ref, got_ref, own_ref, *send_refs):
    pairs = keep_ref.shape[0]
    for apart in range(pairs):
        at = high_ref[0] ^ apart
        total = keep_ref[at].astype(jnp.float32) + got_ref[at].astype(jnp.float32)
        if apart == 0:
            own_ref[...] = total
        else:
            send_refs[apart - 1][...] = total.astype(jnp.bfloat16)


def middle(high, keep, got):
    pairs, slab, wide = keep.shape
    return pl.pallas_call(
        middle_kernel,
        in_specs=[scalar(), whole(), whole()],
        out_specs=(whole(),) * pairs,
        out_shape=(jax.ShapeDtypeStruct((slab, wide), jnp.float32),)
        + (jax.ShapeDtypeStruct((slab, wide), jnp.bfloat16),) * (pairs - 1),
        compiler_params=params(SMALL),
        cost_estimate=cost(1 << 20, 2 << 20),
        name="middle",
    )(high, keep, got)


def mirror_columns(lower, last, precision=None):
    slab, half = lower.shape
    source = lax.broadcasted_iota(jnp.int32, (half, half), 0)
    target = lax.broadcasted_iota(jnp.int32, (half, half), 1)
    mirror = jnp.where(source + target == half, 1.0, 0.0).astype(lower.dtype)
    upper = jnp.dot(lower, mirror, preferred_element_type=jnp.float32, precision=precision)
    lane = lax.broadcasted_iota(jnp.int32, (slab, half), 1)
    return jnp.where(lane == 0, last, upper)


def spread_lines(lines, slab, npix):
    tiles = [lines[at : at + slab] for at in range(0, lines.shape[0] - slab // 2, slab)]
    last = lines[lines.shape[0] - slab // 2 :].astype(jnp.float32)
    last = jnp.concatenate([last[:, :1], last[:, 1:2]], 0)
    count = 2 * npix // 128
    return jnp.concatenate(tiles[:count], 1), jnp.concatenate(tiles[count:], 1), last


def collect_kernel(own_ref, data_ref, weight_ref, data_out, weight_out):
    slab, npix = weight_ref.shape
    half = npix // 2
    data, lower, last = spread_lines(own_ref[...], slab, npix)
    data_out[...] = data_ref[...] + data
    weight_out[:, :half] = weight_ref[:, :half] + lower
    weight_out[:, half:] = weight_ref[:, half:] + mirror_columns(
        lower, last, lax.Precision.HIGHEST
    )


def finish_kernel(*refs):
    *part_refs, data_ref, weight_ref, data_out, weight_out = refs
    slab, npix = weight_ref.shape
    half = npix // 2
    data = data_ref[...]
    weight = weight_ref[:, :half]
    lowers, lasts = [], []
    for part_ref in part_refs:
        part, lower, last = spread_lines(part_ref[...], slab, npix)
        data = data + part.astype(jnp.float32)
        weight = weight + lower.astype(jnp.float32)
        lowers.append(lower)
        lasts.append(last)
    uppers = mirror_columns(jnp.concatenate(lowers, 0), jnp.concatenate(lasts, 0))
    upper = weight_ref[:, half:]
    for number in range(len(part_refs)):
        upper = upper + uppers[number * slab : (number + 1) * slab]
    data_out[...] = data
    weight_out[:, :half] = weight
    weight_out[:, half:] = upper


def add_lines(kernel, name, lines, data, weight):
    return pl.pallas_call(
        kernel,
        out_shape=(
            jax.ShapeDtypeStruct(data.shape, jnp.float32),
            jax.ShapeDtypeStruct(weight.shape, jnp.float32),
        ),
        compiler_params=params(SMALL),
        cost_estimate=cost(1 << 20, 2 << 20),
        name=name,
    )(*lines, data, weight)


def on_device(images, defocus, noise, orient, planes, weights, volume, data_old, weight_old):
    npix = images.shape[1]
    ori = orient.shape[1]
    n_img = lax.axis_size("img")
    n_vol = lax.axis_size("vol")
    rows = npix // n_img
    slab = volume.shape[0]
    deep = n_vol * slab * rows
    many = n_img * rows
    pairs = n_vol // 2
    slot = lax.axis_index("img").astype(jnp.int32).reshape(1)
    place = lax.axis_index("vol").astype(jnp.int32)

    fourier = transform(orient, defocus, images[0], *dft_tables(npix))
    fourier = lax.all_to_all(
        fourier.reshape(n_img, rows, 2 * npix + META), "img", split_axis=0, concat_axis=0, tiled=True
    ).reshape(many, 2 * npix + META)
    vol_rows = lax.all_gather(volume.reshape(slab * rows, 2 * npix), "vol", axis=0, tiled=True)
    lookup = prepare(jnp.swapaxes(planes, 1, 2), jnp.swapaxes(weights, 1, 2), deep)
    filtered, picks, part, about = compare(
        slot, noise, fourier, lookup, vol_rows, ori, rows, n_img
    )
    square = squares(slot, about, ori, rows, npix)
    part = lax.all_to_all(
        part.reshape(n_img, 2, 2 * n_img), "img", split_axis=0, concat_axis=0, tiled=True
    ).reshape(2 * n_img, 2 * n_img)
    probs, share, send = project(
        (place % 2).reshape(1), part, picks, filtered, square, rows, ori, pairs
    )
    mine = lax.dynamic_slice_in_dim(
        probs[:2].reshape(2 * 2, n_img), lax.axis_index("img"), 1, 1
    ).reshape(1, ori)
    got = lax.ppermute(send, "vol", [(v, v ^ 1) for v in range(n_vol)])
    keep = keep_own(share, filtered, square, pairs)
    own, *sends = middle((place // 2).reshape(1), keep, got)
    parts = [
        lax.ppermute(sends[apart - 1], "vol", [(v, v ^ (2 * apart)) for v in range(n_vol)])
        for apart in (2, 3, 1)
    ]
    data, weight = add_lines(
        collect_kernel,
        "collect",
        [own],
        data_old.reshape(slab * rows, 2 * npix),
        weight_old.reshape(slab * rows, npix),
    )
    data, weight = add_lines(finish_kernel, "finish", parts, data, weight)
    return (mine, data.reshape(data_old.shape), weight.reshape(weight_old.shape))


def solution(mesh):
    placed = (
        P(("img", "vol"), None, None),
        P(("img", "vol")),
        P(("img", "vol")),
        P(("img", "vol"), None),
        P(None, None, "img"),
        P(None, None, "img"),
        P("vol", "img", None),
        P("vol", "img", None),
        P("vol", "img", None),
    )
    return jax.shard_map(
        on_device,
        mesh=mesh,
        in_specs=placed,
        out_specs=(P(("img", "vol"), None), P("vol", "img", None), P("vol", "img", None)),
        check_vma=False,
    )
```

```python
import functools
import math

import jax
import jax.numpy as jnp
import ml_dtypes
import numpy as np
from jax import lax
from jax.experimental import pallas as pl
from jax.experimental.pallas import tpu as pltpu
from jax.sharding import PartitionSpec as P

AMP = 0.1
TILT = math.asin(AMP)
TURN = 2.0 * math.pi
TURN_HIGH = math.floor(TURN * 4096) / 4096
TURN_LOW = TURN - TURN_HIGH
SINE = tuple(
    factor / TURN ** (2 * power + 1)
    for power, factor in enumerate(
        (
            6.283185272722434,
            -41.341697068956265,
            81.60502462257806,
            -76.70155117622761,
            42.01616582127327,
            -14.868610992503873,
            3.199693654235983,
        )
    )
)
HUGE = 56 * 1024 * 1024
LARGE = 32 * 1024 * 1024
SMALL = 16 * 1024 * 1024
META = 128


def dft_tables(npix):
    index = np.arange(npix)
    angle = (index[:, None] * index[None, :] % npix) * (2.0 * math.pi / npix)
    scale = 1.0 / math.sqrt(npix)
    parts = [np.cos(angle) * scale, np.sin(angle) * scale]
    halves = [part[: npix // 2, parity::2] for parity in range(2) for part in parts]
    return tuple(
        jnp.asarray(np.concatenate(table, 1).astype(np.float32).astype(ml_dtypes.bfloat16))
        for table in (parts, halves)
    )


def frequency(index, npix):
    return ((index + npix // 2) % npix - npix // 2).astype(jnp.float32) / npix


def params(size):
    return pltpu.CompilerParams(vmem_limit_bytes=size)


def cost(flops, size):
    return pl.CostEstimate(flops=flops, bytes_accessed=size, transcendentals=0)


def whole():
    return pl.BlockSpec(memory_space=pltpu.VMEM)


def scalar():
    return pl.BlockSpec(memory_space=pltpu.SMEM)


def three_parts(value):
    parts = []
    for _ in range(3):
        part = value.astype(jnp.bfloat16).astype(jnp.float32)
        parts.append(part)
        value = value - part
    return parts


def bits(rows):
    assert rows & (rows - 1) == 0
    return rows.bit_length() - 1


def spread_over(rows, shape, image_axis):
    image = lax.broadcasted_iota(jnp.int32, shape, image_axis)
    owner = lax.broadcasted_iota(jnp.int32, shape, 1 - image_axis) >> bits(rows)
    return jnp.where(owner == image, 1.0, 0.0).astype(jnp.bfloat16)


def own_row(values, rows):
    height, width = values.shape
    sublane = lax.broadcasted_iota(jnp.int32, (rows, width), 0)
    lane = lax.broadcasted_iota(jnp.int32, (rows, width), 1) & (rows - 1)
    return jnp.where((sublane == lane)[None], values.reshape(height // rows, rows, width), 0.0)


def transform_kernel(chunk, orient_hbm, defocus_hbm, image_hbm, table_hbm, halves_hbm, out_hbm, orient_ref, defocus_ref, image_ref, wide_ref, table_ref, halves_ref, both_ref, out_ref, in_sems, out_sems):
    npix = image_ref.shape[0]
    half = npix // 2
    ori = orient_ref.shape[1]
    starts = list(range(0, 2 * npix, chunk))
    pairs = [(image_hbm, image_ref)]
    pairs += [(table_hbm.at[:, pl.ds(start, chunk)], table_ref.at[:, pl.ds(start, chunk)]) for start in starts]
    pairs += [(halves_hbm, halves_ref), (orient_hbm, orient_ref), (defocus_hbm, defocus_ref)]
    loads = []
    for number, (source, target) in enumerate(pairs):
        load = pltpu.make_async_copy(source, target, in_sems.at[number])
        load.start()
        loads.append(load)
    loads[0].wait()
    tiles = range(npix // 128)
    for tile in tiles:
        wide_ref[tile] = image_ref[:, tile * 128 : (tile + 1) * 128].astype(jnp.float32)
    image = jnp.concatenate(
        [
            jnp.concatenate([wide_ref[tile, pl.ds(parity, half, 2), :] for tile in tiles], 1)
            for parity in range(2)
        ],
        0,
    ).astype(jnp.bfloat16)
    for number, start in enumerate(starts):
        loads[1 + number].wait()
        first = jnp.dot(
            image, table_ref[:, start : start + chunk], preferred_element_type=jnp.float32
        ).astype(jnp.bfloat16)
        for parity in range(2):
            part = first[parity * half : (parity + 1) * half]
            upper = slice(parity * npix, parity * npix + half)
            lower = slice(parity * npix + half, (parity + 1) * npix)
            if start < npix:
                both_ref[upper, start : start + chunk] = part
                both_ref[lower, npix + start : npix + start + chunk] = -part
            else:
                both_ref[upper, start : start + chunk] = -part
                both_ref[lower, start - npix : start - npix + chunk] = -part
    for load in loads[1 + len(starts) :]:
        load.wait()
    saves = []

    def save(start, size):
        at = pl.ds(start, size)
        copy = pltpu.make_async_copy(out_ref.at[:, at], out_hbm.at[:, at], out_sems.at[len(saves)])
        copy.start()
        saves.append(copy)

    lane = lax.broadcasted_iota(jnp.int32, (8, META), 1)
    codes = jnp.zeros((8, META), jnp.int32)
    for o in range(ori):
        label = orient_ref[0, o]
        codes = jnp.where(lane == o, label & 255, codes)
        codes = jnp.where(lane == ori + o, label >> 8, codes)
    about = codes.astype(jnp.float32)
    parts = three_parts(jnp.full((8, META), defocus_ref[0], jnp.float32))
    for place, part in enumerate(parts, 2 * ori):
        about = jnp.where(lane == place, part, about)
    out_ref[:, 2 * npix :] = jnp.broadcast_to(about[:1], (npix, META)).astype(jnp.bfloat16)
    save(2 * npix, META)
    chunk = chunk // 2
    for start in range(0, 2 * npix, chunk):
        even, odd = (
            jnp.dot(
                halves_ref[:, parity * npix : (parity + 1) * npix],
                both_ref[parity * npix : (parity + 1) * npix, start : start + chunk],
                preferred_element_type=jnp.float32,
            )
            for parity in range(2)
        )
        out_ref[:half, start : start + chunk] = (even + odd).astype(jnp.bfloat16)
        out_ref[half:, start : start + chunk] = (even - odd).astype(jnp.bfloat16)
        save(start, chunk)
    for copy in saves:
        copy.wait()


def transform(orient, defocus, image, table, halves):
    npix = image.shape[0]
    chunk = npix
    pieces = 2 * npix // chunk
    return pl.pallas_call(
        functools.partial(transform_kernel, chunk),
        in_specs=[pl.BlockSpec(memory_space=pl.ANY)] * 5,
        out_specs=pl.BlockSpec(memory_space=pl.ANY),
        out_shape=jax.ShapeDtypeStruct((npix, 2 * npix + META), jnp.bfloat16),
        scratch_shapes=[
            pltpu.SMEM(orient.shape, jnp.int32),
            pltpu.SMEM(defocus.shape, jnp.float32),
            pltpu.VMEM((npix, npix), jnp.bfloat16),
            pltpu.VMEM((npix // 128, npix, 128), jnp.float32),
            pltpu.VMEM((npix, 2 * npix), jnp.bfloat16),
            pltpu.VMEM((npix // 2, 2 * npix), jnp.bfloat16),
            pltpu.VMEM((2 * npix, 2 * npix), jnp.bfloat16),
            pltpu.VMEM((npix, 2 * npix + META), jnp.bfloat16),
            pltpu.SemaphoreType.DMA((pieces + 4,)),
            pltpu.SemaphoreType.DMA((2 * pieces + 1,)),
        ],
        compiler_params=params(HUGE),
        cost_estimate=cost(12 * npix**3, 10 * npix * npix),
        name="transform",
    )(orient, defocus, image, table, halves)


def prepare_kernel(planes_ref, weights_ref, lookup_ref):
    labels, deep = lookup_ref.shape
    rows = planes_ref.shape[1]
    level = lax.broadcasted_iota(jnp.int32, (deep // rows, rows, labels), 0)
    total = jnp.zeros((deep // rows, rows, labels), jnp.float32)
    for k in range(2):
        weight = weights_ref[k].astype(jnp.float32)
        total = total + jnp.where(level == planes_ref[k][None], weight[None], 0.0)
    lookup_ref[...] = jnp.transpose(total.reshape(deep, labels)).astype(jnp.bfloat16)


def prepare(planes, weights, deep):
    labels = planes.shape[2]
    return pl.pallas_call(
        prepare_kernel,
        in_specs=[whole(), whole()],
        out_specs=whole(),
        out_shape=jax.ShapeDtypeStruct((labels, deep), jnp.bfloat16),
        compiler_params=params(SMALL),
        cost_estimate=cost(1 << 22, 1 << 20),
        name="prepare",
    )(planes, weights)


def turn_kernel(volume_ref, turned_ref):
    turned_ref[...] = jnp.transpose(volume_ref[...].astype(jnp.float32)).astype(jnp.bfloat16)


def turn(volume):
    return pl.pallas_call(
        turn_kernel,
        out_shape=jax.ShapeDtypeStruct(volume.shape[::-1], jnp.bfloat16),
        compiler_params=params(SMALL),
        cost_estimate=cost(1 << 22, 1 << 20),
        name="turn",
    )(volume)


def contrast(defocus, row_square, start, width, npix):
    column = start + lax.broadcasted_iota(jnp.int32, (1, width), 1)
    freq_x = frequency(column, npix)
    chi = defocus * (row_square + freq_x * freq_x)
    turns = jnp.floor(chi * (1.0 / TURN) + (TILT / TURN + 0.5))
    angle = ((chi - turns * TURN_HIGH) - turns * TURN_LOW) + TILT
    square = angle * angle
    series = -SINE[-1]
    for term in SINE[-2::-1]:
        series = series * square - term
    return series * angle


def line_geometry(meta, ori, rows, many, npix, slot):
    place = 2 * ori
    defocus = meta[:, place : place + 1] + meta[:, place + 1 : place + 2] + meta[:, place + 2 : place + 3]
    index = (lax.broadcasted_iota(jnp.int32, (many, 1), 0) & (rows - 1)) + slot * rows
    freq_y = jnp.where(index < npix // 2, index, index - npix).astype(jnp.float32) / npix
    return defocus, freq_y * freq_y


def compare_kernel(ori, rows, slot_ref, noise_ref, fourier_ref, lookup_ref, volume_ref, turned_ref, filtered_ref, picks_ref, part_ref, about_ref, mix_ref, power_ref):
    many, wide = filtered_ref.shape
    npix = wide // 2
    deep = volume_ref.shape[0]
    images = many // rows

    meta = fourier_ref[:, wide:]
    here = lax.broadcasted_iota(jnp.int32, (images, many), 0) << bits(rows)
    there = lax.broadcasted_iota(jnp.int32, (images, many), 1)
    pick = jnp.where(here == there, 1.0, 0.0).astype(jnp.bfloat16)
    about = jnp.dot(pick, meta, preferred_element_type=jnp.float32)
    about_ref[...] = about
    label = lax.broadcasted_iota(jnp.int32, (images, lookup_ref.shape[0]), 1).astype(jnp.float32)
    found = []
    for o in range(ori):
        mine = about[:, o : o + 1] + 256.0 * about[:, ori + o : ori + o + 1]
        found.append(jnp.where(label == mine, 1.0, 0.0).astype(jnp.bfloat16))
    found = jnp.dot(
        jnp.concatenate(found, 0), lookup_ref[...], preferred_element_type=jnp.float32
    ).astype(jnp.bfloat16)
    picks_ref[...] = found
    spread = spread_over(rows, (many, images), 1)
    for o in range(ori):
        every = jnp.dot(
            spread, found[o * images : (o + 1) * images], preferred_element_type=jnp.float32
        )
        mix_ref[o * many : (o + 1) * many, :] = (
            own_row(every, rows).reshape(many, deep).astype(jnp.bfloat16)
        )
    defocus, row_square = line_geometry(meta.astype(jnp.float32), ori, rows, many, npix, slot_ref[0])
    def sections(start):
        planes = jnp.concatenate(
            [volume_ref[:, at : at + 128] for at in (start, npix + start)], 1
        )
        return [
            jnp.dot(
                mix_ref[o * many : (o + 1) * many, :], planes, preferred_element_type=jnp.float32
            )
            for o in range(ori)
        ]

    current = sections(0)
    for start in range(0, npix, 128):
        ctf = contrast(defocus, row_square, start, 128, npix)
        for at in (start, npix + start):
            filtered_ref[:, at : at + 128] = (
                ctf * fourier_ref[:, at : at + 128].astype(jnp.float32)
            ).astype(jnp.bfloat16)
        square = ctf * ctf
        following = sections(start + 128) if start + 128 < npix else None
        for o in range(ori):
            section = current[o] * current[o]
            power = square * (section[:, :128] + section[:, 128:])
            if start:
                power = power + power_ref[o]
            power_ref[o] = power
        current = following

    found = own_row(
        jnp.dot(filtered_ref[...], turned_ref[...], preferred_element_type=jnp.float32), rows
    )
    found = jnp.sum(found, axis=1)
    halves = []
    for o in range(ori):
        cross = found * picks_ref[o * images : (o + 1) * images, :].astype(jnp.float32)
        lanes = cross[:, :128]
        for start in range(128, deep, 128):
            lanes = lanes + cross[:, start : start + 128]
        power = jnp.sum(power_ref[o].reshape(images, rows, 128), axis=1)
        halves.append(lanes - 0.5 * power)
    lane = lax.broadcasted_iota(jnp.int32, (images, 128), 1)
    image = lax.broadcasted_iota(jnp.int32, (images, 128), 0)
    noise = jnp.where((image == slot_ref[0]) & (lane == 0), noise_ref[0], 0.0)
    halves = [noise] + [part - halves[0] for part in halves[1:]]
    upper = jnp.concatenate(halves[: ori // 2], 0)
    lower = jnp.concatenate(halves[ori // 2 :], 0)
    upper = jnp.sum(jnp.transpose(upper), axis=0, keepdims=True)
    lower = jnp.sum(jnp.transpose(lower), axis=0, keepdims=True)
    even = (lax.broadcasted_iota(jnp.int32, part_ref.shape, 0) & 1) == 0
    part_ref[...] = jnp.where(even, upper, lower)


def compare(slot, noise, fourier, lookup, volume, turned, ori, rows, copies):
    many = fourier.shape[0]
    deep, wide = volume.shape
    images = many // rows
    return pl.pallas_call(
        functools.partial(compare_kernel, ori, rows),
        in_specs=[scalar()] * 2 + [whole()] * 4,
        out_specs=(whole(),) * 4,
        out_shape=(
            jax.ShapeDtypeStruct((many, wide), jnp.bfloat16),
            jax.ShapeDtypeStruct((ori * images, deep), jnp.bfloat16),
            jax.ShapeDtypeStruct((copies * 2, 2 * images), jnp.float32),
            jax.ShapeDtypeStruct((images, META), jnp.float32),
        ),
        scratch_shapes=[
            pltpu.VMEM((ori * many, deep), jnp.bfloat16),
            pltpu.VMEM((ori, many, 128), jnp.float32),
        ],
        compiler_params=params(LARGE),
        cost_estimate=cost(1 << 31, 5 << 20),
        name="compare",
    )(slot, noise, fourier, lookup, volume, turned)


def squares_kernel(ori, rows, npix, slot_ref, about_ref, square_ref):
    many = square_ref.shape[0]
    images = many // rows
    about = about_ref[...]
    meta = jnp.dot(
        spread_over(rows, (many, images), 1),
        about.astype(jnp.bfloat16),
        preferred_element_type=jnp.float32,
    )
    defocus, row_square = line_geometry(meta, ori, rows, many, npix, slot_ref[0])
    for start in range(0, square_ref.shape[1], 128):
        ctf = contrast(defocus, row_square, start, 128, npix)
        square_ref[:, start : start + 128] = (ctf * ctf).astype(jnp.bfloat16)


def squares(slot, about, ori, rows, npix):
    images = about.shape[0]
    return pl.pallas_call(
        functools.partial(squares_kernel, ori, rows, npix),
        in_specs=[scalar(), whole()],
        out_specs=whole(),
        out_shape=jax.ShapeDtypeStruct((images * rows, npix // 2 + 128), jnp.bfloat16),
        compiler_params=params(SMALL),
        cost_estimate=cost(1 << 27, 1 << 20),
        name="squares",
    )(slot, about)


def pack(target_ref, share, source_ref, start, last):
    pairs = target_ref.shape[0]
    slab = share.shape[0] // pairs
    sums = jnp.dot(share, source_ref[...], preferred_element_type=jnp.float32)
    for number in range(sums.shape[1] // 128):
        value = sums[:, number * 128 : (number + 1) * 128].reshape(pairs, slab, 128)
        at = (start + number) * slab
        if start + number < last:
            target_ref[:, at : at + slab, :] = value.astype(jnp.bfloat16)
        else:
            lane = lax.broadcasted_iota(jnp.int32, (pairs, slab // 2, 128), 2)
            lower = jnp.broadcast_to(value[:, slab // 2 :, :1], lane.shape)
            value = jnp.where(lane == 0, value[:, : slab // 2], lower)
            target_ref[:, at : at + slab // 2, :] = value.astype(jnp.bfloat16)


def pack_both(target_ref, share, filtered_ref, square_ref):
    tiles = filtered_ref.shape[1] // 128
    last = tiles + square_ref.shape[1] // 128 - 1
    pack(target_ref, share, filtered_ref, 0, last)
    pack(target_ref, share, square_ref, tiles, last)


def project_kernel(rows, ori, core_ref, part_ref, picks_ref, filtered_ref, square_ref, probs_ref, share_ref, send_ref):
    many = filtered_ref.shape[0]
    deep = picks_ref.shape[1]
    lanes = part_ref.shape[1]
    images = lanes // 2
    sums = jnp.sum(part_ref[...].reshape(part_ref.shape[0] // 8, 8, lanes), axis=0)
    sums = sums + pltpu.roll(sums, 4, 0)
    sums = sums + pltpu.roll(sums, 2, 0)
    line = lax.broadcasted_iota(jnp.int32, sums.shape, 0) & 1
    lane = lax.broadcasted_iota(jnp.int32, sums.shape, 1)
    noise = jnp.where(line == 0, sums, pltpu.roll(sums, 1, 0))
    noise = jnp.where(lane < images, noise, pltpu.roll(noise, images, 1))
    score = jnp.where((line == 0) & (lane < images), 0.0, sums / noise)
    top = jnp.maximum(score, pltpu.roll(score, 1, 0))
    top = jnp.maximum(top, pltpu.roll(top, images, 1))
    power = jnp.exp(score - top)
    total = power + pltpu.roll(power, 1, 0)
    total = total + pltpu.roll(total, images, 1)
    probs = power / total
    probs_ref[...] = probs
    column = jnp.transpose(jnp.concatenate([probs] * (lanes // 8), 0))
    share = jnp.zeros((images, deep), jnp.float32)
    for o in range(ori):
        half = o % 2
        chance = column[half * images : (half + 1) * images, o // 2 : o // 2 + 1]
        share = share + chance * picks_ref[o * images : (o + 1) * images, :].astype(jnp.float32)
    share = jnp.dot(
        jnp.transpose(share).astype(jnp.bfloat16),
        spread_over(rows, (images, many), 0),
        preferred_element_type=jnp.float32,
    )
    pairs = send_ref.shape[0]
    share = own_row(share, rows).reshape(pairs, 2, deep // (2 * pairs), many)
    first = core_ref[0] == 0
    ours = jnp.where(first, share[:, 0], share[:, 1]).reshape(deep // 2, many)
    theirs = jnp.where(first, share[:, 1], share[:, 0]).reshape(deep // 2, many)
    share_ref[...] = ours.astype(jnp.bfloat16)
    pack_both(send_ref, theirs.astype(jnp.bfloat16), filtered_ref, square_ref)


def packed(deep, filtered, square, pairs):
    slab = deep // (2 * pairs)
    lines = (filtered.shape[1] + square.shape[1]) // 128 * slab - slab // 2
    return jax.ShapeDtypeStruct((pairs, lines, 128), jnp.bfloat16)


def project(core, part, picks, filtered, square, rows, ori, pairs):
    many = filtered.shape[0]
    deep = picks.shape[1]
    return pl.pallas_call(
        functools.partial(project_kernel, rows, ori),
        in_specs=[scalar()] + [whole()] * 4,
        out_specs=(whole(), whole(), whole()),
        out_shape=(
            jax.ShapeDtypeStruct((8, part.shape[1]), jnp.float32),
            jax.ShapeDtypeStruct((deep // 2, many), jnp.bfloat16),
            packed(deep, filtered, square, pairs),
        ),
        compiler_params=params(LARGE),
        cost_estimate=cost(1 << 28, 4 << 20),
        name="project",
    )(core, part, picks, filtered, square)


def keep_kernel(share_ref, filtered_ref, square_ref, keep_ref):
    pack_both(keep_ref, share_ref[...], filtered_ref, square_ref)


def keep_own(share, filtered, square, pairs):
    return pl.pallas_call(
        keep_kernel,
        out_shape=packed(2 * share.shape[0], filtered, square, pairs),
        compiler_params=params(SMALL),
        cost_estimate=cost(1 << 28, 2 << 20),
        name="keep_own",
    )(share, filtered, square)


def middle_kernel(high_ref, keep_ref, got_ref, own_ref, *send_refs):
    pairs = keep_ref.shape[0]
    for apart in range(pairs):
        at = high_ref[0] ^ apart
        total = keep_ref[at].astype(jnp.float32) + got_ref[at].astype(jnp.float32)
        if apart == 0:
            own_ref[...] = total
        else:
            send_refs[apart - 1][...] = total.astype(jnp.bfloat16)


def middle(high, keep, got):
    pairs, slab, wide = keep.shape
    return pl.pallas_call(
        middle_kernel,
        in_specs=[scalar(), whole(), whole()],
        out_specs=(whole(),) * pairs,
        out_shape=(jax.ShapeDtypeStruct((slab, wide), jnp.float32),)
        + (jax.ShapeDtypeStruct((slab, wide), jnp.bfloat16),) * (pairs - 1),
        compiler_params=params(SMALL),
        cost_estimate=cost(1 << 20, 2 << 20),
        name="middle",
    )(high, keep, got)


def mirror_columns(lower, last, precision=None):
    slab, half = lower.shape
    source = lax.broadcasted_iota(jnp.int32, (half, half), 0)
    target = lax.broadcasted_iota(jnp.int32, (half, half), 1)
    mirror = jnp.where(source + target == half, 1.0, 0.0).astype(lower.dtype)
    upper = jnp.dot(lower, mirror, preferred_element_type=jnp.float32, precision=precision)
    lane = lax.broadcasted_iota(jnp.int32, (slab, half), 1)
    return jnp.where(lane == 0, last, upper)


def spread_lines(lines, slab, npix):
    tiles = [lines[at : at + slab] for at in range(0, lines.shape[0] - slab // 2, slab)]
    last = lines[lines.shape[0] - slab // 2 :].astype(jnp.float32)
    last = jnp.concatenate([last[:, :1], last[:, 1:2]], 0)
    count = 2 * npix // 128
    return jnp.concatenate(tiles[:count], 1), jnp.concatenate(tiles[count:], 1), last


def collect_kernel(own_ref, data_ref, weight_ref, data_out, weight_out):
    slab, npix = weight_ref.shape
    half = npix // 2
    data, lower, last = spread_lines(own_ref[...], slab, npix)
    data_out[...] = data_ref[...] + data
    weight_out[:, :half] = weight_ref[:, :half] + lower
    weight_out[:, half:] = weight_ref[:, half:] + mirror_columns(
        lower, last, lax.Precision.HIGHEST
    )


def finish_kernel(*refs):
    *part_refs, data_ref, weight_ref, data_out, weight_out = refs
    slab, npix = weight_ref.shape
    half = npix // 2
    data = data_ref[...]
    weight = weight_ref[:, :half]
    lowers, lasts = [], []
    for part_ref in part_refs:
        part, lower, last = spread_lines(part_ref[...], slab, npix)
        data = data + part.astype(jnp.float32)
        weight = weight + lower.astype(jnp.float32)
        lowers.append(lower)
        lasts.append(last)
    uppers = mirror_columns(jnp.concatenate(lowers, 0), jnp.concatenate(lasts, 0))
    upper = weight_ref[:, half:]
    for number in range(len(part_refs)):
        upper = upper + uppers[number * slab : (number + 1) * slab]
    data_out[...] = data
    weight_out[:, :half] = weight
    weight_out[:, half:] = upper


def add_lines(kernel, name, lines, data, weight):
    return pl.pallas_call(
        kernel,
        out_shape=(
            jax.ShapeDtypeStruct(data.shape, jnp.float32),
            jax.ShapeDtypeStruct(weight.shape, jnp.float32),
        ),
        compiler_params=params(SMALL),
        cost_estimate=cost(1 << 20, 2 << 20),
        name=name,
    )(*lines, data, weight)


def on_device(images, defocus, noise, orient, planes, weights, volume, data_old, weight_old):
    npix = images.shape[1]
    ori = orient.shape[1]
    n_img = lax.axis_size("img")
    n_vol = lax.axis_size("vol")
    rows = npix // n_img
    slab = volume.shape[0]
    deep = n_vol * slab * rows
    many = n_img * rows
    pairs = n_vol // 2
    slot = lax.axis_index("img").astype(jnp.int32).reshape(1)
    place = lax.axis_index("vol").astype(jnp.int32)

    fourier = transform(orient, defocus, images[0], *dft_tables(npix))
    fourier = lax.all_to_all(
        fourier.reshape(n_img, rows, 2 * npix + META), "img", split_axis=0, concat_axis=0, tiled=True
    ).reshape(many, 2 * npix + META)
    vol_rows = lax.all_gather(volume.reshape(slab * rows, 2 * npix), "vol", axis=0, tiled=True)
    lookup = prepare(jnp.swapaxes(planes, 1, 2), jnp.swapaxes(weights, 1, 2), deep)
    filtered, picks, part, about = compare(
        slot, noise, fourier, lookup, vol_rows, turn(vol_rows), ori, rows, n_img
    )
    square = squares(slot, about, ori, rows, npix)
    part = lax.all_to_all(
        part.reshape(n_img, 2, 2 * n_img), "img", split_axis=0, concat_axis=0, tiled=True
    ).reshape(2 * n_img, 2 * n_img)
    probs, share, send = project(
        (place % 2).reshape(1), part, picks, filtered, square, rows, ori, pairs
    )
    mine = lax.dynamic_slice_in_dim(
        probs[:2].reshape(2 * 2, n_img), lax.axis_index("img"), 1, 1
    ).reshape(1, ori)
    got = lax.ppermute(send, "vol", [(v, v ^ 1) for v in range(n_vol)])
    keep = keep_own(share, filtered, square, pairs)
    own, *sends = middle((place // 2).reshape(1), keep, got)
    parts = [
        lax.ppermute(sends[apart - 1], "vol", [(v, v ^ (2 * apart)) for v in range(n_vol)])
        for apart in (2, 3, 1)
    ]
    data, weight = add_lines(
        collect_kernel,
        "collect",
        [own],
        data_old.reshape(slab * rows, 2 * npix),
        weight_old.reshape(slab * rows, npix),
    )
    data, weight = add_lines(finish_kernel, "finish", parts, data, weight)
    return (mine, data.reshape(data_old.shape), weight.reshape(weight_old.shape))


def solution(mesh):
    placed = (
        P(("img", "vol"), None, None),
        P(("img", "vol")),
        P(("img", "vol")),
        P(("img", "vol"), None),
        P(None, None, "img"),
        P(None, None, "img"),
        P("vol", "img", None),
        P("vol", "img", None),
        P("vol", "img", None),
    )
    return jax.shard_map(
        on_device,
        mesh=mesh,
        in_specs=placed,
        out_specs=(P(("img", "vol"), None), P("vol", "img", None), P("vol", "img", None)),
        check_vma=False,
    )
```

```python
import functools
import math

import jax
import jax.numpy as jnp
import ml_dtypes
import numpy as np
from jax import lax
from jax.experimental import pallas as pl
from jax.experimental.pallas import tpu as pltpu
from jax.sharding import PartitionSpec as P

AMP = 0.1
TILT = math.asin(AMP)
TURN = 2.0 * math.pi
TURN_HIGH = math.floor(TURN * 4096) / 4096
TURN_LOW = TURN - TURN_HIGH
SINE = tuple(
    factor / TURN ** (2 * power + 1)
    for power, factor in enumerate(
        (
            6.283185272722434,
            -41.341697068956265,
            81.60502462257806,
            -76.70155117622761,
            42.01616582127327,
            -14.868610992503873,
            3.199693654235983,
        )
    )
)
HUGE = 56 * 1024 * 1024
LARGE = 32 * 1024 * 1024
SMALL = 16 * 1024 * 1024
META = 128


def dft_tables(npix):
    index = np.arange(npix)
    angle = (index[:, None] * index[None, :] % npix) * (2.0 * math.pi / npix)
    scale = 1.0 / math.sqrt(npix)
    parts = [np.cos(angle) * scale, np.sin(angle) * scale]
    halves = [part[: npix // 2, parity::2] for parity in range(2) for part in parts]
    return tuple(
        jnp.asarray(np.concatenate(table, 1).astype(np.float32).astype(ml_dtypes.bfloat16))
        for table in (parts, halves)
    )


def frequency(index, npix):
    return ((index + npix // 2) % npix - npix // 2).astype(jnp.float32) / npix


def params(size):
    return pltpu.CompilerParams(vmem_limit_bytes=size)


def cost(flops, size):
    return pl.CostEstimate(flops=flops, bytes_accessed=size, transcendentals=0)


def whole():
    return pl.BlockSpec(memory_space=pltpu.VMEM)


def scalar():
    return pl.BlockSpec(memory_space=pltpu.SMEM)


def same(a, b):
    return lax.dot_general(a, b, (((1,), (1,)), ((), ())), preferred_element_type=jnp.float32)


def three_parts(value):
    parts = []
    for _ in range(3):
        part = value.astype(jnp.bfloat16).astype(jnp.float32)
        parts.append(part)
        value = value - part
    return parts


def bits(rows):
    assert rows & (rows - 1) == 0
    return rows.bit_length() - 1


def spread_over(rows, shape, image_axis):
    image = lax.broadcasted_iota(jnp.int32, shape, image_axis)
    owner = lax.broadcasted_iota(jnp.int32, shape, 1 - image_axis) >> bits(rows)
    return jnp.where(owner == image, 1.0, 0.0).astype(jnp.bfloat16)


def own_row(values, rows):
    height, width = values.shape
    sublane = lax.broadcasted_iota(jnp.int32, (rows, width), 0)
    lane = lax.broadcasted_iota(jnp.int32, (rows, width), 1) & (rows - 1)
    return jnp.where((sublane == lane)[None], values.reshape(height // rows, rows, width), 0.0)


def transform_kernel(chunk, orient_hbm, defocus_hbm, image_hbm, table_hbm, halves_hbm, out_hbm, orient_ref, defocus_ref, image_ref, wide_ref, table_ref, halves_ref, both_ref, out_ref, in_sems, out_sems):
    npix = image_ref.shape[0]
    half = npix // 2
    ori = orient_ref.shape[1]
    starts = [at + start for start in range(0, npix, chunk) for at in (0, npix)]
    pairs = [(image_hbm, image_ref)]
    pairs += [(table_hbm.at[:, pl.ds(start, chunk)], table_ref.at[:, pl.ds(start, chunk)]) for start in starts]
    pairs += [(halves_hbm, halves_ref), (orient_hbm, orient_ref), (defocus_hbm, defocus_ref)]
    loads = []
    for number, (source, target) in enumerate(pairs):
        load = pltpu.make_async_copy(source, target, in_sems.at[number])
        load.start()
        loads.append(load)
    loads[0].wait()
    tiles = range(npix // 128)
    for tile in tiles:
        wide_ref[tile] = image_ref[:, tile * 128 : (tile + 1) * 128].astype(jnp.float32)
    image = jnp.concatenate(
        [
            jnp.concatenate([wide_ref[tile, pl.ds(parity, half, 2), :] for tile in tiles], 1)
            for parity in range(2)
        ],
        0,
    ).astype(jnp.bfloat16)
    for load in loads[1 + len(starts) :]:
        load.wait()
    saves = []

    def save(start, size):
        at = pl.ds(start, size)
        copy = pltpu.make_async_copy(out_ref.at[:, at], out_hbm.at[:, at], out_sems.at[len(saves)])
        copy.start()
        saves.append(copy)

    lane = lax.broadcasted_iota(jnp.int32, (8, META), 1)
    codes = jnp.zeros((8, META), jnp.int32)
    for o in range(ori):
        label = orient_ref[0, o]
        codes = jnp.where(lane == o, label & 255, codes)
        codes = jnp.where(lane == ori + o, label >> 8, codes)
    about = codes.astype(jnp.float32)
    parts = three_parts(jnp.full((8, META), defocus_ref[0], jnp.float32))
    for place, part in enumerate(parts, 2 * ori):
        about = jnp.where(lane == place, part, about)
    out_ref[:, 2 * npix :] = jnp.broadcast_to(about[:1], (npix, META)).astype(jnp.bfloat16)
    save(2 * npix, META)
    def first_stage(number, start):
        loads[1 + number].wait()
        first = jnp.dot(
            image, table_ref[:, start : start + chunk], preferred_element_type=jnp.float32
        ).astype(jnp.bfloat16)
        for parity in range(2):
            part = first[parity * half : (parity + 1) * half]
            upper = slice(parity * npix, parity * npix + half)
            lower = slice(parity * npix + half, (parity + 1) * npix)
            if start < npix:
                both_ref[upper, start : start + chunk] = part
                both_ref[lower, npix + start : npix + start + chunk] = -part
            else:
                both_ref[upper, start : start + chunk] = -part
                both_ref[lower, start - npix : start - npix + chunk] = -part

    def second_stage(start):
        even, odd = (
            jnp.dot(
                halves_ref[:, parity * npix : (parity + 1) * npix],
                both_ref[parity * npix : (parity + 1) * npix, start : start + chunk],
                preferred_element_type=jnp.float32,
            )
            for parity in range(2)
        )
        out_ref[:half, start : start + chunk] = (even + odd).astype(jnp.bfloat16)
        out_ref[half:, start : start + chunk] = (even - odd).astype(jnp.bfloat16)
        save(start, chunk)

    for number, start in enumerate(starts):
        first_stage(number, start)
        if number % 2:
            second_stage(start - npix)
            second_stage(start)
    for copy in saves:
        copy.wait()


def transform(orient, defocus, image, table, halves):
    npix = image.shape[0]
    chunk = npix // 2
    pieces = 2 * npix // chunk
    return pl.pallas_call(
        functools.partial(transform_kernel, chunk),
        in_specs=[pl.BlockSpec(memory_space=pl.ANY)] * 5,
        out_specs=pl.BlockSpec(memory_space=pl.ANY),
        out_shape=jax.ShapeDtypeStruct((npix, 2 * npix + META), jnp.bfloat16),
        scratch_shapes=[
            pltpu.SMEM(orient.shape, jnp.int32),
            pltpu.SMEM(defocus.shape, jnp.float32),
            pltpu.VMEM((npix, npix), jnp.bfloat16),
            pltpu.VMEM((npix // 128, npix, 128), jnp.float32),
            pltpu.VMEM((npix, 2 * npix), jnp.bfloat16),
            pltpu.VMEM((npix // 2, 2 * npix), jnp.bfloat16),
            pltpu.VMEM((2 * npix, 2 * npix), jnp.bfloat16),
            pltpu.VMEM((npix, 2 * npix + META), jnp.bfloat16),
            pltpu.SemaphoreType.DMA((pieces + 4,)),
            pltpu.SemaphoreType.DMA((pieces + 1,)),
        ],
        compiler_params=params(HUGE),
        cost_estimate=cost(12 * npix**3, 10 * npix * npix),
        name="transform",
    )(orient, defocus, image, table, halves)


def prepare_kernel(planes_ref, weights_ref, lookup_ref):
    deep, labels = lookup_ref.shape
    rows = planes_ref.shape[1]
    level = lax.broadcasted_iota(jnp.int32, (deep // rows, rows, labels), 0)
    total = jnp.zeros((deep // rows, rows, labels), jnp.float32)
    for k in range(2):
        weight = weights_ref[k].astype(jnp.float32)
        total = total + jnp.where(level == planes_ref[k][None], weight[None], 0.0)
    lookup_ref[...] = total.reshape(deep, labels).astype(jnp.bfloat16)


def prepare(planes, weights, deep):
    labels = planes.shape[2]
    return pl.pallas_call(
        prepare_kernel,
        in_specs=[whole(), whole()],
        out_specs=whole(),
        out_shape=jax.ShapeDtypeStruct((deep, labels), jnp.bfloat16),
        compiler_params=params(SMALL),
        cost_estimate=cost(1 << 22, 1 << 20),
        name="prepare",
    )(planes, weights)


def contrast(defocus, row_square, start, width, npix):
    column = start + lax.broadcasted_iota(jnp.int32, (1, width), 1)
    freq_x = frequency(column, npix)
    chi = defocus * (row_square + freq_x * freq_x)
    turns = jnp.floor(chi * (1.0 / TURN) + (TILT / TURN + 0.5))
    angle = ((chi - turns * TURN_HIGH) - turns * TURN_LOW) + TILT
    square = angle * angle
    series = -SINE[-1]
    for term in SINE[-2::-1]:
        series = series * square - term
    return series * angle


def line_geometry(meta, ori, rows, many, npix, slot):
    place = 2 * ori
    defocus = meta[:, place : place + 1] + meta[:, place + 1 : place + 2] + meta[:, place + 2 : place + 3]
    index = (lax.broadcasted_iota(jnp.int32, (many, 1), 0) & (rows - 1)) + slot * rows
    freq_y = jnp.where(index < npix // 2, index, index - npix).astype(jnp.float32) / npix
    return defocus, freq_y * freq_y


def compare_kernel(ori, rows, slot_ref, noise_ref, fourier_ref, lookup_ref, volume_ref, filtered_ref, picks_ref, part_ref, about_ref, mix_ref, power_ref):
    many, wide = filtered_ref.shape
    npix = wide // 2
    deep = volume_ref.shape[0]
    images = many // rows

    meta = fourier_ref[:, wide:]
    here = lax.broadcasted_iota(jnp.int32, (images, many), 0) << bits(rows)
    there = lax.broadcasted_iota(jnp.int32, (images, many), 1)
    pick = jnp.where(here == there, 1.0, 0.0).astype(jnp.bfloat16)
    about = jnp.dot(pick, meta, preferred_element_type=jnp.float32)
    about_ref[...] = about
    label = lax.broadcasted_iota(jnp.int32, (images, lookup_ref.shape[1]), 1).astype(jnp.float32)
    found = []
    for o in range(ori):
        mine = about[:, o : o + 1] + 256.0 * about[:, ori + o : ori + o + 1]
        found.append(jnp.where(label == mine, 1.0, 0.0).astype(jnp.bfloat16))
    found = same(jnp.concatenate(found, 0), lookup_ref[...]).astype(jnp.bfloat16)
    picks_ref[...] = found
    spread = spread_over(rows, (many, images), 1)
    for o in range(ori):
        every = jnp.dot(
            spread, found[o * images : (o + 1) * images], preferred_element_type=jnp.float32
        )
        mix_ref[o * many : (o + 1) * many, :] = (
            own_row(every, rows).reshape(many, deep).astype(jnp.bfloat16)
        )
    defocus, row_square = line_geometry(meta.astype(jnp.float32), ori, rows, many, npix, slot_ref[0])
    def sections(start):
        planes = jnp.concatenate(
            [volume_ref[:, at : at + 128] for at in (start, npix + start)], 1
        )
        return [
            jnp.dot(
                mix_ref[o * many : (o + 1) * many, :], planes, preferred_element_type=jnp.float32
            )
            for o in range(ori)
        ]

    current = sections(0)
    for start in range(0, npix, 128):
        ctf = contrast(defocus, row_square, start, 128, npix)
        for at in (start, npix + start):
            filtered_ref[:, at : at + 128] = (
                ctf * fourier_ref[:, at : at + 128].astype(jnp.float32)
            ).astype(jnp.bfloat16)
        square = ctf * ctf
        following = sections(start + 128) if start + 128 < npix else None
        for o in range(ori):
            section = current[o] * current[o]
            power = square * (section[:, :128] + section[:, 128:])
            if start:
                power = power + power_ref[o]
            power_ref[o] = power
        current = following

    found = own_row(same(filtered_ref[...], volume_ref[...]), rows)
    found = jnp.sum(found, axis=1)
    halves = []
    for o in range(ori):
        cross = found * picks_ref[o * images : (o + 1) * images, :].astype(jnp.float32)
        lanes = cross[:, :128]
        for start in range(128, deep, 128):
            lanes = lanes + cross[:, start : start + 128]
        power = jnp.sum(power_ref[o].reshape(images, rows, 128), axis=1)
        halves.append(lanes - 0.5 * power)
    lane = lax.broadcasted_iota(jnp.int32, (images, 128), 1)
    image = lax.broadcasted_iota(jnp.int32, (images, 128), 0)
    noise = jnp.where((image == slot_ref[0]) & (lane == 0), noise_ref[0], 0.0)
    halves = [noise] + [part - halves[0] for part in halves[1:]]
    upper = jnp.concatenate(halves[: ori // 2], 0)
    lower = jnp.concatenate(halves[ori // 2 :], 0)
    upper = jnp.sum(jnp.transpose(upper), axis=0, keepdims=True)
    lower = jnp.sum(jnp.transpose(lower), axis=0, keepdims=True)
    even = (lax.broadcasted_iota(jnp.int32, part_ref.shape, 0) & 1) == 0
    part_ref[...] = jnp.where(even, upper, lower)


def compare(slot, noise, fourier, lookup, volume, ori, rows, copies):
    many = fourier.shape[0]
    deep, wide = volume.shape
    images = many // rows
    return pl.pallas_call(
        functools.partial(compare_kernel, ori, rows),
        in_specs=[scalar()] * 2 + [whole()] * 3,
        out_specs=(whole(),) * 4,
        out_shape=(
            jax.ShapeDtypeStruct((many, wide), jnp.bfloat16),
            jax.ShapeDtypeStruct((ori * images, deep), jnp.bfloat16),
            jax.ShapeDtypeStruct((copies * 2, 2 * images), jnp.float32),
            jax.ShapeDtypeStruct((images, META), jnp.float32),
        ),
        scratch_shapes=[
            pltpu.VMEM((ori * many, deep), jnp.bfloat16),
            pltpu.VMEM((ori, many, 128), jnp.float32),
        ],
        compiler_params=params(LARGE),
        cost_estimate=cost(1 << 31, 5 << 20),
        name="compare",
    )(slot, noise, fourier, lookup, volume)


def squares_kernel(ori, rows, npix, slot_ref, about_ref, square_ref):
    many = square_ref.shape[0]
    images = many // rows
    about = about_ref[...]
    meta = jnp.dot(
        spread_over(rows, (many, images), 1),
        about.astype(jnp.bfloat16),
        preferred_element_type=jnp.float32,
    )
    defocus, row_square = line_geometry(meta, ori, rows, many, npix, slot_ref[0])
    for start in range(0, square_ref.shape[1], 128):
        ctf = contrast(defocus, row_square, start, 128, npix)
        square_ref[:, start : start + 128] = (ctf * ctf).astype(jnp.bfloat16)


def squares(slot, about, ori, rows, npix):
    images = about.shape[0]
    return pl.pallas_call(
        functools.partial(squares_kernel, ori, rows, npix),
        in_specs=[scalar(), whole()],
        out_specs=whole(),
        out_shape=jax.ShapeDtypeStruct((images * rows, npix // 2 + 128), jnp.bfloat16),
        compiler_params=params(SMALL),
        cost_estimate=cost(1 << 27, 1 << 20),
        name="squares",
    )(slot, about)


def pack(target_ref, share, source_ref, start, last):
    pairs = target_ref.shape[0]
    slab = share.shape[0] // pairs
    sums = jnp.dot(share, source_ref[...], preferred_element_type=jnp.float32)
    for number in range(sums.shape[1] // 128):
        value = sums[:, number * 128 : (number + 1) * 128].reshape(pairs, slab, 128)
        at = (start + number) * slab
        if start + number < last:
            target_ref[:, at : at + slab, :] = value.astype(jnp.bfloat16)
        else:
            lane = lax.broadcasted_iota(jnp.int32, (pairs, slab // 2, 128), 2)
            lower = jnp.broadcast_to(value[:, slab // 2 :, :1], lane.shape)
            value = jnp.where(lane == 0, value[:, : slab // 2], lower)
            target_ref[:, at : at + slab // 2, :] = value.astype(jnp.bfloat16)


def pack_both(target_ref, share, filtered_ref, square_ref):
    tiles = filtered_ref.shape[1] // 128
    last = tiles + square_ref.shape[1] // 128 - 1
    pack(target_ref, share, filtered_ref, 0, last)
    pack(target_ref, share, square_ref, tiles, last)


def project_kernel(rows, ori, core_ref, part_ref, picks_ref, filtered_ref, square_ref, probs_ref, share_ref, send_ref):
    many = filtered_ref.shape[0]
    deep = picks_ref.shape[1]
    lanes = part_ref.shape[1]
    images = lanes // 2
    sums = jnp.sum(part_ref[...].reshape(part_ref.shape[0] // 8, 8, lanes), axis=0)
    sums = sums + pltpu.roll(sums, 4, 0)
    sums = sums + pltpu.roll(sums, 2, 0)
    line = lax.broadcasted_iota(jnp.int32, sums.shape, 0) & 1
    lane = lax.broadcasted_iota(jnp.int32, sums.shape, 1)
    noise = jnp.where(line == 0, sums, pltpu.roll(sums, 1, 0))
    noise = jnp.where(lane < images, noise, pltpu.roll(noise, images, 1))
    score = jnp.where((line == 0) & (lane < images), 0.0, sums / noise)
    top = jnp.maximum(score, pltpu.roll(score, 1, 0))
    top = jnp.maximum(top, pltpu.roll(top, images, 1))
    power = jnp.exp(score - top)
    total = power + pltpu.roll(power, 1, 0)
    total = total + pltpu.roll(total, images, 1)
    probs = power / total
    probs_ref[...] = probs
    column = jnp.transpose(jnp.concatenate([probs] * (lanes // 8), 0))
    share = jnp.zeros((images, deep), jnp.float32)
    for o in range(ori):
        half = o % 2
        chance = column[half * images : (half + 1) * images, o // 2 : o // 2 + 1]
        share = share + chance * picks_ref[o * images : (o + 1) * images, :].astype(jnp.float32)
    share = jnp.dot(
        jnp.transpose(share).astype(jnp.bfloat16),
        spread_over(rows, (images, many), 0),
        preferred_element_type=jnp.float32,
    )
    pairs = send_ref.shape[0]
    share = own_row(share, rows).reshape(pairs, 2, deep // (2 * pairs), many)
    first = core_ref[0] == 0
    ours = jnp.where(first, share[:, 0], share[:, 1]).reshape(deep // 2, many)
    theirs = jnp.where(first, share[:, 1], share[:, 0]).reshape(deep // 2, many)
    share_ref[...] = ours.astype(jnp.bfloat16)
    pack_both(send_ref, theirs.astype(jnp.bfloat16), filtered_ref, square_ref)


def packed(deep, filtered, square, pairs):
    slab = deep // (2 * pairs)
    lines = (filtered.shape[1] + square.shape[1]) // 128 * slab - slab // 2
    return jax.ShapeDtypeStruct((pairs, lines, 128), jnp.bfloat16)


def project(core, part, picks, filtered, square, rows, ori, pairs):
    many = filtered.shape[0]
    deep = picks.shape[1]
    return pl.pallas_call(
        functools.partial(project_kernel, rows, ori),
        in_specs=[scalar()] + [whole()] * 4,
        out_specs=(whole(), whole(), whole()),
        out_shape=(
            jax.ShapeDtypeStruct((8, part.shape[1]), jnp.float32),
            jax.ShapeDtypeStruct((deep // 2, many), jnp.bfloat16),
            packed(deep, filtered, square, pairs),
        ),
        compiler_params=params(LARGE),
        cost_estimate=cost(1 << 28, 4 << 20),
        name="project",
    )(core, part, picks, filtered, square)


def keep_kernel(share_ref, filtered_ref, square_ref, keep_ref):
    pack_both(keep_ref, share_ref[...], filtered_ref, square_ref)


def keep_own(share, filtered, square, pairs):
    return pl.pallas_call(
        keep_kernel,
        out_shape=packed(2 * share.shape[0], filtered, square, pairs),
        compiler_params=params(SMALL),
        cost_estimate=cost(1 << 28, 2 << 20),
        name="keep_own",
    )(share, filtered, square)


def middle_kernel(high_ref, keep_ref, got_ref, own_ref, *send_refs):
    pairs = keep_ref.shape[0]
    for apart in range(pairs):
        at = high_ref[0] ^ apart
        total = keep_ref[at].astype(jnp.float32) + got_ref[at].astype(jnp.float32)
        if apart == 0:
            own_ref[...] = total
        else:
            send_refs[apart - 1][...] = total.astype(jnp.bfloat16)


def middle(high, keep, got):
    pairs, slab, wide = keep.shape
    return pl.pallas_call(
        middle_kernel,
        in_specs=[scalar(), whole(), whole()],
        out_specs=(whole(),) * pairs,
        out_shape=(jax.ShapeDtypeStruct((slab, wide), jnp.float32),)
        + (jax.ShapeDtypeStruct((slab, wide), jnp.bfloat16),) * (pairs - 1),
        compiler_params=params(SMALL),
        cost_estimate=cost(1 << 20, 2 << 20),
        name="middle",
    )(high, keep, got)


def mirror_columns(lower, last, precision=None):
    slab, half = lower.shape
    source = lax.broadcasted_iota(jnp.int32, (half, half), 0)
    target = lax.broadcasted_iota(jnp.int32, (half, half), 1)
    mirror = jnp.where(source + target == half, 1.0, 0.0).astype(lower.dtype)
    upper = jnp.dot(lower, mirror, preferred_element_type=jnp.float32, precision=precision)
    lane = lax.broadcasted_iota(jnp.int32, (slab, half), 1)
    return jnp.where(lane == 0, last, upper)


def spread_lines(lines, slab, npix):
    tiles = [lines[at : at + slab] for at in range(0, lines.shape[0] - slab // 2, slab)]
    last = lines[lines.shape[0] - slab // 2 :].astype(jnp.float32)
    last = jnp.concatenate([last[:, :1], last[:, 1:2]], 0)
    count = 2 * npix // 128
    return jnp.concatenate(tiles[:count], 1), jnp.concatenate(tiles[count:], 1), last


def collect_kernel(own_ref, data_ref, weight_ref, data_out, weight_out):
    slab, npix = weight_ref.shape
    half = npix // 2
    data, lower, last = spread_lines(own_ref[...], slab, npix)
    data_out[...] = data_ref[...] + data
    weight_out[:, :half] = weight_ref[:, :half] + lower
    weight_out[:, half:] = weight_ref[:, half:] + mirror_columns(
        lower, last, lax.Precision.HIGHEST
    )


def finish_kernel(*refs):
    *part_refs, data_ref, weight_ref, data_out, weight_out = refs
    slab, npix = weight_ref.shape
    half = npix // 2
    data = data_ref[...]
    weight = weight_ref[:, :half]
    lowers, lasts = [], []
    for part_ref in part_refs:
        part, lower, last = spread_lines(part_ref[...], slab, npix)
        data = data + part.astype(jnp.float32)
        weight = weight + lower.astype(jnp.float32)
        lowers.append(lower)
        lasts.append(last)
    uppers = mirror_columns(jnp.concatenate(lowers, 0), jnp.concatenate(lasts, 0))
    upper = weight_ref[:, half:]
    for number in range(len(part_refs)):
        upper = upper + uppers[number * slab : (number + 1) * slab]
    data_out[...] = data
    weight_out[:, :half] = weight
    weight_out[:, half:] = upper


def add_lines(kernel, name, lines, data, weight):
    return pl.pallas_call(
        kernel,
        out_shape=(
            jax.ShapeDtypeStruct(data.shape, jnp.float32),
            jax.ShapeDtypeStruct(weight.shape, jnp.float32),
        ),
        compiler_params=params(SMALL),
        cost_estimate=cost(1 << 20, 2 << 20),
        name=name,
    )(*lines, data, weight)


def on_device(images, defocus, noise, orient, planes, weights, volume, data_old, weight_old):
    npix = images.shape[1]
    ori = orient.shape[1]
    n_img = lax.axis_size("img")
    n_vol = lax.axis_size("vol")
    rows = npix // n_img
    slab = volume.shape[0]
    deep = n_vol * slab * rows
    many = n_img * rows
    pairs = n_vol // 2
    slot = lax.axis_index("img").astype(jnp.int32).reshape(1)
    place = lax.axis_index("vol").astype(jnp.int32)

    fourier = transform(orient, defocus, images[0], *dft_tables(npix))
    fourier = lax.all_to_all(
        fourier.reshape(n_img, rows, 2 * npix + META), "img", split_axis=0, concat_axis=0, tiled=True
    ).reshape(many, 2 * npix + META)
    vol_rows = lax.all_gather(volume.reshape(slab * rows, 2 * npix), "vol", axis=0, tiled=True)
    lookup = prepare(jnp.swapaxes(planes, 1, 2), jnp.swapaxes(weights, 1, 2), deep)
    filtered, picks, part, about = compare(
        slot, noise, fourier, lookup, vol_rows, ori, rows, n_img
    )
    square = squares(slot, about, ori, rows, npix)
    part = lax.all_to_all(
        part.reshape(n_img, 2, 2 * n_img), "img", split_axis=0, concat_axis=0, tiled=True
    ).reshape(2 * n_img, 2 * n_img)
    probs, share, send = project(
        (place % 2).reshape(1), part, picks, filtered, square, rows, ori, pairs
    )
    mine = lax.dynamic_slice_in_dim(
        probs[:2].reshape(2 * 2, n_img), lax.axis_index("img"), 1, 1
    ).reshape(1, ori)
    got = lax.ppermute(send, "vol", [(v, v ^ 1) for v in range(n_vol)])
    keep = keep_own(share, filtered, square, pairs)
    own, *sends = middle((place // 2).reshape(1), keep, got)
    parts = [
        lax.ppermute(sends[apart - 1], "vol", [(v, v ^ (2 * apart)) for v in range(n_vol)])
        for apart in (2, 3, 1)
    ]
    data, weight = add_lines(
        collect_kernel,
        "collect",
        [own],
        data_old.reshape(slab * rows, 2 * npix),
        weight_old.reshape(slab * rows, npix),
    )
    data, weight = add_lines(finish_kernel, "finish", parts, data, weight)
    return (mine, data.reshape(data_old.shape), weight.reshape(weight_old.shape))


def solution(mesh):
    placed = (
        P(("img", "vol"), None, None),
        P(("img", "vol")),
        P(("img", "vol")),
        P(("img", "vol"), None),
        P(None, None, "img"),
        P(None, None, "img"),
        P("vol", "img", None),
        P("vol", "img", None),
        P("vol", "img", None),
    )
    return jax.shard_map(
        on_device,
        mesh=mesh,
        in_specs=placed,
        out_specs=(P(("img", "vol"), None), P("vol", "img", None), P("vol", "img", None)),
        check_vma=False,
    )
```
